128 devices in a mesh: space: 32 (over z, x, core), segment: 4 (over y).
Axes of the slice: x: 4, y: 4, z: 4, core: 2. Of those that a mesh axis runs over, the one named last changes fastest.
Arguments:
- features: bfloat16 [4, 32768, 128], P('segment', 'space'), may hold values from -6 to 6
- weights: bfloat16 [4, 27, 128, 128], P('segment'), may hold values from -0.109375 to 0.109375
- cotangent: bfloat16 [4, 32768, 128], P('segment', 'space'), may hold values from -6 to 6
- local_map: int32 [32768, 27], P('space'), may hold values from 0 to 1024, as said below
- send_map: int32 [36864, 27], P('space'), may hold values from 0 to 1024, as said below
- recv_map: int32 [36864], P('space'), may hold values from 0 to 1024, as said below
Outputs:
- mixed: bfloat16 [4, 32768, 128], P('segment', 'space')
- input_grad: bfloat16 [4, 32768, 128], P('segment', 'space')
- weight_grad: float32 [4, 27, 128, 128], P('segment')
The draws below stay inside these ranges and needn't reach their ends.
Inputs may be any that keep to these rules, and one draw needn't show every extreme that they name: Each tile is a block of 8 x 8 x 32 cells of a grid of 4 x 8 tiles, of which exactly 1024 cells are occupied. local_map[p, v, k] is the row of the occupied cell at offset (k // 9 - 1, (k // 3) % 3 - 1, k % 3 - 1) from voxel v inside the same tile, else 1024; offset 13 is the voxel itself, and local_map[p, v, k] = u < 1024 exactly when local_map[p, u, 26 - k] = v. For tile p and direction d, the slots list the cells of the neighbouring tile p + delta(d) that touch tile p (a face of 256 cells, or a vertical edge of 32 cells for a diagonal direction); send_map[p, d, c, k] is the row in tile p of the occupied cell at offset k from slot c's cell, else 1024. A direction without a neighbouring tile has only 1024. recv_map[q, d, c] is the row in tile q of the cell of slot c of the list that tile q - delta(d) holds for direction d, or 1024 where that cell is empty or that tile does not exist.
All inputs are finite; a program needn't handle non-finite values.
Results may differ from the reference program's by a relative error of at most 0.0051.
Values may be sent and summed in bfloat16 or wider, within the bound.
No kernel may reach another device: no remote copies, remote signals or barrier semaphores. Data moves between devices by JAX's collectives and lax.ppermute only.
A program may use at most 64 MiB of HBM per device.

```python
import jax
import jax.numpy as jnp
from jax import lax

C = 128
SIDE = 8
TZ = 32
TILES_X = 4
TILES_Y = 8
SECTIONS = 4
CELLS = 2048
ROWS = 1024
VOXELS = 32768
CAP = 256
HALO = 1152
N_SPACE = 32


DIRECTION_X = (-1, -1, -1, 0, 0, 1, 1, 1)


DIRECTION_Y = (-1, 0, 1, -1, 1, -1, 0, 1)


def geometry(key):

    def tile_order(number):
        return jax.random.permutation(jax.random.fold_in(key, number), CELLS).astype(jnp.int32)
    orders = jax.vmap(tile_order)(jnp.arange(N_SPACE, dtype=jnp.int32))

    def ranking(order):
        return jnp.zeros((CELLS,), jnp.int32).at[order].set(jnp.arange(CELLS, dtype=jnp.int32))
    ranks = jax.vmap(ranking)(orders)
    occupied = jnp.where(ranks < ROWS, ranks, -1)
    grid = occupied.reshape(TILES_Y, TILES_X, SIDE, SIDE, TZ).transpose(1, 2, 0, 3, 4)
    grid = grid.reshape(TILES_X * SIDE, TILES_Y * SIDE, TZ)
    return (orders, jnp.pad(grid, 1, constant_values=-1))


def lookup(grid, coord_x, coord_y, coord_z):
    clip_x = jnp.clip(coord_x + 1, 0, TILES_X * SIDE + 1)
    clip_y = jnp.clip(coord_y + 1, 0, TILES_Y * SIDE + 1)
    clip_z = jnp.clip(coord_z + 1, 0, TZ + 1)
    return grid[clip_x, clip_y, clip_z]


def offset_parts():
    offset = jnp.arange(27, dtype=jnp.int32)
    return (offset // 9 - 1, offset // 3 % 3 - 1, offset % 3 - 1)


def slot_targets():
    slot = jnp.arange(CAP, dtype=jnp.int32)[None, :]
    free = slot // TZ
    depth = slot % TZ
    dir_x = jnp.array(DIRECTION_X, jnp.int32)[:, None]
    dir_y = jnp.array(DIRECTION_Y, jnp.int32)[:, None]
    local_x = jnp.where(dir_x == 1, 0, jnp.where(dir_x == -1, SIDE - 1, free))
    local_y = jnp.where(dir_y == 1, 0, jnp.where(dir_y == -1, SIDE - 1, free))
    usable = (dir_x == 0) | (dir_y == 0) | (free == 0)
    return (dir_x, dir_y, local_x, local_y, depth, usable)


def tile_coords():
    tile = jnp.arange(N_SPACE, dtype=jnp.int32)[:, None, None]
    return (tile % TILES_X, tile // TILES_X)


def compact(values):
    pieces = []
    for number in range(8):
        diagonal = DIRECTION_X[number] != 0 and DIRECTION_Y[number] != 0
        length = TZ if diagonal else CAP
        pieces.append(values[:, number, :length])
    return jnp.concatenate(pieces, 1)


def draw_local_map(key, part):
    orders, grid = geometry(key)
    tile_x, tile_y = tile_coords()
    cell = orders[:, :ROWS, None]
    step_x, step_y, step_z = offset_parts()
    near_x = cell // (SIDE * TZ) + step_x
    near_y = cell // TZ % SIDE + step_y
    near_z = cell % TZ + step_z
    inside = (near_x >= 0) & (near_x < SIDE) & (near_y >= 0) & (near_y < SIDE)
    found = lookup(grid, tile_x * SIDE + near_x, tile_y * SIDE + near_y, near_z)
    return jnp.where(inside & (found >= 0), found, ROWS).astype(jnp.int32).reshape(VOXELS, 27)


def draw_send_map(key, part):
    orders, grid = geometry(key)
    tile_x, tile_y = tile_coords()
    dir_x, dir_y, local_x, local_y, depth, usable = slot_targets()
    dest_x = tile_x + dir_x
    dest_y = tile_y + dir_y
    exists = (dest_x >= 0) & (dest_x < TILES_X) & (dest_y >= 0) & (dest_y < TILES_Y)
    target_x = dest_x * SIDE + local_x
    target_y = dest_y * SIDE + local_y
    target_row = lookup(grid, target_x, target_y, depth)
    valid = exists & usable & (target_row >= 0)
    step_x, step_y, step_z = offset_parts()
    near_x = target_x[..., None] + step_x
    near_y = target_y[..., None] + step_y
    near_z = depth[..., None] + step_z
    in_source = (near_x // SIDE == tile_x[..., None]) & (near_y // SIDE == tile_y[..., None])
    found = lookup(grid, near_x, near_y, near_z)
    keep = valid[..., None] & in_source & (found >= 0)
    full = jnp.where(keep, found, ROWS).astype(jnp.int32)
    return compact(full).reshape(N_SPACE * HALO, 27)


def draw_recv_map(key, part):
    orders, grid = geometry(key)
    tile_x, tile_y = tile_coords()
    dir_x, dir_y, local_x, local_y, depth, usable = slot_targets()
    source_x = tile_x - dir_x
    source_y = tile_y - dir_y
    exists = (source_x >= 0) & (source_x < TILES_X) & (source_y >= 0) & (source_y < TILES_Y)
    found = lookup(grid, tile_x * SIDE + local_x, tile_y * SIDE + local_y, depth)
    keep = exists & usable & (found >= 0)
    full = jnp.where(keep, found, ROWS).astype(jnp.int32)
    return compact(full).reshape(N_SPACE * HALO)


def steps_of(stream_key, shape, shards, least, top_value):
    factor_of, own = 1.0, jax.random.fold_in(stream_key, 6)
    for dim, parts in shards:
        steps = jnp.exp(jax.random.uniform(jax.random.fold_in(own, dim), (parts,), jnp.float32, least / len(shards), top_value / len(shards)))
        factor_of = factor_of * jnp.repeat(steps, shape[dim] // parts).reshape([-1 if axis == dim else 1 for axis in range(len(shape))])
    return factor_of


def bell_draw(stream_key, extent, spread, reach, split=(), kind=jnp.bfloat16):
    values = spread * jax.random.normal(stream_key, extent, jnp.float32)
    if split:
        values = values * steps_of(stream_key, extent, split, -0.22, 0.18)
    return jnp.clip(values, -reach, reach).astype(kind)


def setup_inputs(seed: int = 0) -> dict:
    streams_of = jax.random.split(jax.random.key(seed), 7)
    return {
        "features": bell_draw(streams_of[0], (SECTIONS, VOXELS, C), 1.0, 6.0, ((0, 4), (1, 32))),
        "weights": bell_draw(streams_of[1], (SECTIONS, 27, C, C), (27 * C) ** -0.5, 0.109375, ((0, 4),)),
        "cotangent": bell_draw(streams_of[2], (SECTIONS, VOXELS, C), 1.0, 6.0, ((0, 4), (1, 32))),
        "local_map": draw_local_map(jax.random.fold_in(streams_of[6], 71), 0),
        "send_map": draw_send_map(jax.random.fold_in(streams_of[6], 71), 0),
        "recv_map": draw_recv_map(jax.random.fold_in(streams_of[6], 71), 0),
    }


DIRECTIONS = ((-1, -1), (-1, 0), (-1, 1), (0, -1), (0, 1), (1, -1), (1, 0), (1, 1))


def spans():
    result = []
    start = 0
    for step_x, step_y in DIRECTIONS:
        length = TZ if (step_x != 0 and step_y != 0) else CAP
        result.append((start, length))
        start = start + length
    return result


def take_rows(table, row_ids):
    return jax.vmap(lambda source_rows, picked: jnp.take(source_rows, picked, axis=0))(table, row_ids)


def add_rows(table, row_ids, values):
    return jax.vmap(lambda target_rows, picked, adding: target_rows.at[picked].add(adding))(table, row_ids, values)


def move(values, delta):
    blank = jnp.zeros_like(values)
    if delta > 0:
        return jnp.concatenate([blank[:delta], values[:-delta]], 0)
    return jnp.concatenate([values[-delta:], blank[:-delta]], 0)


def with_zero_row(values):
    return jnp.concatenate([values, jnp.zeros_like(values[:, :1])], 1)


def forward_section(padded, weight, local_map, send_map, recv_map):
    offsets = jnp.arange(27, dtype=jnp.int32)

    def local_step(running, offset):
        gathered = take_rows(padded, local_map[:, :, offset])
        product = jnp.dot(gathered.reshape(-1, C), weight[offset], preferred_element_type=jnp.float32)
        return running + product.reshape(N_SPACE, ROWS, C), None

    local_part, _ = lax.scan(local_step, jnp.zeros((N_SPACE, ROWS, C), jnp.float32), offsets)
    summed = with_zero_row(local_part)
    for number, (step_x, step_y) in enumerate(DIRECTIONS):
        start, length = spans()[number]
        part_send = send_map[:, start:start + length]

        def halo_step(running, offset):
            gathered = take_rows(padded, part_send[:, :, offset])
            product = jnp.dot(gathered.reshape(-1, C), weight[offset], preferred_element_type=jnp.float32)
            return running + product.reshape(N_SPACE, length, C), None

        sent, _ = lax.scan(halo_step, jnp.zeros((N_SPACE, length, C), jnp.float32), offsets)
        arrived = move(sent, step_x + TILES_X * step_y)
        summed = add_rows(summed, recv_map[:, start:start + length], arrived)
    return summed[:, :ROWS]


def backward_section(padded, grad_pre, weight, local_map, send_map, recv_map):
    offsets = jnp.arange(27, dtype=jnp.int32)
    grad_padded = with_zero_row(grad_pre)
    flat_grad = grad_pre.reshape(-1, C)

    def local_step(running, offset):
        gathered_grad = take_rows(grad_padded, local_map[:, :, 26 - offset])
        product = jnp.dot(gathered_grad.reshape(-1, C), weight[offset].T, preferred_element_type=jnp.float32)
        gathered = take_rows(padded, local_map[:, :, offset])
        kernel_part = jnp.dot(gathered.reshape(-1, C).T, flat_grad, preferred_element_type=jnp.float32)
        return running + product.reshape(N_SPACE, ROWS, C), kernel_part

    input_part, weight_grad = lax.scan(local_step, jnp.zeros((N_SPACE, ROWS, C), jnp.float32), offsets)
    summed = with_zero_row(input_part)
    for number, (step_x, step_y) in enumerate(DIRECTIONS):
        start, length = spans()[number]
        part_send = send_map[:, start:start + length]
        returned = move(take_rows(grad_padded, recv_map[:, start:start + length]), -(step_x + TILES_X * step_y))
        flat_returned = returned.reshape(-1, C)

        def halo_step(running, offset):
            row_ids = part_send[:, :, offset]
            term = jnp.dot(flat_returned, weight[offset].T, preferred_element_type=jnp.float32)
            running = add_rows(running, row_ids, term.reshape(N_SPACE, length, C))
            gathered = take_rows(padded, row_ids)
            kernel_part = jnp.dot(gathered.reshape(-1, C).T, flat_returned, preferred_element_type=jnp.float32)
            return running, kernel_part

        summed, extra = lax.scan(halo_step, summed, offsets)
        weight_grad = weight_grad + extra
    return summed[:, :ROWS].astype(jnp.bfloat16), weight_grad


def reference(features, weights, cotangent, local_map, send_map, recv_map):
    local_map = local_map.reshape(N_SPACE, ROWS, 27)
    send_map = send_map.reshape(N_SPACE, HALO, 27)
    recv_map = recv_map.reshape(N_SPACE, HALO)
    paddeds = []
    pre_acts = []
    activations = []
    for section in range(SECTIONS):
        padded = with_zero_row(features[section].reshape(N_SPACE, ROWS, C))
        pre_act = forward_section(padded, weights[section], local_map, send_map, recv_map)
        paddeds.append(padded)
        pre_acts.append(pre_act)
        activations.append(jax.nn.silu(pre_act).astype(jnp.bfloat16))
    mixed_list = []
    input_list = []
    kernel_list = []
    for section in range(SECTIONS):
        partner = section ^ 1
        mixed = activations[section].astype(jnp.float32) + activations[partner].astype(jnp.float32)
        mixed_list.append(mixed.astype(jnp.bfloat16).reshape(VOXELS, C))
        incoming = cotangent[section].astype(jnp.float32) + cotangent[partner].astype(jnp.float32)
        incoming = incoming.reshape(N_SPACE, ROWS, C)
        pre_act = pre_acts[section]
        sigmoid = jax.nn.sigmoid(pre_act)
        grad_pre = (incoming * sigmoid * (1.0 + pre_act * (1.0 - sigmoid))).astype(jnp.bfloat16)
        input_grad, weight_grad = backward_section(paddeds[section], grad_pre, weights[section], local_map, send_map, recv_map)
        input_list.append(input_grad.reshape(VOXELS, C))
        kernel_list.append(weight_grad)
    return jnp.stack(mixed_list), jnp.stack(input_list), jnp.stack(kernel_list)
```

```python
import functools

import jax
import jax.numpy as jnp
from jax import lax
from jax.experimental import pallas as pl
from jax.experimental.pallas import tpu as pltpu
from jax.sharding import PartitionSpec as P

TZ = 32
TILES_X = 4
CAP = 256
ROWS = 1024
C = 128
HALO = 1152

DIRECTIONS = ((-1, -1), (-1, 0), (-1, 1), (0, -1), (0, 1), (1, -1), (1, 0), (1, 1))
BF = jnp.bfloat16
F32 = jnp.float32


def spans():
    result = []
    start = 0
    for step_x, step_y in DIRECTIONS:
        length = TZ if step_x != 0 and step_y != 0 else CAP
        result.append((start, length))
        start = start + length
    return result


SPANS = spans()
FACES = [n for n, (a, b) in enumerate(DIRECTIONS) if a == 0 or b == 0]
CORNERS = [n for n, (a, b) in enumerate(DIRECTIONS) if a != 0 and b != 0]


def toward(step_x, step_y):
    picked = []
    for offset in range(27):
        along_x = offset // 9 - 1
        along_y = offset // 3 % 3 - 1
        if (step_x == 0 or along_x == -step_x) and (step_y == 0 or along_y == -step_y):
            picked.append(offset)
    return picked


def dot(a, b, dims=((1,), (0,))):
    return lax.dot_general(a, b, (dims, ((), ())), preferred_element_type=F32)


def hot(row, rows):
    pos = lax.broadcasted_iota(jnp.int32, (256, 128), 0).astype(jnp.int16)
    count = row.shape[1]
    blocks = []
    for base in range(0, rows, 256):
        rel = (row - base).astype(jnp.int16)
        parts = [
            jnp.where(rel[:, t : t + 128] == pos, BF(1), BF(0)) for t in range(0, count, 128)
        ]
        blocks.append(jnp.concatenate(parts, 1))
    return jnp.concatenate(blocks, 0)


def match(column, row):
    return jnp.where(column == row.astype(jnp.int16), BF(1), BF(0))


def spread(column, count):
    kept = jnp.where(column == ROWS, -1, column)
    return jnp.broadcast_to(kept, (column.shape[0], count)).astype(jnp.int16)


def corner_mask(position, axis, shape):
    lane = lax.broadcasted_iota(jnp.int32, shape, axis)
    return (lane // TZ) == position


def lists_of(number):
    return SPANS[number]


def face_match(number, offset, column, sm_ref):
    start, length = SPANS[number]
    return match(column, sm_ref[offset, :, start : start + length])


def corner_row(place, sm_ref):
    pieces = []
    for number in CORNERS:
        start, length = SPANS[number]
        offset = toward(*DIRECTIONS[number])[place]
        pieces.append(sm_ref[offset, :, start : start + length])
    return jnp.concatenate(pieces, 1)


def corner_column(rc_ref, count):
    pieces = []
    for number in CORNERS:
        start, length = SPANS[7 - number]
        pieces.append(rc_ref[start : start + length, :])
    return spread(jnp.concatenate(pieces, 0), count)


def start_kernel(x_ref, rr_ref, rc_ref, sm_ref, w_ref, part_ref, face_g_ref, corner_g_ref):
    x_t = x_ref[...].astype(F32).T.astype(BF)
    selector = hot(rr_ref[...], ROWS)
    listed = dot(x_t, selector).astype(BF)
    for place, number in enumerate(FACES):
        start, length = SPANS[number]
        other, _ = SPANS[7 - number]
        column = spread(rc_ref[other : other + length, :], length)
        source = listed[:, other : other + length]
        picked = toward(*DIRECTIONS[number])
        gathered = []
        for offset in picked:
            chosen = face_match(number, offset, column, sm_ref)
            gathered.append(dot(source, chosen).astype(BF))
        gathered = jnp.concatenate(gathered, 0)
        face_g_ref[place] = gathered
        weight = jnp.concatenate([w_ref[offset] for offset in picked], 0)
        total = dot(weight, gathered, ((0,), (0,)))
        part_ref[start : start + length, :] = total.T.astype(BF)
    column = corner_column(rc_ref, 4 * TZ)
    source = jnp.concatenate(
        [listed[:, SPANS[7 - n][0] : SPANS[7 - n][0] + TZ] for n in CORNERS], 1
    )
    gathered = []
    for step in range(3):
        chosen = match(column, corner_row(step, sm_ref))
        gathered.append(dot(source, chosen).astype(BF))
    masked = []
    weights = []
    for place, number in enumerate(CORNERS):
        inside = corner_mask(place, 1, (C, 4 * TZ))
        for step in range(3):
            masked.append(jnp.where(inside, gathered[step], BF(0)))
            weights.append(w_ref[toward(*DIRECTIONS[number])[step]])
    masked = jnp.concatenate(masked, 0)
    corner_g_ref[...] = masked
    total = dot(jnp.concatenate(weights, 0), masked, ((0,), (0,))).T.astype(BF)
    for place, number in enumerate(CORNERS):
        start, length = SPANS[number]
        part_ref[start : start + length, :] = total[place * TZ : (place + 1) * TZ, :]


def pair_of(step):
    first = jnp.where(2 * step >= 13, 2 * step + 1, 2 * step)
    second = jnp.where(2 * step + 1 >= 13, 2 * step + 2, 2 * step + 1)
    return first, second


def forward_kernel(x_ref, lm_ref, w_ref, g_ref, pre_ref, x_t, total, *, width):
    step = pl.program_id(0)

    @pl.when(step == 0)
    def _():
        x_t[...] = x_ref[...].astype(F32).T.astype(BF)
        total[...] = dot(w_ref[13], x_t[...], ((0,), (0,)))

    pair = pair_of(step)
    weight = jnp.concatenate([w_ref[k] for k in pair], 0)
    for begin in range(0, ROWS, width):
        cols = slice(begin, begin + width)
        gathered = [dot(x_t[...], hot(lm_ref[k, :, cols], ROWS)).astype(BF) for k in pair]
        gathered = jnp.concatenate(gathered, 0)
        g_ref[:, cols] = gathered
        total[:, cols] += dot(weight, gathered, ((0,), (0,)))

    @pl.when(step == 12)
    def _():
        pre_ref[...] = total[...].T


def activate_kernel(pre_ref, part_ref, rr_ref, cot_ref, pair_ref, act_ref, grad_ref, out_ref):
    selector = hot(rr_ref[...], ROWS)
    pre = pre_ref[...] + dot(selector, part_ref[...])
    gate = 1.0 / (1.0 + jnp.exp(-pre))
    act_ref[...] = (pre * gate).astype(BF)
    upstream = cot_ref[...].astype(F32) + pair_ref[...].astype(F32)
    grad = upstream * gate * (1.0 + pre * (1.0 - gate))
    grad_ref[...] = grad.astype(BF)
    grad_t = grad.T.astype(BF)
    out_ref[...] = dot(grad_t, selector).T.astype(BF)


def weight_kernel(g_ref, grad_ref, x_ref, dw_ref):
    step = pl.program_id(0)
    first, second = pair_of(step)

    @pl.when(step == 0)
    def _():
        dw_ref[13] = dot(x_ref[...], grad_ref[...], ((0,), (0,)))

    both = dot(g_ref[...], grad_ref[...])
    dw_ref[first] = both[:C]
    dw_ref[second] = both[C:]


def return_kernel(back_ref, rc_ref, sm_ref, w_ref, face_g_ref, corner_g_ref, dw_in_ref, dw_ref, placed_ref, total):
    total[...] = dw_in_ref[...]
    for place, number in enumerate(FACES):
        start, length = SPANS[number]
        other, _ = SPANS[7 - number]
        column = spread(rc_ref[other : other + length, :], length)
        back = back_ref[start : start + length, :]
        picked = toward(*DIRECTIONS[number])
        pieces = []
        for offset in picked:
            chosen = face_match(number, offset, column, sm_ref)
            pieces.append(dot(chosen, back).astype(BF))
        pieces = jnp.concatenate(pieces, 1)
        weight = jnp.concatenate([w_ref[offset] for offset in picked], 1)
        placed_ref[other : other + length, :] = dot(pieces, weight, ((1,), (1,)))
        kernel_part = dot(face_g_ref[place], back)
        for index, offset in enumerate(picked):
            total[offset] += kernel_part[index * C : (index + 1) * C, :]
    column = corner_column(rc_ref, 4 * TZ)
    back = jnp.concatenate([back_ref[SPANS[n][0] : SPANS[n][0] + TZ, :] for n in CORNERS], 0)
    kernel_part = dot(corner_g_ref[...], back)
    pieces = []
    weights = []
    spots = [dot(match(column, corner_row(step, sm_ref)), back).astype(BF) for step in range(3)]
    for place, number in enumerate(CORNERS):
        inside = corner_mask(place, 0, (4 * TZ, C))
        for step in range(3):
            offset = toward(*DIRECTIONS[number])[step]
            row = (place * 3 + step) * C
            total[offset] += kernel_part[row : row + C, :]
            pieces.append(jnp.where(inside, spots[step], BF(0)))
            weights.append(w_ref[offset])
    result = dot(jnp.concatenate(pieces, 1), jnp.concatenate(weights, 1), ((1,), (1,)))
    for place, number in enumerate(CORNERS):
        other, length = SPANS[7 - number]
        placed_ref[other : other + length, :] = result[place * TZ : (place + 1) * TZ, :]
    dw_ref[...] = total[...].astype(BF)


def backward_kernel(grad_ref, own_ref, lm_ref, w_ref, out_ref, grad_t, total):
    step = pl.program_id(0)

    @pl.when(step == 0)
    def _():
        grad_t[...] = grad_ref[...].astype(F32).T.astype(BF)
        total[...] = dot(w_ref[13], own_ref[...].astype(F32).T.astype(BF))

    pair = pair_of(step)
    weight = jnp.concatenate([w_ref[k] for k in pair], 1)
    gathered = [dot(grad_t[...], hot(lm_ref[26 - k], ROWS)).astype(BF) for k in pair]
    total[...] += dot(weight, jnp.concatenate(gathered, 0))

    @pl.when(step == 12)
    def _():
        out_ref[...] = total[...].T


def final_kernel(local_ref, placed_ref, rr_ref, act_ref, pair_ref, mixed_ref, out_ref):
    placed = placed_ref[...]
    high = placed.astype(BF)
    low = (placed - high.astype(F32)).astype(BF)
    both = dot(hot(rr_ref[...], ROWS), jnp.concatenate([high, low], 1))
    out_ref[...] = (local_ref[...] + both[:, :C] + both[:, C:]).astype(BF)
    mixed_ref[...] = (act_ref[...].astype(F32) + pair_ref[...].astype(F32)).astype(BF)


PARAMS = pltpu.CompilerParams(vmem_limit_bytes=48 * 2**20)


def shape(dims, dtype):
    return jax.ShapeDtypeStruct(dims, dtype)


def whole(dims):
    return pl.BlockSpec(dims, lambda *ids: (0,) * len(dims))


def shifted(value, steps):
    count = lax.axis_size("space")
    initial, last = (max(0, -steps), min(count, count - steps))
    return lax.ppermute(value, "space", [(i, i + steps) for i in range(initial, last)])


def exchange(lists, orient):
    received = []
    for number, (step_x, step_y) in enumerate(DIRECTIONS):
        start, length = SPANS[number]
        received.append(
            shifted(lists[start : start + length], orient * (step_x + TILES_X * step_y))
        )
    return jnp.concatenate(received, 0)


def swapped(array):
    return lax.ppermute(array, "segment", [(i, i ^ 1) for i in range(lax.axis_size("segment"))])


def xor_send(value, bits):
    return lax.ppermute(value, "space", [(i, i ^ bits) for i in range(lax.axis_size("space"))])


def add_up(pieces):
    total = pieces[0].astype(F32)
    for piece in pieces[1:]:
        total = total + piece.astype(F32)
    return total.astype(BF)


def reduce_weights(dw):
    me = lax.axis_index("space")
    core, x_at = me % 2, me // 2 % 4
    halves = dw.reshape(2, -1, C)
    pick = functools.partial(lax.dynamic_index_in_dim, axis=0, keepdims=False)
    half = add_up([pick(halves, core), xor_send(pick(halves, 1 - core), 1)])
    quarters = half.reshape(4, -1, C)
    got = [pick(quarters, x_at)]
    for bits in (1, 2, 3):
        got.append(xor_send(pick(quarters, x_at ^ bits), bits * 2))
    quarter = add_up(got)
    got = [xor_send(quarter, bits * 8) for bits in (1, 2, 3)]
    z_at = me // 8
    stacked = jnp.stack([quarter] + got)
    quarter = add_up([pick(stacked, z_at ^ index) for index in range(4)])
    got = jnp.stack([quarter] + [xor_send(quarter, bits * 2) for bits in (1, 2, 3)])
    half = jnp.stack([pick(got, x_at ^ index) for index in range(4)])
    got = jnp.stack([half, xor_send(half, 1)])
    both = jnp.stack([pick(got, core), pick(got, 1 - core)])
    return both.reshape(dw.shape).astype(F32)


def on_device(features, weights, cotangent, local_map, send_map, recv_map):
    x = features[0]
    w = weights[0]
    cot = cotangent[0]
    lm = local_map.T.reshape(27, 1, ROWS)
    sm = send_map.T.reshape(27, 1, HALO)
    rr = recv_map.reshape(1, HALO)
    rc = recv_map.reshape(HALO, 1)
    part, face_g, corner_g = pl.pallas_call(
        start_kernel,
        out_shape=[shape((HALO, C), BF), shape((4, 9 * C, CAP), BF), shape((12 * C, 4 * TZ), BF)],
        compiler_params=PARAMS,
        name="start",
    )(x, rr, rc, sm, w)
    arrived = exchange(part, 1)
    cot_pair = swapped(cot)
    gathered, pre = pl.pallas_call(
        functools.partial(forward_kernel, width=512),
        grid=(13,),
        in_specs=[whole((ROWS, C)), whole((27, 1, ROWS)), whole((27, C, C))],
        out_specs=[pl.BlockSpec((2 * C, ROWS), lambda j: (j, 0)), whole((ROWS, C))],
        out_shape=[shape((26 * C, ROWS), BF), shape((ROWS, C), F32)],
        scratch_shapes=[pltpu.VMEM((C, ROWS), BF), pltpu.VMEM((C, ROWS), F32)],
        compiler_params=PARAMS,
        name="forward",
    )(x, lm, w)
    act, grad, outgoing = pl.pallas_call(
        activate_kernel,
        out_shape=[shape((ROWS, C), BF), shape((ROWS, C), BF), shape((HALO, C), BF)],
        compiler_params=PARAMS,
        name="activate",
    )(pre, arrived, rr, cot, cot_pair)
    returned = exchange(outgoing, -1)
    act_pair = swapped(act)
    dw_local = pl.pallas_call(
        weight_kernel,
        grid=(13,),
        in_specs=[pl.BlockSpec((2 * C, ROWS), lambda j: (j, 0)), whole((ROWS, C)), whole((ROWS, C))],
        out_specs=whole((27, C, C)),
        out_shape=shape((27, C, C), F32),
        compiler_params=PARAMS,
        name="weight",
    )(gathered, grad, x)
    dw, placed = pl.pallas_call(
        return_kernel,
        out_shape=[shape((27, C, C), BF), shape((HALO, C), F32)],
        scratch_shapes=[pltpu.VMEM((27, C, C), F32)],
        compiler_params=PARAMS,
        name="returning",
    )(returned, rc, sm, w, face_g, corner_g, dw_local)
    weight_grad = reduce_weights(dw)
    parts = []
    size = ROWS // 2
    for begin in range(0, ROWS, size):
        parts.append(
            pl.pallas_call(
                backward_kernel,
                grid=(13,),
                in_specs=[whole((ROWS, C)), pl.BlockSpec((size, C), lambda j, at=begin // size: (at, 0)),
                          pl.BlockSpec((27, 1, size), lambda j, at=begin // size: (0, 0, at)), whole((27, C, C))],
                out_specs=whole((size, C)),
                out_shape=shape((size, C), F32),
                scratch_shapes=[pltpu.VMEM((C, ROWS), BF), pltpu.VMEM((C, size), F32)],
                compiler_params=PARAMS,
                name="backward",
            )(grad, grad, lm, w)
        )
    local = jnp.concatenate(parts, 0)
    mixed, input_grad = pl.pallas_call(
        final_kernel,
        out_shape=[shape((ROWS, C), BF), shape((ROWS, C), BF)],
        compiler_params=PARAMS,
        name="final",
    )(local, placed, rr, act, act_pair)
    return (mixed[None], input_grad[None], weight_grad[None])


def solution(mesh):
    in_specs = (
        P("segment", "space", None),
        P("segment", None, None, None),
        P("segment", "space", None),
        P("space", None),
        P("space", None),
        P("space"),
    )
    out_specs = (
        P("segment", "space", None),
        P("segment", "space", None),
        P("segment", None, None, None),
    )
    return jax.shard_map(
        on_device, mesh=mesh, in_specs=in_specs, out_specs=out_specs, check_vma=False
    )
```

```python
import functools

import jax
import jax.numpy as jnp
from jax import lax
from jax.experimental import pallas as pl
from jax.experimental.pallas import tpu as pltpu
from jax.sharding import PartitionSpec as P

TZ = 32
TILES_X = 4
CAP = 256
ROWS = 1024
C = 128
HALO = 1152

DIRECTIONS = ((-1, -1), (-1, 0), (-1, 1), (0, -1), (0, 1), (1, -1), (1, 0), (1, 1))
BF = jnp.bfloat16
F32 = jnp.float32


def spans():
    result = []
    start = 0
    for step_x, step_y in DIRECTIONS:
        length = TZ if step_x != 0 and step_y != 0 else CAP
        result.append((start, length))
        start = start + length
    return result


SPANS = spans()
FACES = [n for n, (a, b) in enumerate(DIRECTIONS) if a == 0 or b == 0]
CORNERS = [n for n, (a, b) in enumerate(DIRECTIONS) if a != 0 and b != 0]


def toward(step_x, step_y):
    picked = []
    for offset in range(27):
        along_x = offset // 9 - 1
        along_y = offset // 3 % 3 - 1
        if (step_x == 0 or along_x == -step_x) and (step_y == 0 or along_y == -step_y):
            picked.append(offset)
    return picked


def dot(a, b, dims=((1,), (0,))):
    return lax.dot_general(a, b, (dims, ((), ())), preferred_element_type=F32)


def hot(row, rows):
    pos = lax.broadcasted_iota(jnp.int32, (256, 128), 0).astype(jnp.int16)
    count = row.shape[1]
    blocks = []
    for base in range(0, rows, 256):
        rel = (row - base).astype(jnp.int16)
        parts = [
            jnp.where(rel[:, t : t + 128] == pos, BF(1), BF(0)) for t in range(0, count, 128)
        ]
        blocks.append(jnp.concatenate(parts, 1))
    return jnp.concatenate(blocks, 0)


def match(column, row):
    return jnp.where(column == row.astype(jnp.int16), BF(1), BF(0))


def spread(column, count):
    kept = jnp.where(column == ROWS, -1, column)
    return jnp.broadcast_to(kept, (column.shape[0], count)).astype(jnp.int16)


def corner_mask(position, axis, shape):
    lane = lax.broadcasted_iota(jnp.int32, shape, axis)
    return (lane // TZ) == position


def lists_of(number):
    return SPANS[number]


def face_match(number, offset, column, sm_ref):
    start, length = SPANS[number]
    return match(column, sm_ref[offset, :, start : start + length])


def corner_row(place, sm_ref):
    pieces = []
    for number in CORNERS:
        start, length = SPANS[number]
        offset = toward(*DIRECTIONS[number])[place]
        pieces.append(sm_ref[offset, :, start : start + length])
    return jnp.concatenate(pieces, 1)


def corner_column(rc_ref, count):
    pieces = []
    for number in CORNERS:
        start, length = SPANS[7 - number]
        pieces.append(rc_ref[start : start + length, :])
    return spread(jnp.concatenate(pieces, 0), count)


def number_of(step_x, step_y):
    return DIRECTIONS.index((step_x, step_y))


def pack_sides(lists, orient, sides, xa_ref, xb_ref, ya_ref, yb_ref):
    x_odd, y_odd = sides[0] == 1, sides[1] == 1

    def x_side(side):
        picked = [(orient * side, 0), (orient * side, -orient), (orient * side, orient)]
        return jnp.concatenate([lists[number_of(*d)] for d in picked], 0)

    plus, minus = x_side(1), x_side(-1)
    xa_ref[...] = jnp.where(x_odd, minus, plus)
    xb_ref[...] = jnp.where(x_odd, plus, minus)
    plus, minus = lists[number_of(0, orient)], lists[number_of(0, -orient)]
    ya_ref[...] = jnp.where(y_odd, minus, plus)
    yb_ref[...] = jnp.where(y_odd, plus, minus)


def unpack_sides(orient, sides, xa, xb, ya, yb):
    x_odd, y_odd = sides[0] == 1, sides[1] == 1

    def of_side(side, odd, a, b):
        return jnp.where(odd, b, a) if side == 1 else jnp.where(odd, a, b)

    lists = []
    for step_x, step_y in DIRECTIONS:
        if step_y == 0:
            lists.append(of_side(-orient * step_x, x_odd, xa[:CAP], xb[:CAP]))
        elif step_x == 0:
            lists.append(of_side(-orient * step_y, y_odd, ya[:CAP], yb[:CAP]))
        else:
            first = of_side(-orient * step_y, y_odd, ya[CAP : CAP + TZ], yb[CAP : CAP + TZ])
            second = of_side(-orient * step_y, y_odd, ya[CAP + TZ :], yb[CAP + TZ :])
            lists.append(of_side(-orient * step_x, x_odd, first, second))
    return lists


def start_kernel(side_ref, x_ref, rr_ref, rc_ref, sm_ref, w_ref, xa_ref, xb_ref, ya_ref, yb_ref, face_g_ref, corner_g_ref):
    lists = [None] * 8
    x_t = x_ref[...].astype(F32).T.astype(BF)
    selector = hot(rr_ref[...], ROWS)
    listed = dot(x_t, selector).astype(BF)
    for place, number in enumerate(FACES):
        start, length = SPANS[number]
        other, _ = SPANS[7 - number]
        column = spread(rc_ref[other : other + length, :], length)
        source = listed[:, other : other + length]
        picked = toward(*DIRECTIONS[number])
        gathered = []
        for offset in picked:
            chosen = face_match(number, offset, column, sm_ref)
            gathered.append(dot(source, chosen).astype(BF))
        gathered = jnp.concatenate(gathered, 0)
        face_g_ref[place] = gathered
        weight = jnp.concatenate([w_ref[offset] for offset in picked], 0)
        total = dot(weight, gathered, ((0,), (0,)))
        lists[number] = total.T.astype(BF)
    column = corner_column(rc_ref, 4 * TZ)
    source = jnp.concatenate(
        [listed[:, SPANS[7 - n][0] : SPANS[7 - n][0] + TZ] for n in CORNERS], 1
    )
    gathered = []
    for step in range(3):
        chosen = match(column, corner_row(step, sm_ref))
        gathered.append(dot(source, chosen).astype(BF))
    masked = []
    weights = []
    for place, number in enumerate(CORNERS):
        inside = corner_mask(place, 1, (C, 4 * TZ))
        for step in range(3):
            masked.append(jnp.where(inside, gathered[step], BF(0)))
            weights.append(w_ref[toward(*DIRECTIONS[number])[step]])
    masked = jnp.concatenate(masked, 0)
    corner_g_ref[...] = masked
    total = dot(jnp.concatenate(weights, 0), masked, ((0,), (0,))).T.astype(BF)
    for place, number in enumerate(CORNERS):
        lists[number] = total[place * TZ : (place + 1) * TZ, :]
    pack_sides(lists, 1, (side_ref[0], side_ref[1]), xa_ref, xb_ref, ya_ref, yb_ref)


def pair_of(step):
    first = jnp.where(2 * step >= 13, 2 * step + 1, 2 * step)
    second = jnp.where(2 * step + 1 >= 13, 2 * step + 2, 2 * step + 1)
    return first, second


def forward_kernel(x_ref, lm_ref, w_ref, g_ref, pre_ref, x_t, total, *, width):
    step = pl.program_id(0)

    @pl.when(step == 0)
    def _():
        x_t[...] = x_ref[...].astype(F32).T.astype(BF)
        total[...] = dot(w_ref[13], x_t[...], ((0,), (0,)))

    pair = pair_of(step)
    weight = jnp.concatenate([w_ref[k] for k in pair], 0)
    for begin in range(0, ROWS, width):
        cols = slice(begin, begin + width)
        gathered = [dot(x_t[...], hot(lm_ref[k, :, cols], ROWS)).astype(BF) for k in pair]
        gathered = jnp.concatenate(gathered, 0)
        g_ref[:, cols] = gathered
        total[:, cols] += dot(weight, gathered, ((0,), (0,)))

    @pl.when(step == 12)
    def _():
        pre_ref[...] = total[...].T


def activate_kernel(
    side_ref, pre_ref, ixa_ref, ixb_ref, iya_ref, iyb_ref, rr_ref, cot_ref, pair_ref,
    act_ref, grad_ref, xa_ref, xb_ref, ya_ref, yb_ref,
):
    sides = (side_ref[0], side_ref[1])
    arrived = unpack_sides(1, sides, ixa_ref[...], ixb_ref[...], iya_ref[...], iyb_ref[...])
    selector = hot(rr_ref[...], ROWS)
    pre = pre_ref[...] + dot(selector, jnp.concatenate(arrived, 0))
    gate = 1.0 / (1.0 + jnp.exp(-pre))
    act_ref[...] = (pre * gate).astype(BF)
    upstream = cot_ref[...].astype(F32) + pair_ref[...].astype(F32)
    grad = upstream * gate * (1.0 + pre * (1.0 - gate))
    grad_ref[...] = grad.astype(BF)
    listed = dot(grad.T.astype(BF), selector).T.astype(BF)
    lists = [listed[start : start + length] for start, length in SPANS]
    pack_sides(lists, -1, sides, xa_ref, xb_ref, ya_ref, yb_ref)


def weight_kernel(g_ref, grad_ref, x_ref, dw_ref):
    step = pl.program_id(0)

    @pl.when(step == 0)
    def _():
        dw_ref[13] = dot(x_ref[...], grad_ref[...], ((0,), (0,)))

    total = dot(g_ref[...], grad_ref[...])
    dw_ref[pl.ds(14 * step, 13)] = total.reshape(13, C, C)


def return_kernel(side_ref, ixa_ref, ixb_ref, iya_ref, iyb_ref, rc_ref, sm_ref, w_ref, face_g_ref, corner_g_ref, dw_in_ref, dw_ref, placed_ref, total):
    total[...] = dw_in_ref[...]
    sides = (side_ref[0], side_ref[1])
    returned = unpack_sides(-1, sides, ixa_ref[...], ixb_ref[...], iya_ref[...], iyb_ref[...])
    for place, number in enumerate(FACES):
        start, length = SPANS[number]
        other, _ = SPANS[7 - number]
        column = spread(rc_ref[other : other + length, :], length)
        back = returned[number]
        picked = toward(*DIRECTIONS[number])
        pieces = []
        for offset in picked:
            chosen = face_match(number, offset, column, sm_ref)
            pieces.append(dot(chosen, back).astype(BF))
        pieces = jnp.concatenate(pieces, 1)
        weight = jnp.concatenate([w_ref[offset] for offset in picked], 1)
        placed_ref[other : other + length, :] = dot(pieces, weight, ((1,), (1,)))
        kernel_part = dot(face_g_ref[place], back)
        for index, offset in enumerate(picked):
            total[offset] += kernel_part[index * C : (index + 1) * C, :]
    column = corner_column(rc_ref, 4 * TZ)
    back = jnp.concatenate([returned[n] for n in CORNERS], 0)
    kernel_part = dot(corner_g_ref[...], back)
    pieces = []
    weights = []
    spots = [dot(match(column, corner_row(step, sm_ref)), back).astype(BF) for step in range(3)]
    for place, number in enumerate(CORNERS):
        inside = corner_mask(place, 0, (4 * TZ, C))
        for step in range(3):
            offset = toward(*DIRECTIONS[number])[step]
            row = (place * 3 + step) * C
            total[offset] += kernel_part[row : row + C, :]
            pieces.append(jnp.where(inside, spots[step], BF(0)))
            weights.append(w_ref[offset])
    result = dot(jnp.concatenate(pieces, 1), jnp.concatenate(weights, 1), ((1,), (1,)))
    for place, number in enumerate(CORNERS):
        other, length = SPANS[7 - number]
        placed_ref[other : other + length, :] = result[place * TZ : (place + 1) * TZ, :]
    dw_ref[...] = total[...].astype(BF)


def backward_kernel(grad_ref, own_ref, lm_ref, w_ref, out_ref, grad_t, total):
    step = pl.program_id(0)

    @pl.when(step == 0)
    def _():
        grad_t[...] = grad_ref[...].astype(F32).T.astype(BF)
        total[...] = dot(w_ref[13], own_ref[...].astype(F32).T.astype(BF))

    pair = pair_of(step)
    weight = jnp.concatenate([w_ref[k] for k in pair], 1)
    gathered = [dot(grad_t[...], hot(lm_ref[26 - k], ROWS)).astype(BF) for k in pair]
    total[...] += dot(weight, jnp.concatenate(gathered, 0))

    @pl.when(step == 12)
    def _():
        out_ref[...] = total[...].T


def final_kernel(local_ref, placed_ref, rr_ref, act_ref, pair_ref, mixed_ref, out_ref):
    placed = placed_ref[...]
    high = placed.astype(BF)
    low = (placed - high.astype(F32)).astype(BF)
    both = dot(hot(rr_ref[...], ROWS), jnp.concatenate([high, low], 1))
    out_ref[...] = (local_ref[...] + both[:, :C] + both[:, C:]).astype(BF)
    mixed_ref[...] = (act_ref[...].astype(F32) + pair_ref[...].astype(F32)).astype(BF)


PARAMS = pltpu.CompilerParams(vmem_limit_bytes=48 * 2**20)


def shape(dims, dtype):
    return jax.ShapeDtypeStruct(dims, dtype)


def whole(dims):
    return pl.BlockSpec(dims, lambda *ids: (0,) * len(dims))


def pairing(axis, which):
    pairs = []
    for tile in range(lax.axis_size("space")):
        at_x, at_y = tile % TILES_X, tile // TILES_X
        tiles_y = lax.axis_size("space") // TILES_X
        if axis == "x":
            move = 1 if (at_x + which) % 2 == 0 else -1
            at_x = (at_x + move) % TILES_X
        else:
            move = 1 if (at_y + which) % 2 == 0 else -1
            at_y = (at_y + move) % tiles_y
        pairs.append((tile, at_y * TILES_X + at_x))
    return pairs


def exchange_x(xa, xb):
    return [lax.ppermute(v, "space", pairing("x", n)) for n, v in enumerate((xa, xb))]


def exchange_y(ya, yb, xa, xb, sides):
    sent = []
    for which, own in enumerate((ya, yb)):
        down = sides[1] != which
        corners = [jnp.where(down, v[CAP : CAP + TZ], v[CAP + TZ :]) for v in (xa, xb)]
        sent.append(jnp.concatenate([own] + corners, 0))
    return [lax.ppermute(v, "space", pairing("y", n)) for n, v in enumerate(sent)]


def swapped(array):
    return lax.ppermute(array, "segment", [(i, i ^ 1) for i in range(lax.axis_size("segment"))])


def xor_send(value, bits):
    return lax.ppermute(value, "space", [(i, i ^ bits) for i in range(lax.axis_size("space"))])


def add_up(pieces):
    total = pieces[0].astype(F32)
    for piece in pieces[1:]:
        total = total + piece.astype(F32)
    return total.astype(BF)


def pick(array, index):
    return lax.dynamic_index_in_dim(array, index, 0, False)


def cost(flops, data):
    return pl.CostEstimate(flops=int(flops), bytes_accessed=int(data), transcendentals=0)


def tie(value, other):
    return lax.optimization_barrier((value, other))[0]


def on_device(features, weights, cotangent, local_map, send_map, recv_map):
    x = features[0]
    w = weights[0]
    cot = cotangent[0]
    lm = local_map.T.reshape(27, 1, ROWS)
    sm = send_map.T.reshape(27, 1, HALO)
    rr = recv_map.reshape(1, HALO)
    rc = recv_map.reshape(HALO, 1)
    me = lax.axis_index("space")
    sides = jnp.stack([me % 2, me // TILES_X % 2]).astype(jnp.int32)
    smem = pl.BlockSpec(memory_space=pltpu.SMEM)
    vmem = pl.BlockSpec(memory_space=pltpu.VMEM)
    out_lists = [shape((CAP + 2 * TZ, C), BF)] * 2 + [shape((CAP, C), BF)] * 2
    xa, xb, ya, yb, face_g, corner_g = pl.pallas_call(
        start_kernel,
        in_specs=[smem] + [vmem] * 5,
        out_shape=out_lists + [shape((4, 9 * C, CAP), BF), shape((12 * C, 4 * TZ), BF)],
        compiler_params=PARAMS,
        cost_estimate=cost(2e9, 4e6),
        name="start",
    )(sides, x, rr, rc, sm, w)
    cot_pair = swapped(cot)
    in_x = exchange_x(xa, xb)
    in_y = exchange_y(ya, yb, *in_x, sides)
    gathered, pre = pl.pallas_call(
        functools.partial(forward_kernel, width=512),
        grid=(13,),
        in_specs=[whole((ROWS, C)), whole((27, 1, ROWS)), whole((27, C, C))],
        out_specs=[pl.BlockSpec((2 * C, ROWS), lambda j: (j, 0)), whole((ROWS, C))],
        out_shape=[shape((26 * C, ROWS), BF), shape((ROWS, C), F32)],
        scratch_shapes=[pltpu.VMEM((C, ROWS), BF), pltpu.VMEM((C, ROWS), F32)],
        compiler_params=PARAMS,
        cost_estimate=cost(15e9, 9e6),
        name="forward",
    )(x, lm, w)
    act, grad, xa, xb, ya, yb = pl.pallas_call(
        activate_kernel,
        in_specs=[smem] + [vmem] * 8,
        out_shape=[shape((ROWS, C), BF)] * 2 + out_lists,
        compiler_params=PARAMS,
        cost_estimate=cost(1.5e9, 3e6),
        name="activate",
    )(sides, pre, *in_x, *in_y, rr, cot, cot_pair)
    in_x = exchange_x(xa, xb)
    in_y = exchange_y(ya, yb, *in_x, sides)
    dw_local = pl.pallas_call(
        weight_kernel,
        grid=(2,),
        in_specs=[pl.BlockSpec((13 * C, ROWS), lambda j: (j, 0)), whole((ROWS, C)), whole((ROWS, C))],
        out_specs=whole((27, C, C)),
        out_shape=shape((27, C, C), F32),
        compiler_params=PARAMS,
        cost_estimate=cost(4e9, 9e6),
        name="weight",
    )(gathered, grad, x)

    size = ROWS // 4

    def backward(index, grad):
        return pl.pallas_call(
            backward_kernel,
            grid=(13,),
            in_specs=[whole((ROWS, C)), pl.BlockSpec((size, C), lambda j: (index, 0)),
                      pl.BlockSpec((27, 1, size), lambda j: (0, 0, index)), whole((27, C, C))],
            out_specs=whole((size, C)),
            out_shape=shape((size, C), F32),
            scratch_shapes=[pltpu.VMEM((C, ROWS), BF), pltpu.VMEM((C, size), F32)],
            compiler_params=PARAMS,
            cost_estimate=cost(5e9, 2e6),
            name="backward",
        )(grad, grad, lm, w)

    locals_ = [backward(0, tie(grad, dw_local))]
    dw, placed = pl.pallas_call(
        return_kernel,
        in_specs=[smem] + [vmem] * 10,
        out_shape=[shape((27, C, C), BF), shape((HALO, C), F32)],
        scratch_shapes=[pltpu.VMEM((27, C, C), F32)],
        compiler_params=PARAMS,
        cost_estimate=cost(3e9, 4e6),
        name="returning",
    )(sides, *in_x, *in_y, rc, sm, w, face_g, corner_g, tie(dw_local, locals_[0]))
    act_pair = swapped(tie(act, dw))

    core, x_at, z_at = me % 2, me // 2 % 4, me // 8
    halves = dw.reshape(2, -1, C)
    got = xor_send(pick(halves, 1 - core), 1)
    locals_.append(backward(1, tie(grad, dw)))
    half = add_up([pick(halves, core), tie(got, locals_[1])])
    quarters = half.reshape(4, -1, C)
    got = [xor_send(pick(quarters, x_at ^ bits), bits * 2) for bits in (1, 2, 3)]
    locals_.append(backward(2, tie(grad, half)))
    quarter = add_up([pick(quarters, x_at)] + [tie(v, locals_[2]) for v in got])
    got = [xor_send(quarter, bits * 8) for bits in (1, 2, 3)]
    locals_.append(backward(3, tie(grad, quarter)))
    stacked = jnp.stack([quarter] + [tie(v, locals_[3]) for v in got])
    quarter = add_up([pick(stacked, z_at ^ index) for index in range(4)])
    got = jnp.stack([quarter] + [xor_send(quarter, bits * 2) for bits in (1, 2, 3)])
    local = tie(jnp.concatenate(locals_, 0), quarter)
    mixed, input_grad = pl.pallas_call(
        final_kernel,
        out_shape=[shape((ROWS, C), BF), shape((ROWS, C), BF)],
        compiler_params=PARAMS,
        cost_estimate=cost(1e9, 3e6),
        name="final",
    )(local, placed, rr, act, act_pair)
    half = jnp.stack([pick(got, x_at ^ index) for index in range(4)])
    got = jnp.stack([half, xor_send(half, 1)])
    both = jnp.stack([pick(got, core), pick(got, 1 - core)])
    weight_grad = both.reshape(dw.shape).astype(F32)
    return (mixed[None], input_grad[None], weight_grad[None])


def solution(mesh):
    in_specs = (
        P("segment", "space", None),
        P("segment", None, None, None),
        P("segment", "space", None),
        P("space", None),
        P("space", None),
        P("space"),
    )
    out_specs = (
        P("segment", "space", None),
        P("segment", "space", None),
        P("segment", None, None, None),
    )
    return jax.shard_map(
        on_device, mesh=mesh, in_specs=in_specs, out_specs=out_specs, check_vma=False
    )
```

```python
import functools

import jax
import jax.numpy as jnp
from jax import lax
from jax.experimental import pallas as pl
from jax.experimental.pallas import tpu as pltpu
from jax.sharding import PartitionSpec as P

TZ = 32
TILES_X = 4
CAP = 256
ROWS = 1024
C = 128
HALO = 1152

DIRECTIONS = ((-1, -1), (-1, 0), (-1, 1), (0, -1), (0, 1), (1, -1), (1, 0), (1, 1))
BF = jnp.bfloat16
F32 = jnp.float32


def spans():
    result = []
    start = 0
    for step_x, step_y in DIRECTIONS:
        length = TZ if step_x != 0 and step_y != 0 else CAP
        result.append((start, length))
        start = start + length
    return result


SPANS = spans()
FACES = [n for n, (a, b) in enumerate(DIRECTIONS) if a == 0 or b == 0]
CORNERS = [n for n, (a, b) in enumerate(DIRECTIONS) if a != 0 and b != 0]


def toward(step_x, step_y):
    picked = []
    for offset in range(27):
        along_x = offset // 9 - 1
        along_y = offset // 3 % 3 - 1
        if (step_x == 0 or along_x == -step_x) and (step_y == 0 or along_y == -step_y):
            picked.append(offset)
    return picked


def dot(a, b, dims=((1,), (0,))):
    return lax.dot_general(a, b, (dims, ((), ())), preferred_element_type=F32)


def hot(row, rows):
    pos = lax.broadcasted_iota(jnp.int32, (256, 128), 0).astype(jnp.int16)
    count = row.shape[1]
    blocks = []
    for base in range(0, rows, 256):
        rel = (row - base).astype(jnp.int16)
        parts = [
            jnp.where(rel[:, t : t + 128] == pos, BF(1), BF(0)) for t in range(0, count, 128)
        ]
        blocks.append(jnp.concatenate(parts, 1))
    return jnp.concatenate(blocks, 0)


def match(column, row):
    return jnp.where(column == row.astype(jnp.int16), BF(1), BF(0))


def spread(column, count):
    kept = jnp.where(column == ROWS, -1, column)
    return jnp.broadcast_to(kept, (column.shape[0], count)).astype(jnp.int16)


def column_of(row):
    return jnp.broadcast_to(row.astype(F32), (8, row.shape[1])).T[:, :1].astype(jnp.int32)


def corner_mask(position, axis, shape):
    lane = lax.broadcasted_iota(jnp.int32, shape, axis)
    return (lane // TZ) == position


def lists_of(number):
    return SPANS[number]


def face_match(number, offset, column, sm_ref):
    start, length = SPANS[number]
    return match(column, sm_ref[offset : offset + 1, start : start + length])


def corner_row(place, sm_ref):
    pieces = []
    for number in CORNERS:
        start, length = SPANS[number]
        offset = toward(*DIRECTIONS[number])[place]
        pieces.append(sm_ref[offset : offset + 1, start : start + length])
    return jnp.concatenate(pieces, 1)


def corner_column(rc, count):
    pieces = []
    for number in CORNERS:
        start, length = SPANS[7 - number]
        pieces.append(rc[start : start + length, :])
    return spread(jnp.concatenate(pieces, 0), count)


def number_of(step_x, step_y):
    return DIRECTIONS.index((step_x, step_y))


def pack_sides(lists, orient, sides, xa_ref, xb_ref, ya_ref, yb_ref):
    x_odd, y_odd = sides[0] == 1, sides[1] == 1

    def x_side(side):
        picked = [(orient * side, 0), (orient * side, -orient), (orient * side, orient)]
        return jnp.concatenate([lists[number_of(*d)] for d in picked], 0)

    plus, minus = x_side(1), x_side(-1)
    xa_ref[...] = jnp.where(x_odd, minus, plus)
    xb_ref[...] = jnp.where(x_odd, plus, minus)
    plus, minus = lists[number_of(0, orient)], lists[number_of(0, -orient)]
    ya_ref[...] = jnp.where(y_odd, minus, plus)
    yb_ref[...] = jnp.where(y_odd, plus, minus)


def unpack_sides(orient, sides, xa, xb, ya, yb):
    x_odd, y_odd = sides[0] == 1, sides[1] == 1

    def of_side(side, odd, a, b):
        return jnp.where(odd, b, a) if side == 1 else jnp.where(odd, a, b)

    lists = []
    for step_x, step_y in DIRECTIONS:
        if step_y == 0:
            lists.append(of_side(-orient * step_x, x_odd, xa[:CAP], xb[:CAP]))
        elif step_x == 0:
            lists.append(of_side(-orient * step_y, y_odd, ya[:CAP], yb[:CAP]))
        else:
            first = of_side(-orient * step_y, y_odd, ya[CAP : CAP + TZ], yb[CAP : CAP + TZ])
            second = of_side(-orient * step_y, y_odd, ya[CAP + TZ :], yb[CAP + TZ :])
            lists.append(of_side(-orient * step_x, x_odd, first, second))
    return lists


def start_kernel(side_ref, x_ref, rr_ref, sm_ref, w_ref, xa_ref, xb_ref, ya_ref, yb_ref, face_g_ref, corner_g_ref):
    lists = [None] * 8
    rc = column_of(rr_ref[...])
    x_t = x_ref[...].astype(F32).T.astype(BF)
    selector = hot(rr_ref[...], ROWS)
    listed = dot(x_t, selector).astype(BF)
    for place, number in enumerate(FACES):
        start, length = SPANS[number]
        other, _ = SPANS[7 - number]
        column = spread(rc[other : other + length, :], length)
        source = listed[:, other : other + length]
        picked = toward(*DIRECTIONS[number])
        gathered = []
        for offset in picked:
            chosen = face_match(number, offset, column, sm_ref)
            gathered.append(dot(source, chosen).astype(BF))
        gathered = jnp.concatenate(gathered, 0)
        face_g_ref[place] = gathered
        weight = jnp.concatenate([w_ref[offset] for offset in picked], 0)
        total = dot(weight, gathered, ((0,), (0,)))
        lists[number] = total.T.astype(BF)
    column = corner_column(rc, 4 * TZ)
    source = jnp.concatenate(
        [listed[:, SPANS[7 - n][0] : SPANS[7 - n][0] + TZ] for n in CORNERS], 1
    )
    gathered = []
    for step in range(3):
        chosen = match(column, corner_row(step, sm_ref))
        gathered.append(dot(source, chosen).astype(BF))
    masked = []
    weights = []
    for place, number in enumerate(CORNERS):
        inside = corner_mask(place, 1, (C, 4 * TZ))
        for step in range(3):
            masked.append(jnp.where(inside, gathered[step], BF(0)))
            weights.append(w_ref[toward(*DIRECTIONS[number])[step]])
    masked = jnp.concatenate(masked, 0)
    corner_g_ref[...] = masked
    total = dot(jnp.concatenate(weights, 0), masked, ((0,), (0,))).T.astype(BF)
    for place, number in enumerate(CORNERS):
        lists[number] = total[place * TZ : (place + 1) * TZ, :]
    pack_sides(lists, 1, (side_ref[0], side_ref[1]), xa_ref, xb_ref, ya_ref, yb_ref)


def forward_kernel(x_ref, lm_ref, w_ref, g_ref, pre_ref, x_t, total, *, width):
    step = pl.program_id(0)

    @pl.when(step == 0)
    def _():
        x_t[...] = x_ref[...].astype(F32).T.astype(BF)
        total[...] = dot(w_ref[13], x_t[...], ((0,), (0,)))

    source = x_t[...]
    weight = jnp.concatenate([w_ref[14 * step + i] for i in range(13)], 0)
    for begin in range(0, ROWS, width):
        cols = slice(begin, begin + width)
        gathered = [
            dot(source, hot(lm_ref[pl.ds(14 * step + i, 1), cols], ROWS)).astype(BF) for i in range(13)
        ]
        gathered = jnp.concatenate(gathered, 0)
        g_ref[:, cols] = gathered
        total[:, cols] += dot(weight, gathered, ((0,), (0,)))

    @pl.when(step == 1)
    def _():
        pre_ref[...] = total[...].T


def activate_kernel(
    side_ref, pre_ref, ixa_ref, ixb_ref, iya_ref, iyb_ref, rr_ref, cot_ref, pair_ref,
    act_ref, grad_ref, xa_ref, xb_ref, ya_ref, yb_ref,
):
    sides = (side_ref[0], side_ref[1])
    arrived = unpack_sides(1, sides, ixa_ref[...], ixb_ref[...], iya_ref[...], iyb_ref[...])
    selector = hot(rr_ref[...], ROWS)
    pre = pre_ref[...] + dot(selector, jnp.concatenate(arrived, 0))
    gate = 1.0 / (1.0 + jnp.exp(-pre))
    act_ref[...] = (pre * gate).astype(BF)
    upstream = cot_ref[...].astype(F32) + pair_ref[...].astype(F32)
    grad = upstream * gate * (1.0 + pre * (1.0 - gate))
    grad_ref[...] = grad.astype(BF)
    listed = dot(grad.T.astype(BF), selector).T.astype(BF)
    lists = [listed[start : start + length] for start, length in SPANS]
    pack_sides(lists, -1, sides, xa_ref, xb_ref, ya_ref, yb_ref)


def weight_kernel(g_ref, grad_ref, x_ref, dw_ref):
    step = pl.program_id(0)

    @pl.when(step == 0)
    def _():
        dw_ref[13] = dot(x_ref[...], grad_ref[...], ((0,), (0,)))

    total = dot(g_ref[...], grad_ref[...])
    dw_ref[pl.ds(14 * step, 13)] = total.reshape(13, C, C)


def return_kernel(side_ref, ixa_ref, ixb_ref, iya_ref, iyb_ref, rr_ref, sm_ref, w_ref, face_g_ref, corner_g_ref, dw_in_ref, dw_ref, placed_ref, total):
    total[...] = dw_in_ref[...]
    rc = column_of(rr_ref[...])
    sides = (side_ref[0], side_ref[1])
    returned = unpack_sides(-1, sides, ixa_ref[...], ixb_ref[...], iya_ref[...], iyb_ref[...])
    for place, number in enumerate(FACES):
        start, length = SPANS[number]
        other, _ = SPANS[7 - number]
        column = spread(rc[other : other + length, :], length)
        back = returned[number]
        picked = toward(*DIRECTIONS[number])
        pieces = []
        for offset in picked:
            chosen = face_match(number, offset, column, sm_ref)
            pieces.append(dot(chosen, back).astype(BF))
        pieces = jnp.concatenate(pieces, 1)
        weight = jnp.concatenate([w_ref[offset] for offset in picked], 1)
        placed_ref[other : other + length, :] = dot(pieces, weight, ((1,), (1,)))
        kernel_part = dot(face_g_ref[place], back)
        for index, offset in enumerate(picked):
            total[offset] += kernel_part[index * C : (index + 1) * C, :]
    column = corner_column(rc, 4 * TZ)
    back = jnp.concatenate([returned[n] for n in CORNERS], 0)
    kernel_part = dot(corner_g_ref[...], back)
    pieces = []
    weights = []
    spots = [dot(match(column, corner_row(step, sm_ref)), back).astype(BF) for step in range(3)]
    for place, number in enumerate(CORNERS):
        inside = corner_mask(place, 0, (4 * TZ, C))
        for step in range(3):
            offset = toward(*DIRECTIONS[number])[step]
            row = (place * 3 + step) * C
            total[offset] += kernel_part[row : row + C, :]
            pieces.append(jnp.where(inside, spots[step], BF(0)))
            weights.append(w_ref[offset])
    result = dot(jnp.concatenate(pieces, 1), jnp.concatenate(weights, 1), ((1,), (1,)))
    for place, number in enumerate(CORNERS):
        other, length = SPANS[7 - number]
        placed_ref[other : other + length, :] = result[place * TZ : (place + 1) * TZ, :]
    dw_ref[...] = total[...].astype(BF)


def backward_kernel(grad_ref, lm_ref, w_ref, out_ref, *, begin):
    size = out_ref.shape[0]
    source = grad_ref[...].astype(F32).T.astype(BF)
    gathered = []
    for k in range(27):
        if k == 13:
            gathered.append(source[:, begin : begin + size])
        else:
            gathered.append(dot(source, hot(lm_ref[26 - k : 27 - k, begin : begin + size], ROWS)).astype(BF))
    weight = jnp.concatenate([w_ref[k] for k in range(27)], 1)
    out_ref[...] = dot(weight, jnp.concatenate(gathered, 0)).T


def final_kernel(*refs):
    placed_ref, rr_ref, act_ref, pair_ref, mixed_ref, out_ref = refs[-6:]
    placed = placed_ref[...]
    high = placed.astype(BF)
    low = (placed - high.astype(F32)).astype(BF)
    both = dot(hot(rr_ref[...], ROWS), jnp.concatenate([high, low], 1))
    both = both[:, :C] + both[:, C:]
    size = ROWS // len(refs[:-6])
    for index, ref in enumerate(refs[:-6]):
        rows = slice(index * size, (index + 1) * size)
        out_ref[rows, :] = (ref[...] + both[rows]).astype(BF)
    mixed_ref[...] = (act_ref[...].astype(F32) + pair_ref[...].astype(F32)).astype(BF)


def assemble_kernel(bits_ref, own_ref, one_ref, two_ref, four_ref, out_ref):
    place = bits_ref[0] * 4 + bits_ref[1] * 2 + bits_ref[2]
    blocks = [own_ref[...], one_ref[...]] + [two_ref[i] for i in range(2)] + [four_ref[i] for i in range(4)]
    for distance, block in enumerate(blocks):
        out_ref[place ^ distance] = block.astype(F32)


PARAMS = pltpu.CompilerParams(vmem_limit_bytes=48 * 2**20)


def shape(dims, dtype):
    return jax.ShapeDtypeStruct(dims, dtype)


def whole(dims):
    return pl.BlockSpec(dims, lambda *ids: (0,) * len(dims))


def pairing(axis, which):
    pairs = []
    for tile in range(lax.axis_size("space")):
        at_x, at_y = tile % TILES_X, tile // TILES_X
        tiles_y = lax.axis_size("space") // TILES_X
        if axis == "x":
            move = 1 if (at_x + which) % 2 == 0 else -1
            at_x = (at_x + move) % TILES_X
        else:
            move = 1 if (at_y + which) % 2 == 0 else -1
            at_y = (at_y + move) % tiles_y
        pairs.append((tile, at_y * TILES_X + at_x))
    return pairs


def exchange_x(xa, xb):
    return [lax.ppermute(v, "space", pairing("x", n)) for n, v in enumerate((xa, xb))]


def exchange_y(ya, yb, xa, xb, sides):
    sent = []
    for which, own in enumerate((ya, yb)):
        down = sides[1] != which
        corners = [jnp.where(down, v[CAP : CAP + TZ], v[CAP + TZ :]) for v in (xa, xb)]
        sent.append(jnp.concatenate([own] + corners, 0))
    return [lax.ppermute(v, "space", pairing("y", n)) for n, v in enumerate(sent)]


def swapped(array):
    return lax.ppermute(array, "segment", [(i, i ^ 1) for i in range(lax.axis_size("segment"))])


def xor_send(value, bits):
    return lax.ppermute(value, "space", [(i, i ^ bits) for i in range(lax.axis_size("space"))])


def add_up(pieces):
    total = pieces[0].astype(F32)
    for piece in pieces[1:]:
        total = total + piece.astype(F32)
    return total.astype(BF)


def pick(array, index):
    return lax.dynamic_index_in_dim(array, index, 0, False)


def cost(flops, data):
    return pl.CostEstimate(flops=int(flops), bytes_accessed=int(data), transcendentals=0)


def tie(value, other):
    return lax.optimization_barrier((value, other))[0]


def on_device(features, weights, cotangent, local_map, send_map, recv_map):
    x = features[0]
    w = weights[0]
    cot = cotangent[0]
    lm = local_map.T
    sm = send_map.T
    rr = recv_map.reshape(1, HALO)
    me = lax.axis_index("space")
    sides = jnp.stack([me % 2, me // TILES_X % 2]).astype(jnp.int32)
    smem = pl.BlockSpec(memory_space=pltpu.SMEM)
    vmem = pl.BlockSpec(memory_space=pltpu.VMEM)
    out_lists = [shape((CAP + 2 * TZ, C), BF)] * 2 + [shape((CAP, C), BF)] * 2
    xa, xb, ya, yb, face_g, corner_g = pl.pallas_call(
        start_kernel,
        in_specs=[smem] + [vmem] * 4,
        out_shape=out_lists + [shape((4, 9 * C, CAP), BF), shape((12 * C, 4 * TZ), BF)],
        compiler_params=PARAMS,
        cost_estimate=cost(2e9, 4e6),
        name="start",
    )(sides, x, rr, sm, w)
    cot_pair = swapped(cot)
    in_x = exchange_x(xa, xb)
    in_y = exchange_y(ya, yb, *in_x, sides)
    gathered, pre = pl.pallas_call(
        functools.partial(forward_kernel, width=512),
        grid=(2,),
        in_specs=[whole((ROWS, C)), whole((27, ROWS)), whole((27, C, C))],
        out_specs=[pl.BlockSpec((13 * C, ROWS), lambda j: (j, 0)), whole((ROWS, C))],
        out_shape=[shape((26 * C, ROWS), BF), shape((ROWS, C), F32)],
        scratch_shapes=[pltpu.VMEM((C, ROWS), BF), pltpu.VMEM((C, ROWS), F32)],
        compiler_params=PARAMS,
        cost_estimate=cost(15e9, 9e6),
        name="forward",
    )(x, lm, w)
    act, grad, xa, xb, ya, yb = pl.pallas_call(
        activate_kernel,
        in_specs=[smem] + [vmem] * 8,
        out_shape=[shape((ROWS, C), BF)] * 2 + out_lists,
        compiler_params=PARAMS,
        cost_estimate=cost(1.5e9, 3e6),
        name="activate",
    )(sides, pre, *in_x, *in_y, rr, cot, cot_pair)
    in_x = exchange_x(xa, xb)
    in_y = exchange_y(ya, yb, *in_x, sides)
    dw_local = pl.pallas_call(
        weight_kernel,
        grid=(2,),
        in_specs=[pl.BlockSpec((13 * C, ROWS), lambda j: (j, 0)), whole((ROWS, C)), whole((ROWS, C))],
        out_specs=whole((27, C, C)),
        out_shape=shape((27, C, C), F32),
        compiler_params=PARAMS,
        cost_estimate=cost(4e9, 9e6),
        name="weight",
    )(gathered, grad, x)

    parts = 4
    size = ROWS // parts

    def backward(index, grad):
        return pl.pallas_call(
            functools.partial(backward_kernel, begin=index * size),
            out_shape=shape((size, C), F32),
            compiler_params=PARAMS,
            cost_estimate=cost(3e9, 2e6),
            name="backward",
        )(grad, lm, w)

    act_pair = swapped(act)
    act_pair, dw_local = lax.optimization_barrier((act_pair, dw_local))
    dw, placed = pl.pallas_call(
        return_kernel,
        in_specs=[smem] + [vmem] * 10,
        out_shape=[shape((27, C, C), BF), shape((HALO, C), F32)],
        scratch_shapes=[pltpu.VMEM((27, C, C), F32)],
        compiler_params=PARAMS,
        cost_estimate=cost(3e9, 4e6),
        name="returning",
    )(sides, *in_x, *in_y, rr, sm, w, face_g, corner_g, dw_local)

    bits = [me % 2, me // 2 % 2, me // 4 % 2]
    blocks = dw.reshape(2, 2, 2, -1, C)
    locals_ = []
    for stage, place in enumerate((1, 2, 4)):
        kept, sent = pick(blocks, bits[stage]), pick(blocks, 1 - bits[stage])
        got = xor_send(sent, place)
        locals_.append(backward(stage, tie(grad, sent)))
        blocks = add_up([kept, tie(got, locals_[-1])])
    got = xor_send(blocks, 8)
    locals_.append(backward(3, tie(grad, blocks)))
    blocks = add_up([blocks, tie(got, locals_[-1])])
    got = xor_send(blocks, 16)
    mixed, input_grad = pl.pallas_call(
        final_kernel,
        out_shape=[shape((ROWS, C), BF), shape((ROWS, C), BF)],
        compiler_params=PARAMS,
        cost_estimate=cost(1e9, 3e6),
        name="final",
    )(*locals_, tie(placed, blocks), rr, act, act_pair)
    own = add_up([blocks, tie(got, input_grad)])
    one = xor_send(own, 4)
    two = xor_send(jnp.stack([own, one]), 2)
    four = xor_send(jnp.concatenate([jnp.stack([own, one]), two], 0), 1)
    weight_grad = pl.pallas_call(
        assemble_kernel,
        in_specs=[smem] + [vmem] * 4,
        out_shape=shape((8,) + own.shape, F32),
        compiler_params=PARAMS,
        cost_estimate=cost(1e6, 3e6),
        name="assemble",
    )(jnp.stack(bits).astype(jnp.int32), own, one, two, four)
    weight_grad = weight_grad.reshape(dw.shape)
    return (mixed[None], input_grad[None], weight_grad[None])


def solution(mesh):
    in_specs = (
        P("segment", "space", None),
        P("segment", None, None, None),
        P("segment", "space", None),
        P("space", None),
        P("space", None),
        P("space"),
    )
    out_specs = (
        P("segment", "space", None),
        P("segment", "space", None),
        P("segment", None, None, None),
    )
    return jax.shard_map(
        on_device, mesh=mesh, in_specs=in_specs, out_specs=out_specs, check_vma=False
    )
```

```python
import functools

import jax
import jax.numpy as jnp
from jax import lax
from jax.experimental import pallas as pl
from jax.experimental.pallas import tpu as pltpu
from jax.sharding import PartitionSpec as P

TZ = 32
TILES_X = 4
CAP = 256
ROWS = 1024
C = 128
HALO = 1152

DIRECTIONS = ((-1, -1), (-1, 0), (-1, 1), (0, -1), (0, 1), (1, -1), (1, 0), (1, 1))
BF = jnp.bfloat16
F32 = jnp.float32


def spans():
    result = []
    start = 0
    for step_x, step_y in DIRECTIONS:
        length = TZ if step_x != 0 and step_y != 0 else CAP
        result.append((start, length))
        start = start + length
    return result


SPANS = spans()
FACES = [n for n, (a, b) in enumerate(DIRECTIONS) if a == 0 or b == 0]
CORNERS = [n for n, (a, b) in enumerate(DIRECTIONS) if a != 0 and b != 0]


def toward(step_x, step_y):
    picked = []
    for offset in range(27):
        along_x = offset // 9 - 1
        along_y = offset // 3 % 3 - 1
        if (step_x == 0 or along_x == -step_x) and (step_y == 0 or along_y == -step_y):
            picked.append(offset)
    return picked


def dot(a, b, dims=((1,), (0,))):
    return lax.dot_general(a, b, (dims, ((), ())), preferred_element_type=F32)


def hot(row, rows):
    pos = lax.broadcasted_iota(jnp.int32, (256, 128), 0).astype(jnp.int16)
    count = row.shape[1]
    blocks = []
    for base in range(0, rows, 256):
        rel = (row - base).astype(jnp.int16)
        parts = [
            jnp.where(rel[:, t : t + 128] == pos, BF(1), BF(0)) for t in range(0, count, 128)
        ]
        blocks.append(jnp.concatenate(parts, 1))
    return jnp.concatenate(blocks, 0)


def spread(column, count):
    kept = jnp.where(column == ROWS, -1, column)
    return jnp.broadcast_to(kept, (column.shape[0], count)).astype(jnp.int16)


def places_from_one(rows):
    return (lax.broadcasted_iota(jnp.int32, (rows, 128), 0) + 1).astype(BF)


def positions(column, row):
    rows, count = column.shape
    numbers = places_from_one(rows)
    numbers = jnp.concatenate([numbers] * (count // 128), 1)
    found = jnp.where(column == row.astype(jnp.int16), numbers, BF(0))
    while rows > 16:
        rows //= 2
        found = jnp.maximum(found[:rows], found[rows:])
    return jnp.max(found.astype(F32), axis=0, keepdims=True)


def match(row, rows):
    numbers = places_from_one(rows)
    row = row.astype(BF)
    parts = [jnp.where(row[:, t : t + 128] == numbers, BF(1), BF(0)) for t in range(0, row.shape[1], 128)]
    return jnp.concatenate(parts, 1)


def face_rows(block):
    block = block.astype(F32)
    return [jnp.concatenate([block[k : k + 1], block[16 + k : 17 + k]], 1) for k in range(9)]


def column_of(row):
    return jnp.broadcast_to(row.astype(F32), (8, row.shape[1])).T[:, :1].astype(jnp.int32)


def inside(place, axis, dims):
    return (lax.broadcasted_iota(jnp.int32, dims, axis) // TZ) == place


def number_of(step_x, step_y):
    return DIRECTIONS.index((step_x, step_y))


def pack_sides(lists, orient, sides, xa_ref, xb_ref, ya_ref, yb_ref):
    x_odd, y_odd = sides[0] == 1, sides[1] == 1

    def x_side(side):
        picked = [(orient * side, 0), (orient * side, -orient), (orient * side, orient)]
        return jnp.concatenate([lists[number_of(*d)] for d in picked], 0)

    plus, minus = x_side(1), x_side(-1)
    xa_ref[...] = jnp.where(x_odd, minus, plus)
    xb_ref[...] = jnp.where(x_odd, plus, minus)
    plus, minus = lists[number_of(0, orient)], lists[number_of(0, -orient)]
    ya_ref[...] = jnp.where(y_odd, minus, plus)
    yb_ref[...] = jnp.where(y_odd, plus, minus)


def unpack_sides(orient, sides, face, edge, xa, xb, ya, yb):
    x_odd, y_odd = sides[0] == 1, sides[1] == 1

    def of_side(side, odd, a, b):
        return jnp.where(odd, b, a) if side == 1 else jnp.where(odd, a, b)

    lists = []
    for step_x, step_y in DIRECTIONS:
        if step_y == 0:
            lists.append(of_side(-orient * step_x, x_odd, xa[:face], xb[:face]))
        elif step_x == 0:
            lists.append(of_side(-orient * step_y, y_odd, ya[:face], yb[:face]))
        else:
            first = of_side(-orient * step_y, y_odd, ya[face : face + edge], yb[face : face + edge])
            second = of_side(-orient * step_y, y_odd, ya[face + edge :], yb[face + edge :])
            lists.append(of_side(-orient * step_x, x_odd, first, second))
    return lists


def start_kernel(side_ref, x_ref, rr_ref, sm_ref, xa_ref, xb_ref, ya_ref, yb_ref, face_p_ref, edge_p_ref):
    lists = [None] * 8
    row = rr_ref[...]
    column = column_of(row)
    listed = dot(x_ref[...].astype(F32).T.astype(BF), hot(row, ROWS)).T.astype(BF)
    for place, number in enumerate(FACES):
        start, length = SPANS[number]
        other, _ = SPANS[7 - number]
        wide = spread(column[other : other + length], length)
        found = [
            positions(wide, sm_ref[offset : offset + 1, start : start + length])
            for offset in toward(*DIRECTIONS[number])
        ]
        found = jnp.concatenate(found + [jnp.zeros((7, length), F32)], 0)
        found = jnp.concatenate([found[:, :128], found[:, 128:]], 0).astype(BF)
        face_p_ref[place] = found
        lists[number] = jnp.concatenate([listed[other : other + length], found], 0)
    wide = spread(
        jnp.concatenate([column[SPANS[7 - n][0] : SPANS[7 - n][0] + TZ] for n in CORNERS], 0), 4 * TZ
    )
    found = []
    for step in range(3):
        pieces = []
        for number in CORNERS:
            start, length = SPANS[number]
            offset = toward(*DIRECTIONS[number])[step]
            pieces.append(sm_ref[offset : offset + 1, start : start + length])
        found.append(positions(wide, jnp.concatenate(pieces, 1)))
    found = jnp.concatenate(found + [jnp.zeros((13, 4 * TZ), F32)], 0).astype(BF)
    edge_p_ref[...] = found
    for number in CORNERS:
        other, length = SPANS[7 - number]
        lists[number] = jnp.concatenate([listed[other : other + length], found], 0)
    pack_sides(lists, 1, (side_ref[0], side_ref[1]), xa_ref, xb_ref, ya_ref, yb_ref)


def forward_kernel(x_ref, lm_ref, w_ref, g_ref, pre_ref, x_t, total, *, width):
    step = pl.program_id(0)

    @pl.when(step == 0)
    def _():
        x_t[...] = x_ref[...].astype(F32).T.astype(BF)
        total[...] = dot(w_ref[13], x_t[...], ((0,), (0,)))

    source = x_t[...]
    weight = jnp.concatenate([w_ref[14 * step + i] for i in range(13)], 0)
    for begin in range(0, ROWS, width):
        cols = slice(begin, begin + width)
        gathered = [
            dot(source, hot(lm_ref[pl.ds(14 * step + i, 1), cols], ROWS)).astype(BF) for i in range(13)
        ]
        gathered = jnp.concatenate(gathered, 0)
        g_ref[:, cols] = gathered
        total[:, cols] += dot(weight, gathered, ((0,), (0,)))

    @pl.when(step == 1)
    def _():
        pre_ref[...] = total[...].T


def high_low(values):
    high = values.astype(BF)
    return jnp.concatenate([high, (values - high.astype(F32)).astype(BF)], 1)


def activate_kernel(
    side_ref, pre_ref, ixa_ref, ixb_ref, iya_ref, iyb_ref, rr_ref, cot_ref, pair_ref, w_ref,
    act_ref, grad_ref, xa_ref, xb_ref, ya_ref, yb_ref, dw_ref,
):
    sides = (side_ref[0], side_ref[1])
    arrived = unpack_sides(
        1, sides, CAP + 32, TZ + 16, ixa_ref[...], ixb_ref[...], iya_ref[...], iyb_ref[...]
    )
    sums = [None] * 8
    sources = []
    for number in FACES:
        picked = toward(*DIRECTIONS[number])
        source = arrived[number][:CAP].astype(F32).T.astype(BF)
        sources.append(source)
        gathered = [dot(source, match(row, CAP)).astype(BF) for row in face_rows(arrived[number][CAP:])]
        weight = jnp.concatenate([w_ref[offset] for offset in picked], 0)
        sums[number] = dot(weight, jnp.concatenate(gathered, 0), ((0,), (0,))).T
    edge_source = jnp.concatenate([arrived[n][:TZ] for n in CORNERS], 0).astype(F32).T.astype(BF)
    edge_found = jnp.zeros((16, 4 * TZ), F32)
    for place, number in enumerate(CORNERS):
        rows = arrived[number][TZ:].astype(F32)
        edge_found = jnp.where(inside(place, 1, rows.shape), rows, edge_found)
    gathered = [dot(edge_source, match(edge_found[k : k + 1], 4 * TZ)).astype(BF) for k in range(3)]
    masked = []
    weights = []
    for place, number in enumerate(CORNERS):
        for step in range(3):
            masked.append(jnp.where(inside(place, 1, (C, 4 * TZ)), gathered[step], BF(0)))
            weights.append(w_ref[toward(*DIRECTIONS[number])[step]])
    total = dot(jnp.concatenate(weights, 0), jnp.concatenate(masked, 0), ((0,), (0,))).T
    for place, number in enumerate(CORNERS):
        sums[number] = total[place * TZ : (place + 1) * TZ]

    selector = hot(rr_ref[...], ROWS)
    both = dot(selector, high_low(jnp.concatenate(sums, 0)))
    pre = pre_ref[...] + both[:, :C] + both[:, C:]
    gate = 1.0 / (1.0 + jnp.exp(-pre))
    act_ref[...] = (pre * gate).astype(BF)
    upstream = cot_ref[...].astype(F32) + pair_ref[...].astype(F32)
    grad = upstream * gate * (1.0 + pre * (1.0 - gate))
    grad_ref[...] = grad.astype(BF)
    listed = dot(grad.T.astype(BF), selector).T.astype(BF)
    lists = [listed[start : start + length] for start, length in SPANS]
    pack_sides(lists, -1, sides, xa_ref, xb_ref, ya_ref, yb_ref)

    dw_ref[...] = jnp.zeros_like(dw_ref)
    for source, number in zip(sources, FACES):
        pieces = [
            dot(match(row, CAP), lists[number]).astype(BF) for row in face_rows(arrived[number][CAP:])
        ]
        part = dot(source, jnp.concatenate(pieces, 1))
        for index, offset in enumerate(toward(*DIRECTIONS[number])):
            dw_ref[offset] += part[:, index * C : (index + 1) * C]
    back = jnp.concatenate([lists[n] for n in CORNERS], 0)
    spots = [dot(match(edge_found[k : k + 1], 4 * TZ), back).astype(BF) for k in range(3)]
    pieces = [
        jnp.where(inside(place, 0, (4 * TZ, C)), spots[step], BF(0)) for place in range(4) for step in range(3)
    ]
    part = dot(edge_source, jnp.concatenate(pieces, 1))
    for place, number in enumerate(CORNERS):
        for step in range(3):
            index = 3 * place + step
            dw_ref[toward(*DIRECTIONS[number])[step]] += part[:, index * C : (index + 1) * C]


def weight_kernel(g_ref, grad_ref, x_ref, halo_ref, dw_ref):
    step = pl.program_id(0)

    @pl.when(step == 0)
    def _():
        dw_ref[13] = halo_ref[13] + dot(x_ref[...], grad_ref[...], ((0,), (0,)))

    total = dot(g_ref[...], grad_ref[...])
    dw_ref[pl.ds(14 * step, 13)] = halo_ref[pl.ds(14 * step, 13)] + total.reshape(13, C, C)


def return_kernel(side_ref, ixa_ref, ixb_ref, iya_ref, iyb_ref, face_p_ref, edge_p_ref, w_ref, placed_ref):
    sides = (side_ref[0], side_ref[1])
    returned = unpack_sides(-1, sides, CAP, TZ, ixa_ref[...], ixb_ref[...], iya_ref[...], iyb_ref[...])
    for place, number in enumerate(FACES):
        other, length = SPANS[7 - number]
        pieces = [dot(match(row, CAP), returned[number]).astype(BF) for row in face_rows(face_p_ref[place])]
        weight = jnp.concatenate([w_ref[offset] for offset in toward(*DIRECTIONS[number])], 1)
        placed_ref[other : other + length, :] = dot(jnp.concatenate(pieces, 1), weight, ((1,), (1,)))
    back = jnp.concatenate([returned[n] for n in CORNERS], 0)
    found = edge_p_ref[...].astype(F32)
    spots = [dot(match(found[k : k + 1], 4 * TZ), back).astype(BF) for k in range(3)]
    pieces = []
    weights = []
    for place, number in enumerate(CORNERS):
        for step in range(3):
            pieces.append(jnp.where(inside(place, 0, (4 * TZ, C)), spots[step], BF(0)))
            weights.append(w_ref[toward(*DIRECTIONS[number])[step]])
    result = dot(jnp.concatenate(pieces, 1), jnp.concatenate(weights, 1), ((1,), (1,)))
    for place, number in enumerate(CORNERS):
        other, length = SPANS[7 - number]
        placed_ref[other : other + length, :] = result[place * TZ : (place + 1) * TZ, :]


def backward_kernel(grad_ref, lm_ref, w_ref, out_ref, *, begin):
    size = out_ref.shape[0]
    source = grad_ref[...].astype(F32).T.astype(BF)
    gathered = []
    for k in range(27):
        if k == 13:
            gathered.append(source[:, begin : begin + size])
        else:
            gathered.append(dot(source, hot(lm_ref[26 - k : 27 - k, begin : begin + size], ROWS)).astype(BF))
    weight = jnp.concatenate([w_ref[k] for k in range(27)], 1)
    out_ref[...] = dot(weight, jnp.concatenate(gathered, 0)).T


def final_kernel(*refs):
    placed_ref, rr_ref, act_ref, pair_ref, mixed_ref, out_ref = refs[-6:]
    both = dot(hot(rr_ref[...], ROWS), high_low(placed_ref[...]))
    both = both[:, :C] + both[:, C:]
    size = ROWS // len(refs[:-6])
    for index, ref in enumerate(refs[:-6]):
        rows = slice(index * size, (index + 1) * size)
        out_ref[rows, :] = (ref[...] + both[rows]).astype(BF)
    mixed_ref[...] = (act_ref[...].astype(F32) + pair_ref[...].astype(F32)).astype(BF)


def assemble_kernel(bits_ref, own_ref, one_ref, two_ref, four_ref, out_ref):
    place = bits_ref[0] * 4 + bits_ref[1] * 2 + bits_ref[2]
    blocks = [own_ref[...], one_ref[...]] + [two_ref[i] for i in range(2)] + [four_ref[i] for i in range(4)]
    for distance, block in enumerate(blocks):
        out_ref[place ^ distance] = block.astype(F32)


PARAMS = pltpu.CompilerParams(vmem_limit_bytes=48 * 2**20)


def shape(dims, dtype):
    return jax.ShapeDtypeStruct(dims, dtype)


def whole(dims):
    return pl.BlockSpec(dims, lambda *ids: (0,) * len(dims))


def pairing(axis, which):
    pairs = []
    for tile in range(lax.axis_size("space")):
        at_x, at_y = tile % TILES_X, tile // TILES_X
        tiles_y = lax.axis_size("space") // TILES_X
        if axis == "x":
            move = 1 if (at_x + which) % 2 == 0 else -1
            at_x = (at_x + move) % TILES_X
        else:
            move = 1 if (at_y + which) % 2 == 0 else -1
            at_y = (at_y + move) % tiles_y
        pairs.append((tile, at_y * TILES_X + at_x))
    return pairs


def exchange_x(xa, xb):
    return [lax.ppermute(v, "space", pairing("x", n)) for n, v in enumerate((xa, xb))]


def exchange_y(ya, yb, xa, xb, sides, face, edge):
    sent = []
    for which, own in enumerate((ya, yb)):
        down = sides[1] != which
        corners = [jnp.where(down, v[face : face + edge], v[face + edge :]) for v in (xa, xb)]
        sent.append(jnp.concatenate([own] + corners, 0))
    return [lax.ppermute(v, "space", pairing("y", n)) for n, v in enumerate(sent)]


def swapped(array):
    return lax.ppermute(array, "segment", [(i, i ^ 1) for i in range(lax.axis_size("segment"))])


def xor_send(value, bits):
    return lax.ppermute(value, "space", [(i, i ^ bits) for i in range(lax.axis_size("space"))])


def pick(array, index):
    return lax.dynamic_index_in_dim(array, index, 0, False)


def cost(flops, data):
    return pl.CostEstimate(flops=int(flops), bytes_accessed=int(data), transcendentals=0)


def tie(value, other):
    return lax.optimization_barrier((value, other))[0]


def on_device(features, weights, cotangent, local_map, send_map, recv_map):
    x = features[0]
    w = weights[0]
    cot = cotangent[0]
    lm = local_map.T
    sm = send_map.T
    rr = recv_map.reshape(1, HALO)
    me = lax.axis_index("space")
    sides = jnp.stack([me % 2, me // TILES_X % 2]).astype(jnp.int32)
    smem = pl.BlockSpec(memory_space=pltpu.SMEM)
    vmem = pl.BlockSpec(memory_space=pltpu.VMEM)
    def lists_shape(face, edge):
        return [shape((face + 2 * edge, C), BF)] * 2 + [shape((face, C), BF)] * 2

    xa, xb, ya, yb, face_p, edge_p = pl.pallas_call(
        start_kernel,
        in_specs=[smem] + [vmem] * 3,
        out_shape=lists_shape(CAP + 32, TZ + 16) + [shape((4, 32, C), BF), shape((16, C), BF)],
        compiler_params=PARAMS,
        cost_estimate=cost(2e9, 4e6),
        name="start",
    )(sides, x, rr, sm)
    cot_pair = swapped(cot)
    in_x = exchange_x(xa, xb)
    in_y = exchange_y(ya, yb, *in_x, sides, CAP + 32, TZ + 16)
    gathered, pre = pl.pallas_call(
        functools.partial(forward_kernel, width=512),
        grid=(2,),
        in_specs=[whole((ROWS, C)), whole((27, ROWS)), whole((27, C, C))],
        out_specs=[pl.BlockSpec((13 * C, ROWS), lambda j: (j, 0)), whole((ROWS, C))],
        out_shape=[shape((26 * C, ROWS), BF), shape((ROWS, C), F32)],
        scratch_shapes=[pltpu.VMEM((C, ROWS), BF), pltpu.VMEM((C, ROWS), F32)],
        compiler_params=PARAMS,
        cost_estimate=cost(15e9, 9e6),
        name="forward",
    )(x, lm, w)
    act, grad, xa, xb, ya, yb, dw_halo = pl.pallas_call(
        activate_kernel,
        in_specs=[smem] + [vmem] * 9,
        out_shape=[shape((ROWS, C), BF)] * 2 + lists_shape(CAP, TZ) + [shape((27, C, C), F32)],
        compiler_params=PARAMS,
        cost_estimate=cost(4e9, 3e6),
        name="activate",
    )(sides, pre, *in_x, *in_y, rr, cot, cot_pair, w)
    dw = pl.pallas_call(
        weight_kernel,
        grid=(2,),
        in_specs=[pl.BlockSpec((13 * C, ROWS), lambda j: (j, 0)), whole((ROWS, C)), whole((ROWS, C)), whole((27, C, C))],
        out_specs=whole((27, C, C)),
        out_shape=shape((27, C, C), F32),
        compiler_params=PARAMS,
        cost_estimate=cost(4e9, 9e6),
        name="weight",
    )(gathered, grad, x, dw_halo)

    size = ROWS // 4

    def backward(index, grad):
        return pl.pallas_call(
            functools.partial(backward_kernel, begin=index * size),
            out_shape=shape((size, C), F32),
            compiler_params=PARAMS,
            cost_estimate=cost(3e9, 2e6),
            name="backward",
        )(grad, lm, w)

    bits = [me % 2, me // 2 % 2, me // 8 % 2]
    blocks = dw.reshape(2, 2, 2, -1, C)

    def halve(blocks, stage):
        sent = pick(blocks, 1 - bits[stage]).astype(BF)
        return pick(blocks, bits[stage]), sent

    kept, sent = halve(blocks, 0)
    got = xor_send(sent, 1)
    in_x = exchange_x(tie(xa, sent), tie(xb, sent))
    locals_ = [backward(0, tie(grad, sent))]
    blocks = kept + tie(got, locals_[0]).astype(F32)

    kept, sent = halve(blocks, 1)
    got = xor_send(sent, 2)
    in_y = exchange_y(tie(ya, sent), tie(yb, sent), *in_x, sides, CAP, TZ)
    locals_.append(backward(1, tie(grad, sent)))
    blocks = kept + tie(got, locals_[1]).astype(F32)

    kept, sent = halve(blocks, 2)
    got = xor_send(sent, 8)
    placed = pl.pallas_call(
        return_kernel,
        in_specs=[smem] + [vmem] * 7,
        out_shape=shape((HALO, C), F32),
        compiler_params=PARAMS,
        cost_estimate=cost(3e9, 4e6),
        name="returning",
    )(sides, *in_x, *in_y, face_p, edge_p, tie(w, sent))
    own = (kept + tie(got, placed).astype(F32)).astype(BF)

    got = xor_send(own, 4)
    locals_.append(backward(2, tie(grad, own)))
    own = (own.astype(F32) + tie(got, locals_[2]).astype(F32)).astype(BF)
    got = xor_send(own, 16)
    act_pair = swapped(tie(act, own))
    locals_.append(backward(3, tie(grad, own)))
    own = (own.astype(F32) + tie(got, locals_[3]).astype(F32)).astype(BF)
    one = xor_send(own, 8)
    mixed, input_grad = pl.pallas_call(
        final_kernel,
        out_shape=[shape((ROWS, C), BF), shape((ROWS, C), BF)],
        compiler_params=PARAMS,
        cost_estimate=cost(1e9, 3e6),
        name="final",
    )(*locals_, tie(placed, own), rr, act, act_pair)
    one = tie(one, input_grad)
    two = xor_send(jnp.stack([own, one]), 2)
    four = xor_send(jnp.concatenate([jnp.stack([own, one]), two], 0), 1)
    weight_grad = pl.pallas_call(
        assemble_kernel,
        in_specs=[smem] + [vmem] * 4,
        out_shape=shape((8,) + own.shape, F32),
        compiler_params=PARAMS,
        cost_estimate=cost(1e6, 3e6),
        name="assemble",
    )(jnp.stack(bits).astype(jnp.int32), own, one, two, four)
    return (mixed[None], input_grad[None], weight_grad.reshape(dw.shape)[None])


def solution(mesh):
    in_specs = (
        P("segment", "space", None),
        P("segment", None, None, None),
        P("segment", "space", None),
        P("space", None),
        P("space", None),
        P("space"),
    )
    out_specs = (
        P("segment", "space", None),
        P("segment", "space", None),
        P("segment", None, None, None),
    )
    return jax.shard_map(
        on_device, mesh=mesh, in_specs=in_specs, out_specs=out_specs, check_vma=False
    )
```

```python
import functools

import jax
import jax.numpy as jnp
from jax import lax
from jax.experimental import pallas as pl
from jax.experimental.pallas import tpu as pltpu
from jax.sharding import PartitionSpec as P

TZ = 32
TILES_X = 4
CAP = 256
ROWS = 1024
C = 128
HALO = 1152

DIRECTIONS = ((-1, -1), (-1, 0), (-1, 1), (0, -1), (0, 1), (1, -1), (1, 0), (1, 1))
BF = jnp.bfloat16
F32 = jnp.float32


def spans():
    result = []
    start = 0
    for step_x, step_y in DIRECTIONS:
        length = TZ if step_x != 0 and step_y != 0 else CAP
        result.append((start, length))
        start = start + length
    return result


SPANS = spans()
FACES = [n for n, (a, b) in enumerate(DIRECTIONS) if a == 0 or b == 0]
CORNERS = [n for n, (a, b) in enumerate(DIRECTIONS) if a != 0 and b != 0]


def toward(step_x, step_y):
    picked = []
    for offset in range(27):
        along_x = offset // 9 - 1
        along_y = offset // 3 % 3 - 1
        if (step_x == 0 or along_x == -step_x) and (step_y == 0 or along_y == -step_y):
            picked.append(offset)
    return picked


def dot(a, b, dims=((1,), (0,))):
    return lax.dot_general(a, b, (dims, ((), ())), preferred_element_type=F32)


def hot(row, rows):
    pos = lax.broadcasted_iota(jnp.int32, (256, 128), 0).astype(jnp.int16)
    count = row.shape[1]
    blocks = []
    for base in range(0, rows, 256):
        rel = (row - base).astype(jnp.int16)
        parts = [
            jnp.where(rel[:, t : t + 128] == pos, BF(1), BF(0)) for t in range(0, count, 128)
        ]
        blocks.append(jnp.concatenate(parts, 1))
    return jnp.concatenate(blocks, 0)


def spread(column, count):
    kept = jnp.where(column == ROWS, -1, column)
    return jnp.broadcast_to(kept, (column.shape[0], count)).astype(jnp.int16)


def places_from_one(rows):
    return (lax.broadcasted_iota(jnp.int32, (rows, 128), 0) + 1).astype(BF)


def positions(column, row):
    rows, count = column.shape
    numbers = places_from_one(rows)
    numbers = jnp.concatenate([numbers] * (count // 128), 1)
    found = jnp.where(column == row.astype(jnp.int16), numbers, BF(0))
    while rows > 16:
        rows //= 2
        found = jnp.maximum(found[:rows], found[rows:])
    return jnp.max(found.astype(F32), axis=0, keepdims=True)


def match(row, rows):
    numbers = places_from_one(rows)
    row = row.astype(BF)
    parts = [jnp.where(row[:, t : t + 128] == numbers, BF(1), BF(0)) for t in range(0, row.shape[1], 128)]
    return jnp.concatenate(parts, 1)


def face_rows(block):
    block = block.astype(F32)
    return [jnp.concatenate([block[k : k + 1], block[16 + k : 17 + k]], 1) for k in range(9)]


def column_of(row):
    return jnp.broadcast_to(row.astype(F32), (8, row.shape[1])).T[:, :1].astype(jnp.int32)


def inside(place, axis, dims):
    return (lax.broadcasted_iota(jnp.int32, dims, axis) // TZ) == place


def number_of(step_x, step_y):
    return DIRECTIONS.index((step_x, step_y))


def pack_sides(lists, orient, sides, xa_ref, xb_ref, ya_ref, yb_ref):
    x_odd, y_odd = sides[0] == 1, sides[1] == 1

    def x_side(side):
        picked = [(orient * side, 0), (orient * side, -orient), (orient * side, orient)]
        return jnp.concatenate([lists[number_of(*d)] for d in picked], 0)

    plus, minus = x_side(1), x_side(-1)
    xa_ref[...] = jnp.where(x_odd, minus, plus)
    xb_ref[...] = jnp.where(x_odd, plus, minus)
    plus, minus = lists[number_of(0, orient)], lists[number_of(0, -orient)]
    ya_ref[...] = jnp.where(y_odd, minus, plus)
    yb_ref[...] = jnp.where(y_odd, plus, minus)


def unpack_sides(orient, sides, face, edge, xa, xb, ya, yb):
    x_odd, y_odd = sides[0] == 1, sides[1] == 1

    def of_side(side, odd, a, b):
        return jnp.where(odd, b, a) if side == 1 else jnp.where(odd, a, b)

    lists = []
    for step_x, step_y in DIRECTIONS:
        if step_y == 0:
            lists.append(of_side(-orient * step_x, x_odd, xa[:face], xb[:face]))
        elif step_x == 0:
            lists.append(of_side(-orient * step_y, y_odd, ya[:face], yb[:face]))
        else:
            first = of_side(-orient * step_y, y_odd, ya[face : face + edge], yb[face : face + edge])
            second = of_side(-orient * step_y, y_odd, ya[face + edge :], yb[face + edge :])
            lists.append(of_side(-orient * step_x, x_odd, first, second))
    return lists


def start_kernel(side_ref, x_ref, rr_ref, sm_ref, xa_ref, xb_ref, ya_ref, yb_ref, face_p_ref, edge_p_ref):
    lists = [None] * 8
    row = rr_ref[...]
    column = column_of(row)
    listed = dot(x_ref[...].astype(F32).T.astype(BF), hot(row, ROWS)).T.astype(BF)
    for place, number in enumerate(FACES):
        start, length = SPANS[number]
        other, _ = SPANS[7 - number]
        wide = spread(column[other : other + length], length)
        found = [
            positions(wide, sm_ref[offset : offset + 1, start : start + length])
            for offset in toward(*DIRECTIONS[number])
        ]
        found = jnp.concatenate(found + [jnp.zeros((7, length), F32)], 0)
        found = jnp.concatenate([found[:, :128], found[:, 128:]], 0).astype(BF)
        face_p_ref[place] = found
        lists[number] = jnp.concatenate([listed[other : other + length], found], 0)
    wide = spread(
        jnp.concatenate([column[SPANS[7 - n][0] : SPANS[7 - n][0] + TZ] for n in CORNERS], 0), 4 * TZ
    )
    found = []
    for step in range(3):
        pieces = []
        for number in CORNERS:
            start, length = SPANS[number]
            offset = toward(*DIRECTIONS[number])[step]
            pieces.append(sm_ref[offset : offset + 1, start : start + length])
        found.append(positions(wide, jnp.concatenate(pieces, 1)))
    found = jnp.concatenate(found + [jnp.zeros((13, 4 * TZ), F32)], 0).astype(BF)
    edge_p_ref[...] = found
    for number in CORNERS:
        other, length = SPANS[7 - number]
        lists[number] = jnp.concatenate([listed[other : other + length], found], 0)
    pack_sides(lists, 1, (side_ref[0], side_ref[1]), xa_ref, xb_ref, ya_ref, yb_ref)


def forward_kernel(x_ref, lm_ref, w_ref, *refs, width, first):
    g_ref, sum_ref = refs[-2:]
    source = x_ref[...].astype(F32).T.astype(BF)
    offsets = range(first, first + 13)
    weight = jnp.concatenate([w_ref[k] for k in offsets], 0)
    for begin in range(0, ROWS, width):
        cols = slice(begin, begin + width)
        gathered = [dot(source, hot(lm_ref[k : k + 1, cols], ROWS)).astype(BF) for k in offsets]
        gathered = jnp.concatenate(gathered, 0)
        g_ref[:, cols] = gathered
        part = dot(weight, gathered, ((0,), (0,)))
        if first == 0:
            sum_ref[:, cols] = part + dot(w_ref[13], source[:, cols], ((0,), (0,)))
        else:
            sum_ref[cols, :] = (part + refs[0][:, cols]).T


def spots_of(rows, count, values):
    chosen = jnp.concatenate([match(row, count) for row in rows], 0)
    spots = dot(chosen, values).astype(BF)
    return jnp.concatenate([spots[k * count : (k + 1) * count] for k in range(len(rows))], 1)


def high_low(values):
    high = values.astype(BF)
    return jnp.concatenate([high, (values - high.astype(F32)).astype(BF)], 1)


def activate_kernel(
    side_ref, pre_ref, ixa_ref, ixb_ref, iya_ref, iyb_ref, rr_ref, cot_ref, pair_ref, w_ref, x_ref, g0_ref, g1_ref,
    act_ref, grad_ref, xa_ref, xb_ref, ya_ref, yb_ref, kept_ref, sent_ref,
    h0_ref, h1_ref, total, sems,
):
    pltpu.make_async_copy(g0_ref, h0_ref, sems.at[0]).start()
    pltpu.make_async_copy(g1_ref, h1_ref, sems.at[1]).start()
    sides = (side_ref[0], side_ref[1])
    arrived = unpack_sides(
        1, sides, CAP + 32, TZ + 16, ixa_ref[...], ixb_ref[...], iya_ref[...], iyb_ref[...]
    )
    sums = [None] * 8
    sources = []
    for number in FACES:
        picked = toward(*DIRECTIONS[number])
        source = arrived[number][:CAP].astype(F32).T.astype(BF)
        sources.append(source)
        chosen = jnp.concatenate([match(row, CAP) for row in face_rows(arrived[number][CAP:])], 1)
        gathered = dot(source, chosen).astype(BF)
        gathered = [gathered[:, k * CAP : (k + 1) * CAP] for k in range(9)]
        weight = jnp.concatenate([w_ref[offset] for offset in picked], 0)
        sums[number] = dot(weight, jnp.concatenate(gathered, 0), ((0,), (0,))).T
    edge_source = jnp.concatenate([arrived[n][:TZ] for n in CORNERS], 0).astype(F32).T.astype(BF)
    edge_found = jnp.zeros((16, 4 * TZ), F32)
    for place, number in enumerate(CORNERS):
        rows = arrived[number][TZ:].astype(F32)
        edge_found = jnp.where(inside(place, 1, rows.shape), rows, edge_found)
    gathered = [dot(edge_source, match(edge_found[k : k + 1], 4 * TZ)).astype(BF) for k in range(3)]
    masked = []
    weights = []
    for place, number in enumerate(CORNERS):
        for step in range(3):
            masked.append(jnp.where(inside(place, 1, (C, 4 * TZ)), gathered[step], BF(0)))
            weights.append(w_ref[toward(*DIRECTIONS[number])[step]])
    edge_sums = dot(jnp.concatenate(weights, 0), jnp.concatenate(masked, 0), ((0,), (0,))).T
    for place, number in enumerate(CORNERS):
        sums[number] = edge_sums[place * TZ : (place + 1) * TZ]

    selector = hot(rr_ref[...], ROWS)
    both = dot(selector, high_low(jnp.concatenate(sums, 0)))
    pre = pre_ref[...] + both[:, :C] + both[:, C:]
    gate = 1.0 / (1.0 + jnp.exp(-pre))
    act_ref[...] = (pre * gate).astype(BF)
    upstream = cot_ref[...].astype(F32) + pair_ref[...].astype(F32)
    grad = upstream * gate * (1.0 + pre * (1.0 - gate))
    grad_ref[...] = grad.astype(BF)
    listed = dot(grad.T.astype(BF), selector).T.astype(BF)
    lists = [listed[start : start + length] for start, length in SPANS]
    pack_sides(lists, -1, sides, xa_ref, xb_ref, ya_ref, yb_ref)

    for begin, buffer, held, semaphore in zip((0, 14), (g0_ref, g1_ref), (h0_ref, h1_ref), (0, 1)):
        pltpu.make_async_copy(buffer, held, sems.at[semaphore]).wait()
        total[begin * C : (begin + 13) * C, :] = dot(held[...], grad.astype(BF))
    total[13 * C : 14 * C, :] = dot(x_ref[...], grad.astype(BF), ((0,), (0,)))

    for source, number in zip(sources, FACES):
        part = dot(source, spots_of(face_rows(arrived[number][CAP:]), CAP, lists[number]))
        for index, offset in enumerate(toward(*DIRECTIONS[number])):
            total[offset * C : (offset + 1) * C, :] += part[:, index * C : (index + 1) * C]
    back = jnp.concatenate([lists[n] for n in CORNERS], 0)
    spots = spots_of([edge_found[k : k + 1] for k in range(3)], 4 * TZ, back)
    pieces = [
        jnp.where(inside(place, 0, (4 * TZ, C)), spots[:, k * C : (k + 1) * C], BF(0))
        for place in range(4) for k in range(3)
    ]
    part = dot(edge_source, jnp.concatenate(pieces, 1))
    for place, number in enumerate(CORNERS):
        for step in range(3):
            index, offset = 3 * place + step, toward(*DIRECTIONS[number])[step]
            total[offset * C : (offset + 1) * C, :] += part[:, index * C : (index + 1) * C]
    half = kept_ref.shape[0]
    kept_ref[...] = total[pl.ds(pl.multiple_of(side_ref[2] * half, 8), half), :]
    sent_ref[...] = total[pl.ds(pl.multiple_of((1 - side_ref[2]) * half, 8), half), :].astype(BF)


def return_kernel(side_ref, ixa_ref, ixb_ref, iya_ref, iyb_ref, face_p_ref, edge_p_ref, w_ref, placed_ref):
    sides = (side_ref[0], side_ref[1])
    returned = unpack_sides(-1, sides, CAP, TZ, ixa_ref[...], ixb_ref[...], iya_ref[...], iyb_ref[...])
    for place, number in enumerate(FACES):
        other, length = SPANS[7 - number]
        pieces = spots_of(face_rows(face_p_ref[place]), CAP, returned[number])
        weight = jnp.concatenate([w_ref[offset] for offset in toward(*DIRECTIONS[number])], 1)
        placed_ref[other : other + length, :] = dot(pieces, weight, ((1,), (1,)))
    back = jnp.concatenate([returned[n] for n in CORNERS], 0)
    found = edge_p_ref[...].astype(F32)
    spots = [dot(match(found[k : k + 1], 4 * TZ), back).astype(BF) for k in range(3)]
    pieces = []
    weights = []
    for place, number in enumerate(CORNERS):
        for step in range(3):
            pieces.append(jnp.where(inside(place, 0, (4 * TZ, C)), spots[step], BF(0)))
            weights.append(w_ref[toward(*DIRECTIONS[number])[step]])
    result = dot(jnp.concatenate(pieces, 1), jnp.concatenate(weights, 1), ((1,), (1,)))
    for place, number in enumerate(CORNERS):
        other, length = SPANS[7 - number]
        placed_ref[other : other + length, :] = result[place * TZ : (place + 1) * TZ, :]


def backward_kernel(grad_ref, lm_ref, w_ref, out_ref, *, begin):
    size = out_ref.shape[0]
    source = grad_ref[...].astype(F32).T.astype(BF)
    gathered = []
    for k in range(27):
        if k == 13:
            gathered.append(source[:, begin : begin + size])
        else:
            gathered.append(dot(source, hot(lm_ref[26 - k : 27 - k, begin : begin + size], ROWS)).astype(BF))
    weight = jnp.concatenate([w_ref[k] for k in range(27)], 1)
    out_ref[...] = dot(weight, jnp.concatenate(gathered, 0)).T


def final_kernel(*refs):
    placed_ref, rr_ref, act_ref, pair_ref, mixed_ref, out_ref = refs[-6:]
    both = dot(hot(rr_ref[...], ROWS), high_low(placed_ref[...]))
    both = both[:, :C] + both[:, C:]
    size = ROWS // len(refs[:-6])
    for index, ref in enumerate(refs[:-6]):
        rows = slice(index * size, (index + 1) * size)
        out_ref[rows, :] = (ref[...] + both[rows]).astype(BF)
    mixed_ref[...] = (act_ref[...].astype(F32) + pair_ref[...].astype(F32)).astype(BF)


def assemble_kernel(bits_ref, own_ref, one_ref, two_ref, four_ref, out_ref):
    place = bits_ref[0] * 4 + bits_ref[1] * 2 + bits_ref[2]
    blocks = [own_ref[...], one_ref[...]] + [two_ref[i] for i in range(2)] + [four_ref[i] for i in range(4)]
    for distance, block in enumerate(blocks):
        out_ref[place ^ distance] = block.astype(F32)


PARAMS = pltpu.CompilerParams(vmem_limit_bytes=48 * 2**20)


def shape(dims, dtype):
    return jax.ShapeDtypeStruct(dims, dtype)


def whole(dims):
    return pl.BlockSpec(dims, lambda *ids: (0,) * len(dims))


def pairing(axis, which):
    pairs = []
    for tile in range(lax.axis_size("space")):
        at_x, at_y = tile % TILES_X, tile // TILES_X
        tiles_y = lax.axis_size("space") // TILES_X
        if axis == "x":
            move = 1 if (at_x + which) % 2 == 0 else -1
            at_x = (at_x + move) % TILES_X
        else:
            move = 1 if (at_y + which) % 2 == 0 else -1
            at_y = (at_y + move) % tiles_y
        pairs.append((tile, at_y * TILES_X + at_x))
    return pairs


def exchange_x(xa, xb):
    return [lax.ppermute(v, "space", pairing("x", n)) for n, v in enumerate((xa, xb))]


def exchange_y(ya, yb, xa, xb, sides, face, edge):
    sent = []
    for which, own in enumerate((ya, yb)):
        down = sides[1] != which
        corners = [jnp.where(down, v[face : face + edge], v[face + edge :]) for v in (xa, xb)]
        sent.append(jnp.concatenate([own] + corners, 0))
    return [lax.ppermute(v, "space", pairing("y", n)) for n, v in enumerate(sent)]


def swapped(array):
    return lax.ppermute(array, "segment", [(i, i ^ 1) for i in range(lax.axis_size("segment"))])


def xor_send(value, bits):
    return lax.ppermute(value, "space", [(i, i ^ bits) for i in range(lax.axis_size("space"))])


def pick(array, index):
    return lax.dynamic_index_in_dim(array, index, 0, False)


def cost(flops, data):
    return pl.CostEstimate(flops=int(flops), bytes_accessed=int(data), transcendentals=0)


def tie(value, other):
    return lax.optimization_barrier((value, other))[0]


def on_device(features, weights, cotangent, local_map, send_map, recv_map):
    x = features[0]
    w = weights[0]
    cot = cotangent[0]
    lm = local_map.T
    sm = send_map.T
    rr = recv_map.reshape(1, HALO)
    me = lax.axis_index("space")
    sides = jnp.stack([me % 2, me // TILES_X % 2, me % 2]).astype(jnp.int32)
    smem = pl.BlockSpec(memory_space=pltpu.SMEM)
    vmem = pl.BlockSpec(memory_space=pltpu.VMEM)
    def lists_shape(face, edge):
        return [shape((face + 2 * edge, C), BF)] * 2 + [shape((face, C), BF)] * 2

    xa, xb, ya, yb, face_p, edge_p = pl.pallas_call(
        start_kernel,
        in_specs=[smem] + [vmem] * 3,
        out_shape=lists_shape(CAP + 32, TZ + 16) + [shape((4, 32, C), BF), shape((16, C), BF)],
        compiler_params=PARAMS,
        cost_estimate=cost(2e9, 4e6),
        name="start",
    )(sides, x, rr, sm)
    cot_pair = swapped(cot)
    in_x = exchange_x(xa, xb)

    def forward(first, dims, *before):
        return pl.pallas_call(
            functools.partial(forward_kernel, width=512, first=first),
            out_shape=[shape((13 * C, ROWS), BF), shape(dims, F32)],
            compiler_params=PARAMS,
            cost_estimate=cost(7e9, 5e6),
            name="forward",
        )(x, lm, w, *before)

    g0, pre = forward(0, (C, ROWS))
    in_x = [tie(v, pre) for v in in_x]
    in_y = exchange_y(ya, yb, *in_x, sides, CAP + 32, TZ + 16)
    g1, pre = forward(14, (ROWS, C), pre)
    half = 27 * C // 2
    act, grad, xa, xb, ya, yb, kept, sent = pl.pallas_call(
        activate_kernel,
        in_specs=[smem] + [vmem] * 10 + [pl.BlockSpec(memory_space=pl.ANY)] * 2,
        out_shape=[shape((ROWS, C), BF)] * 2 + lists_shape(CAP, TZ) + [shape((half, C), F32), shape((half, C), BF)],
        scratch_shapes=[pltpu.VMEM((13 * C, ROWS), BF)] * 2 + [pltpu.VMEM((27 * C, C), F32), pltpu.SemaphoreType.DMA((2,))],
        compiler_params=PARAMS,
        cost_estimate=cost(8e9, 9e6),
        name="activate",
    )(sides, pre, *in_x, *[tie(v, pre) for v in in_y], rr, cot, cot_pair, w, x, g0, g1)

    size = ROWS // 4

    def backward(index, grad):
        return pl.pallas_call(
            functools.partial(backward_kernel, begin=index * size),
            out_shape=shape((size, C), F32),
            compiler_params=PARAMS,
            cost_estimate=cost(3e9, 2e6),
            name="backward",
        )(grad, lm, w)

    bits = [me % 2, me // 2 % 2, me // 8 % 2]

    def halve(blocks, stage):
        return pick(blocks, bits[stage]), pick(blocks, 1 - bits[stage]).astype(BF)

    def plus(one, two):
        return one.astype(F32) + two.astype(F32)

    locals_ = []
    got = xor_send(sent, 1)
    in_x = exchange_x(xa, xb)
    kept, sent = halve(plus(kept, got).reshape(2, 2, -1, C), 1)
    got = xor_send(sent, 2)
    in_y = exchange_y(tie(ya, sent), tie(yb, sent), *in_x, sides, CAP, TZ)
    locals_.append(backward(0, tie(grad, sent)))
    kept, sent = halve(plus(kept, tie(got, locals_[0])), 2)
    got = xor_send(sent, 8)
    locals_.append(backward(1, tie(grad, sent)))
    own = plus(kept, tie(got, locals_[1])).astype(BF)
    got = xor_send(own, 4)
    placed = pl.pallas_call(
        return_kernel,
        in_specs=[smem] + [vmem] * 7,
        out_shape=shape((HALO, C), F32),
        compiler_params=PARAMS,
        cost_estimate=cost(3e9, 4e6),
        name="returning",
    )(sides, *in_x, *in_y, face_p, edge_p, tie(w, own))
    own = plus(own, tie(got, placed)).astype(BF)
    got = xor_send(own, 16)
    act_pair = swapped(tie(act, own))
    locals_.append(backward(2, tie(grad, own)))
    own = plus(own, tie(got, locals_[2])).astype(BF)
    one = xor_send(own, 8)
    locals_.append(backward(3, tie(grad, own)))
    one = tie(one, locals_[3])
    two = xor_send(jnp.stack([own, one]), 2)
    mixed, input_grad = pl.pallas_call(
        final_kernel,
        out_shape=[shape((ROWS, C), BF), shape((ROWS, C), BF)],
        compiler_params=PARAMS,
        cost_estimate=cost(1e9, 3e6),
        name="final",
    )(*locals_, tie(placed, one), rr, act, act_pair)
    two = tie(two, input_grad)
    four = xor_send(jnp.concatenate([jnp.stack([own, one]), two], 0), 1)
    weight_grad = pl.pallas_call(
        assemble_kernel,
        in_specs=[smem] + [vmem] * 4,
        out_shape=shape((8,) + own.shape, F32),
        compiler_params=PARAMS,
        cost_estimate=cost(1e6, 3e6),
        name="assemble",
    )(jnp.stack(bits).astype(jnp.int32), own, one, two, four)
    return (mixed[None], input_grad[None], weight_grad.reshape(w.shape)[None])


def solution(mesh):
    in_specs = (
        P("segment", "space", None),
        P("segment", None, None, None),
        P("segment", "space", None),
        P("space", None),
        P("space", None),
        P("space"),
    )
    out_specs = (
        P("segment", "space", None),
        P("segment", "space", None),
        P("segment", None, None, None),
    )
    return jax.shard_map(
        on_device, mesh=mesh, in_specs=in_specs, out_specs=out_specs, check_vma=False
    )
```

```python
import functools

import jax
import jax.numpy as jnp
from jax import lax
from jax.experimental import pallas as pl
from jax.experimental.pallas import tpu as pltpu
from jax.sharding import PartitionSpec as P

TZ = 32
TILES_X = 4
CAP = 256
ROWS = 1024
C = 128
HALO = 1152

DIRECTIONS = ((-1, -1), (-1, 0), (-1, 1), (0, -1), (0, 1), (1, -1), (1, 0), (1, 1))
BF = jnp.bfloat16
F32 = jnp.float32


def spans():
    result = []
    start = 0
    for step_x, step_y in DIRECTIONS:
        length = TZ if step_x != 0 and step_y != 0 else CAP
        result.append((start, length))
        start = start + length
    return result


SPANS = spans()
FACES = [n for n, (a, b) in enumerate(DIRECTIONS) if a == 0 or b == 0]
CORNERS = [n for n, (a, b) in enumerate(DIRECTIONS) if a != 0 and b != 0]


def toward(step_x, step_y):
    picked = []
    for offset in range(27):
        along_x = offset // 9 - 1
        along_y = offset // 3 % 3 - 1
        if (step_x == 0 or along_x == -step_x) and (step_y == 0 or along_y == -step_y):
            picked.append(offset)
    return picked


def dot(a, b, dims=((1,), (0,))):
    return lax.dot_general(a, b, (dims, ((), ())), preferred_element_type=F32)


def hot(row, rows):
    pos = lax.broadcasted_iota(jnp.int32, (256, 128), 0).astype(jnp.int16)
    count = row.shape[1]
    blocks = []
    for base in range(0, rows, 256):
        rel = (row - base).astype(jnp.int16)
        parts = [
            jnp.where(rel[:, t : t + 128] == pos, BF(1), BF(0)) for t in range(0, count, 128)
        ]
        blocks.append(jnp.concatenate(parts, 1))
    return jnp.concatenate(blocks, 0)


def spread(column, count):
    kept = jnp.where(column == ROWS, -1, column)
    return jnp.broadcast_to(kept, (column.shape[0], count)).astype(jnp.int16)


def places_from_one(rows):
    return (lax.broadcasted_iota(jnp.int32, (rows, 128), 0) + 1).astype(BF)


def positions(column, row):
    rows, count = column.shape
    numbers = places_from_one(rows)
    numbers = jnp.concatenate([numbers] * (count // 128), 1)
    found = jnp.where(column == row.astype(jnp.int16), numbers, BF(0))
    while rows > 16:
        rows //= 2
        found = jnp.maximum(found[:rows], found[rows:])
    return jnp.max(found.astype(F32), axis=0, keepdims=True)


def match(row, rows):
    numbers = places_from_one(rows)
    row = row.astype(BF)
    parts = [jnp.where(row[:, t : t + 128] == numbers, BF(1), BF(0)) for t in range(0, row.shape[1], 128)]
    return jnp.concatenate(parts, 1)


def face_rows(block):
    block = block.astype(F32)
    return [jnp.concatenate([block[k : k + 1], block[16 + k : 17 + k]], 1) for k in range(9)]


def column_of(row):
    return jnp.broadcast_to(row.astype(F32), (8, row.shape[1])).T[:, :1].astype(jnp.int32)


def inside(place, axis, dims):
    return (lax.broadcasted_iota(jnp.int32, dims, axis) // TZ) == place


def number_of(step_x, step_y):
    return DIRECTIONS.index((step_x, step_y))


def pack_sides(lists, orient, sides, xa_ref, xb_ref, ya_ref, yb_ref):
    x_odd, y_odd = sides[0] == 1, sides[1] == 1

    def x_side(side):
        picked = [(orient * side, 0), (orient * side, -orient), (orient * side, orient)]
        return jnp.concatenate([lists[number_of(*d)] for d in picked], 0)

    plus, minus = x_side(1), x_side(-1)
    xa_ref[...] = jnp.where(x_odd, minus, plus)
    xb_ref[...] = jnp.where(x_odd, plus, minus)
    plus, minus = lists[number_of(0, orient)], lists[number_of(0, -orient)]
    ya_ref[...] = jnp.where(y_odd, minus, plus)
    yb_ref[...] = jnp.where(y_odd, plus, minus)


def unpack_sides(orient, sides, face, edge, xa, xb, ya, yb):
    x_odd, y_odd = sides[0] == 1, sides[1] == 1

    def of_side(side, odd, a, b):
        return jnp.where(odd, b, a) if side == 1 else jnp.where(odd, a, b)

    lists = []
    for step_x, step_y in DIRECTIONS:
        if step_y == 0:
            lists.append(of_side(-orient * step_x, x_odd, xa[:face], xb[:face]))
        elif step_x == 0:
            lists.append(of_side(-orient * step_y, y_odd, ya[:face], yb[:face]))
        else:
            first = of_side(-orient * step_y, y_odd, ya[face : face + edge], yb[face : face + edge])
            second = of_side(-orient * step_y, y_odd, ya[face + edge :], yb[face + edge :])
            lists.append(of_side(-orient * step_x, x_odd, first, second))
    return lists


def start_kernel(side_ref, x_ref, rr_ref, sm_ref, xa_ref, xb_ref, ya_ref, yb_ref, face_p_ref, edge_p_ref):
    lists = [None] * 8
    row = rr_ref[...]
    column = column_of(row)
    listed = dot(x_ref[...].astype(F32).T.astype(BF), hot(row, ROWS)).T.astype(BF)
    for place, number in enumerate(FACES):
        start, length = SPANS[number]
        other, _ = SPANS[7 - number]
        wide = spread(column[other : other + length], length)
        found = [
            positions(wide, sm_ref[offset : offset + 1, start : start + length])
            for offset in toward(*DIRECTIONS[number])
        ]
        found = jnp.concatenate(found + [jnp.zeros((7, length), F32)], 0)
        found = jnp.concatenate([found[:, :128], found[:, 128:]], 0).astype(BF)
        face_p_ref[place] = found
        lists[number] = jnp.concatenate([listed[other : other + length], found], 0)
    wide = spread(
        jnp.concatenate([column[SPANS[7 - n][0] : SPANS[7 - n][0] + TZ] for n in CORNERS], 0), 4 * TZ
    )
    found = []
    for step in range(3):
        pieces = []
        for number in CORNERS:
            start, length = SPANS[number]
            offset = toward(*DIRECTIONS[number])[step]
            pieces.append(sm_ref[offset : offset + 1, start : start + length])
        found.append(positions(wide, jnp.concatenate(pieces, 1)))
    found = jnp.concatenate(found + [jnp.zeros((13, 4 * TZ), F32)], 0).astype(BF)
    edge_p_ref[...] = found
    for number in CORNERS:
        other, length = SPANS[7 - number]
        lists[number] = jnp.concatenate([listed[other : other + length], found], 0)
    pack_sides(lists, 1, (side_ref[0], side_ref[1]), xa_ref, xb_ref, ya_ref, yb_ref)


def forward_kernel(x_ref, lm_ref, w_ref, *refs, width, first):
    g_ref, sum_ref, held, sems = refs[-4:]
    copies = []
    source = x_ref[...].astype(F32).T.astype(BF)
    offsets = range(first, first + 13)
    weight = jnp.concatenate([w_ref[k] for k in offsets], 0)
    for begin in range(0, ROWS, width):
        cols = slice(begin, begin + width)
        gathered = [dot(source, hot(lm_ref[k : k + 1, cols], ROWS)).astype(BF) for k in offsets]
        gathered = jnp.concatenate(gathered, 0)
        held[:, cols] = gathered
        copies.append(pltpu.make_async_copy(held.at[:, cols], g_ref.at[:, cols], sems.at[begin // width]))
        copies[-1].start()
        part = dot(weight, gathered, ((0,), (0,)))
        if first == 0:
            sum_ref[:, cols] = part + dot(w_ref[13], source[:, cols], ((0,), (0,)))
        else:
            sum_ref[cols, :] = (part + refs[0][:, cols]).T
    for copy in copies:
        copy.wait()


def spots_of(rows, count, values):
    return jnp.concatenate([dot(match(row, count), values).astype(BF) for row in rows], 1)


def high_low(values):
    high = values.astype(BF)
    return jnp.concatenate([high, (values - high.astype(F32)).astype(BF)], 1)


def activate_kernel(
    side_ref, pre_ref, ixa_ref, ixb_ref, iya_ref, iyb_ref, rr_ref, cot_ref, pair_ref, w_ref, x_ref, g0_ref, g1_ref,
    act_ref, grad_ref, xa_ref, xb_ref, ya_ref, yb_ref, kept_ref, sent_ref,
    h0_ref, h1_ref, total, sems,
):
    pltpu.make_async_copy(g0_ref, h0_ref, sems.at[0]).start()
    pltpu.make_async_copy(g1_ref, h1_ref, sems.at[1]).start()
    sides = (side_ref[0], side_ref[1])
    arrived = unpack_sides(
        1, sides, CAP + 32, TZ + 16, ixa_ref[...], ixb_ref[...], iya_ref[...], iyb_ref[...]
    )
    sums = [None] * 8
    sources = []
    for number in FACES:
        picked = toward(*DIRECTIONS[number])
        source = arrived[number][:CAP].astype(F32).T.astype(BF)
        sources.append(source)
        gathered = [dot(source, match(row, CAP)).astype(BF) for row in face_rows(arrived[number][CAP:])]
        weight = jnp.concatenate([w_ref[offset] for offset in picked], 0)
        sums[number] = dot(weight, jnp.concatenate(gathered, 0), ((0,), (0,))).T
    edge_source = jnp.concatenate([arrived[n][:TZ] for n in CORNERS], 0).astype(F32).T.astype(BF)
    edge_found = jnp.zeros((16, 4 * TZ), F32)
    for place, number in enumerate(CORNERS):
        rows = arrived[number][TZ:].astype(F32)
        edge_found = jnp.where(inside(place, 1, rows.shape), rows, edge_found)
    gathered = [dot(edge_source, match(edge_found[k : k + 1], 4 * TZ)).astype(BF) for k in range(3)]
    masked = []
    weights = []
    for place, number in enumerate(CORNERS):
        for step in range(3):
            masked.append(jnp.where(inside(place, 1, (C, 4 * TZ)), gathered[step], BF(0)))
            weights.append(w_ref[toward(*DIRECTIONS[number])[step]])
    edge_sums = dot(jnp.concatenate(weights, 0), jnp.concatenate(masked, 0), ((0,), (0,))).T
    for place, number in enumerate(CORNERS):
        sums[number] = edge_sums[place * TZ : (place + 1) * TZ]

    selector = hot(rr_ref[...], ROWS)
    both = dot(selector, high_low(jnp.concatenate(sums, 0)))
    pre = pre_ref[...] + both[:, :C] + both[:, C:]
    gate = 1.0 / (1.0 + jnp.exp(-pre))
    act_ref[...] = (pre * gate).astype(BF)
    upstream = cot_ref[...].astype(F32) + pair_ref[...].astype(F32)
    grad = upstream * gate * (1.0 + pre * (1.0 - gate))
    grad_ref[...] = grad.astype(BF)
    listed = dot(grad.T.astype(BF), selector).T.astype(BF)
    lists = [listed[start : start + length] for start, length in SPANS]
    pack_sides(lists, -1, sides, xa_ref, xb_ref, ya_ref, yb_ref)

    for begin, buffer, held, semaphore in zip((0, 14), (g0_ref, g1_ref), (h0_ref, h1_ref), (0, 1)):
        pltpu.make_async_copy(buffer, held, sems.at[semaphore]).wait()
        total[begin * C : (begin + 13) * C, :] = dot(held[...], grad.astype(BF))
    total[13 * C : 14 * C, :] = dot(x_ref[...], grad.astype(BF), ((0,), (0,)))

    for source, number in zip(sources, FACES):
        part = dot(source, spots_of(face_rows(arrived[number][CAP:]), CAP, lists[number]))
        for index, offset in enumerate(toward(*DIRECTIONS[number])):
            total[offset * C : (offset + 1) * C, :] += part[:, index * C : (index + 1) * C]
    back = jnp.concatenate([lists[n] for n in CORNERS], 0)
    spots = spots_of([edge_found[k : k + 1] for k in range(3)], 4 * TZ, back)
    pieces = [
        jnp.where(inside(place, 0, (4 * TZ, C)), spots[:, k * C : (k + 1) * C], BF(0))
        for place in range(4) for k in range(3)
    ]
    part = dot(edge_source, jnp.concatenate(pieces, 1))
    for place, number in enumerate(CORNERS):
        for step in range(3):
            index, offset = 3 * place + step, toward(*DIRECTIONS[number])[step]
            total[offset * C : (offset + 1) * C, :] += part[:, index * C : (index + 1) * C]
    half = kept_ref.shape[0]
    kept_ref[...] = total[pl.ds(pl.multiple_of(side_ref[2] * half, 8), half), :]
    sent_ref[...] = total[pl.ds(pl.multiple_of((1 - side_ref[2]) * half, 8), half), :].astype(BF)


def return_kernel(side_ref, ixa_ref, ixb_ref, iya_ref, iyb_ref, face_p_ref, edge_p_ref, w_ref, placed_ref):
    sides = (side_ref[0], side_ref[1])
    returned = unpack_sides(-1, sides, CAP, TZ, ixa_ref[...], ixb_ref[...], iya_ref[...], iyb_ref[...])
    for place, number in enumerate(FACES):
        other, length = SPANS[7 - number]
        pieces = spots_of(face_rows(face_p_ref[place]), CAP, returned[number])
        weight = jnp.concatenate([w_ref[offset] for offset in toward(*DIRECTIONS[number])], 1)
        placed_ref[other : other + length, :] = dot(pieces, weight, ((1,), (1,)))
    back = jnp.concatenate([returned[n] for n in CORNERS], 0)
    found = edge_p_ref[...].astype(F32)
    spots = [dot(match(found[k : k + 1], 4 * TZ), back).astype(BF) for k in range(3)]
    pieces = []
    weights = []
    for place, number in enumerate(CORNERS):
        for step in range(3):
            pieces.append(jnp.where(inside(place, 0, (4 * TZ, C)), spots[step], BF(0)))
            weights.append(w_ref[toward(*DIRECTIONS[number])[step]])
    result = dot(jnp.concatenate(pieces, 1), jnp.concatenate(weights, 1), ((1,), (1,)))
    for place, number in enumerate(CORNERS):
        other, length = SPANS[7 - number]
        placed_ref[other : other + length, :] = result[place * TZ : (place + 1) * TZ, :]


def backward_kernel(grad_ref, lm_ref, w_ref, out_ref, *, begin):
    size = out_ref.shape[0]
    source = grad_ref[...].astype(F32).T.astype(BF)
    gathered = []
    for k in range(27):
        if k == 13:
            gathered.append(source[:, begin : begin + size])
        else:
            gathered.append(dot(source, hot(lm_ref[26 - k : 27 - k, begin : begin + size], ROWS)).astype(BF))
    weight = jnp.concatenate([w_ref[k] for k in range(27)], 1)
    out_ref[...] = dot(weight, jnp.concatenate(gathered, 0)).T


def final_kernel(*refs):
    placed_ref, rr_ref, act_ref, pair_ref, mixed_ref, out_ref = refs[-6:]
    both = dot(hot(rr_ref[...], ROWS), high_low(placed_ref[...]))
    both = both[:, :C] + both[:, C:]
    size = ROWS // len(refs[:-6])
    for index, ref in enumerate(refs[:-6]):
        rows = slice(index * size, (index + 1) * size)
        out_ref[rows, :] = (ref[...] + both[rows]).astype(BF)
    mixed_ref[...] = (act_ref[...].astype(F32) + pair_ref[...].astype(F32)).astype(BF)


def assemble_kernel(bits_ref, own_ref, one_ref, two_ref, four_ref, out_ref):
    place = bits_ref[0] * 4 + bits_ref[1] * 2 + bits_ref[2]
    blocks = [own_ref[...], one_ref[...]] + [two_ref[i] for i in range(2)] + [four_ref[i] for i in range(4)]
    for distance, block in enumerate(blocks):
        out_ref[place ^ distance] = block.astype(F32)


PARAMS = pltpu.CompilerParams(vmem_limit_bytes=48 * 2**20)


def shape(dims, dtype):
    return jax.ShapeDtypeStruct(dims, dtype)


def whole(dims):
    return pl.BlockSpec(dims, lambda *ids: (0,) * len(dims))


def pairing(axis, which):
    pairs = []
    for tile in range(lax.axis_size("space")):
        at_x, at_y = tile % TILES_X, tile // TILES_X
        tiles_y = lax.axis_size("space") // TILES_X
        if axis == "x":
            move = 1 if (at_x + which) % 2 == 0 else -1
            at_x = (at_x + move) % TILES_X
        else:
            move = 1 if (at_y + which) % 2 == 0 else -1
            at_y = (at_y + move) % tiles_y
        pairs.append((tile, at_y * TILES_X + at_x))
    return pairs


def exchange_x(xa, xb):
    return [lax.ppermute(v, "space", pairing("x", n)) for n, v in enumerate((xa, xb))]


def exchange_y(ya, yb, xa, xb, sides, face, edge):
    sent = []
    for which, own in enumerate((ya, yb)):
        down = sides[1] != which
        corners = [jnp.where(down, v[face : face + edge], v[face + edge :]) for v in (xa, xb)]
        sent.append(jnp.concatenate([own] + corners, 0))
    return [lax.ppermute(v, "space", pairing("y", n)) for n, v in enumerate(sent)]


def swapped(array):
    return lax.ppermute(array, "segment", [(i, i ^ 1) for i in range(lax.axis_size("segment"))])


def xor_send(value, bits):
    return lax.ppermute(value, "space", [(i, i ^ bits) for i in range(lax.axis_size("space"))])


def pick(array, index):
    return lax.dynamic_index_in_dim(array, index, 0, False)


def cost(flops, data):
    return pl.CostEstimate(flops=int(flops), bytes_accessed=int(data), transcendentals=0)


def tie(value, other):
    return lax.optimization_barrier((value, other))[0]


def on_device(features, weights, cotangent, local_map, send_map, recv_map):
    x = features[0]
    w = weights[0]
    cot = cotangent[0]
    lm = local_map.T
    sm = send_map.T
    rr = recv_map.reshape(1, HALO)
    me = lax.axis_index("space")
    sides = jnp.stack([me % 2, me // TILES_X % 2, me % 2]).astype(jnp.int32)
    smem = pl.BlockSpec(memory_space=pltpu.SMEM)
    vmem = pl.BlockSpec(memory_space=pltpu.VMEM)
    def lists_shape(face, edge):
        return [shape((face + 2 * edge, C), BF)] * 2 + [shape((face, C), BF)] * 2

    xa, xb, ya, yb, face_p, edge_p = pl.pallas_call(
        start_kernel,
        in_specs=[smem] + [vmem] * 3,
        out_shape=lists_shape(CAP + 32, TZ + 16) + [shape((4, 32, C), BF), shape((16, C), BF)],
        compiler_params=PARAMS,
        cost_estimate=cost(2e9, 4e6),
        name="start",
    )(sides, x, rr, sm)
    cot_pair = swapped(cot)
    in_x = exchange_x(xa, xb)

    def forward(first, dims, *before):
        return pl.pallas_call(
            functools.partial(forward_kernel, width=512, first=first),
            out_specs=[pl.BlockSpec(memory_space=pltpu.HBM), vmem],
            scratch_shapes=[pltpu.VMEM((13 * C, ROWS), BF), pltpu.SemaphoreType.DMA((2,))],
            out_shape=[shape((13 * C, ROWS), BF), shape(dims, F32)],
            compiler_params=pltpu.CompilerParams(vmem_limit_bytes=58 * 2**20),
            cost_estimate=cost(7e9, 5e6),
            name="forward",
        )(x, lm, w, *before)

    g0, pre = forward(0, (C, ROWS))
    in_x = [tie(v, pre) for v in in_x]
    in_y = exchange_y(ya, yb, *in_x, sides, CAP + 32, TZ + 16)
    g1, pre = forward(14, (ROWS, C), pre)
    half = 27 * C // 2
    act, grad, xa, xb, ya, yb, kept, sent = pl.pallas_call(
        activate_kernel,
        in_specs=[smem] + [vmem] * 10 + [pl.BlockSpec(memory_space=pltpu.HBM)] * 2,
        out_shape=[shape((ROWS, C), BF)] * 2 + lists_shape(CAP, TZ) + [shape((half, C), F32), shape((half, C), BF)],
        scratch_shapes=[pltpu.VMEM((13 * C, ROWS), BF)] * 2 + [pltpu.VMEM((27 * C, C), F32), pltpu.SemaphoreType.DMA((2,))],
        compiler_params=PARAMS,
        cost_estimate=cost(8e9, 9e6),
        name="activate",
    )(sides, pre, *in_x, *[tie(v, pre) for v in in_y], rr, cot, cot_pair, w, x, g0, g1)

    size = ROWS // 4

    def backward(index, grad):
        return pl.pallas_call(
            functools.partial(backward_kernel, begin=index * size),
            out_shape=shape((size, C), F32),
            compiler_params=PARAMS,
            cost_estimate=cost(3e9, 2e6),
            name="backward",
        )(grad, lm, w)

    bits = [me % 2, me // 2 % 2, me // 8 % 2]

    def halve(blocks, stage):
        return pick(blocks, bits[stage]), pick(blocks, 1 - bits[stage]).astype(BF)

    def plus(one, two):
        return one.astype(F32) + two.astype(F32)

    locals_ = []
    got = xor_send(sent, 1)
    in_x = exchange_x(xa, xb)
    kept, sent = halve(plus(kept, got).reshape(2, 2, -1, C), 1)
    got = xor_send(sent, 2)
    in_y = exchange_y(tie(ya, sent), tie(yb, sent), *in_x, sides, CAP, TZ)
    locals_.append(backward(0, tie(grad, sent)))
    kept, sent = halve(plus(kept, tie(got, locals_[0])), 2)
    got = xor_send(sent, 8)
    locals_.append(backward(1, tie(grad, sent)))
    own = plus(kept, tie(got, locals_[1])).astype(BF)
    got = xor_send(own, 4)
    placed = pl.pallas_call(
        return_kernel,
        in_specs=[smem] + [vmem] * 7,
        out_shape=shape((HALO, C), F32),
        compiler_params=PARAMS,
        cost_estimate=cost(3e9, 4e6),
        name="returning",
    )(sides, *in_x, *in_y, face_p, edge_p, tie(w, own))
    own = plus(own, tie(got, placed)).astype(BF)
    got = xor_send(own, 16)
    act_pair = swapped(tie(act, own))
    locals_.append(backward(2, tie(grad, own)))
    own = plus(own, tie(got, locals_[2])).astype(BF)
    one = xor_send(own, 8)
    locals_.append(backward(3, tie(grad, own)))
    one = tie(one, locals_[3])
    two = xor_send(jnp.stack([own, one]), 2)
    mixed, input_grad = pl.pallas_call(
        final_kernel,
        out_shape=[shape((ROWS, C), BF), shape((ROWS, C), BF)],
        compiler_params=PARAMS,
        cost_estimate=cost(1e9, 3e6),
        name="final",
    )(*locals_, tie(placed, one), rr, act, act_pair)
    two = tie(two, input_grad)
    four = xor_send(jnp.concatenate([jnp.stack([own, one]), two], 0), 1)
    weight_grad = pl.pallas_call(
        assemble_kernel,
        in_specs=[smem] + [vmem] * 4,
        out_shape=shape((8,) + own.shape, F32),
        compiler_params=PARAMS,
        cost_estimate=cost(1e6, 3e6),
        name="assemble",
    )(jnp.stack(bits).astype(jnp.int32), own, one, two, four)
    return (mixed[None], input_grad[None], weight_grad.reshape(w.shape)[None])


def solution(mesh):
    in_specs = (
        P("segment", "space", None),
        P("segment", None, None, None),
        P("segment", "space", None),
        P("space", None),
        P("space", None),
        P("space"),
    )
    out_specs = (
        P("segment", "space", None),
        P("segment", "space", None),
        P("segment", None, None, None),
    )
    return jax.shard_map(
        on_device, mesh=mesh, in_specs=in_specs, out_specs=out_specs, check_vma=False
    )
```

```python
import functools

import jax
import jax.numpy as jnp
from jax import lax
from jax.experimental import pallas as pl
from jax.experimental.pallas import tpu as pltpu
from jax.sharding import PartitionSpec as P

TZ = 32
TILES_X = 4
CAP = 256
ROWS = 1024
C = 128
HALO = 1152

DIRECTIONS = ((-1, -1), (-1, 0), (-1, 1), (0, -1), (0, 1), (1, -1), (1, 0), (1, 1))
BF = jnp.bfloat16
F32 = jnp.float32


def spans():
    result = []
    start = 0
    for step_x, step_y in DIRECTIONS:
        length = TZ if step_x != 0 and step_y != 0 else CAP
        result.append((start, length))
        start = start + length
    return result


SPANS = spans()
FACES = [n for n, (a, b) in enumerate(DIRECTIONS) if a == 0 or b == 0]
CORNERS = [n for n, (a, b) in enumerate(DIRECTIONS) if a != 0 and b != 0]


def toward(step_x, step_y):
    picked = []
    for offset in range(27):
        along_x = offset // 9 - 1
        along_y = offset // 3 % 3 - 1
        if (step_x == 0 or along_x == -step_x) and (step_y == 0 or along_y == -step_y):
            picked.append(offset)
    return picked


def dot(a, b, dims=((1,), (0,))):
    return lax.dot_general(a, b, (dims, ((), ())), preferred_element_type=F32)


def hot(row, rows):
    pos = lax.broadcasted_iota(jnp.int32, (256, 128), 0).astype(jnp.int16)
    count = row.shape[1]
    blocks = []
    for base in range(0, rows, 256):
        rel = (row - base).astype(jnp.int16)
        parts = [
            jnp.where(rel[:, t : t + 128] == pos, BF(1), BF(0)) for t in range(0, count, 128)
        ]
        blocks.append(jnp.concatenate(parts, 1))
    return jnp.concatenate(blocks, 0)


def spread(column, count):
    kept = jnp.where(column == ROWS, -1, column)
    return jnp.broadcast_to(kept, (column.shape[0], count)).astype(jnp.int16)


def places_from_one(rows):
    return (lax.broadcasted_iota(jnp.int32, (rows, 128), 0) + 1).astype(BF)


def positions(column, row):
    rows, count = column.shape
    numbers = places_from_one(rows)
    numbers = jnp.concatenate([numbers] * (count // 128), 1)
    found = jnp.where(column == row.astype(jnp.int16), numbers, BF(0))
    while rows > 16:
        rows //= 2
        found = jnp.maximum(found[:rows], found[rows:])
    return jnp.max(found.astype(F32), axis=0, keepdims=True)


def match(row, rows):
    numbers = places_from_one(rows)
    row = row.astype(BF)
    parts = [jnp.where(row[:, t : t + 128] == numbers, BF(1), BF(0)) for t in range(0, row.shape[1], 128)]
    return jnp.concatenate(parts, 1)


def face_rows(block):
    block = block.astype(F32)
    return [jnp.concatenate([block[k : k + 1], block[16 + k : 17 + k]], 1) for k in range(9)]


def column_of(row):
    return jnp.broadcast_to(row.astype(F32), (8, row.shape[1])).T[:, :1].astype(jnp.int32)


def inside(place, axis, dims):
    return (lax.broadcasted_iota(jnp.int32, dims, axis) // TZ) == place


def number_of(step_x, step_y):
    return DIRECTIONS.index((step_x, step_y))


def pack_sides(lists, orient, sides, xa_ref, xb_ref, ya_ref, yb_ref):
    x_odd, y_odd = sides[0] == 1, sides[1] == 1

    def x_side(side):
        picked = [(orient * side, 0), (orient * side, -orient), (orient * side, orient)]
        return jnp.concatenate([lists[number_of(*d)] for d in picked], 0)

    plus, minus = x_side(1), x_side(-1)
    xa_ref[...] = jnp.where(x_odd, minus, plus)
    xb_ref[...] = jnp.where(x_odd, plus, minus)
    plus, minus = lists[number_of(0, orient)], lists[number_of(0, -orient)]
    ya_ref[...] = jnp.where(y_odd, minus, plus)
    yb_ref[...] = jnp.where(y_odd, plus, minus)


def unpack_sides(orient, sides, face, edge, xa, xb, ya, yb):
    x_odd, y_odd = sides[0] == 1, sides[1] == 1

    def of_side(side, odd, a, b):
        return jnp.where(odd, b, a) if side == 1 else jnp.where(odd, a, b)

    lists = []
    for step_x, step_y in DIRECTIONS:
        if step_y == 0:
            lists.append(of_side(-orient * step_x, x_odd, xa[:face], xb[:face]))
        elif step_x == 0:
            lists.append(of_side(-orient * step_y, y_odd, ya[:face], yb[:face]))
        else:
            first = of_side(-orient * step_y, y_odd, ya[face : face + edge], yb[face : face + edge])
            second = of_side(-orient * step_y, y_odd, ya[face + edge :], yb[face + edge :])
            lists.append(of_side(-orient * step_x, x_odd, first, second))
    return lists


def start_kernel(side_ref, x_ref, rr_ref, sm_ref, xa_ref, xb_ref, ya_ref, yb_ref, face_p_ref, edge_p_ref):
    lists = [None] * 8
    row = rr_ref[...]
    column = column_of(row)
    listed = dot(x_ref[...].astype(F32).T.astype(BF), hot(row, ROWS)).T.astype(BF)
    for place, number in enumerate(FACES):
        start, length = SPANS[number]
        other, _ = SPANS[7 - number]
        wide = spread(column[other : other + length], length)
        found = [
            positions(wide, sm_ref[offset : offset + 1, start : start + length])
            for offset in toward(*DIRECTIONS[number])
        ]
        found = jnp.concatenate(found + [jnp.zeros((7, length), F32)], 0)
        found = jnp.concatenate([found[:, :128], found[:, 128:]], 0).astype(BF)
        face_p_ref[place] = found
        lists[number] = jnp.concatenate([listed[other : other + length], found], 0)
    wide = spread(
        jnp.concatenate([column[SPANS[7 - n][0] : SPANS[7 - n][0] + TZ] for n in CORNERS], 0), 4 * TZ
    )
    found = []
    for step in range(3):
        pieces = []
        for number in CORNERS:
            start, length = SPANS[number]
            offset = toward(*DIRECTIONS[number])[step]
            pieces.append(sm_ref[offset : offset + 1, start : start + length])
        found.append(positions(wide, jnp.concatenate(pieces, 1)))
    found = jnp.concatenate(found + [jnp.zeros((13, 4 * TZ), F32)], 0).astype(BF)
    edge_p_ref[...] = found
    for number in CORNERS:
        other, length = SPANS[7 - number]
        lists[number] = jnp.concatenate([listed[other : other + length], found], 0)
    pack_sides(lists, 1, (side_ref[0], side_ref[1]), xa_ref, xb_ref, ya_ref, yb_ref)


def forward_kernel(x_ref, lm_ref, w_ref, g_ref, pre_ref, x_t, total, *, width):
    step = pl.program_id(0)

    @pl.when(step == 0)
    def _():
        x_t[...] = x_ref[...].astype(F32).T.astype(BF)
        total[...] = dot(w_ref[13], x_t[...], ((0,), (0,)))

    source = x_t[...]
    weight = jnp.concatenate([w_ref[14 * step + i] for i in range(13)], 0)
    for begin in range(0, ROWS, width):
        cols = slice(begin, begin + width)
        gathered = [
            dot(source, hot(lm_ref[pl.ds(14 * step + i, 1), cols], ROWS)).astype(BF) for i in range(13)
        ]
        gathered = jnp.concatenate(gathered, 0)
        g_ref[:, cols] = gathered
        total[:, cols] += dot(weight, gathered, ((0,), (0,)))

    @pl.when(step == 1)
    def _():
        pre_ref[...] = total[...].T


def high_low(values):
    high = values.astype(BF)
    return jnp.concatenate([high, (values - high.astype(F32)).astype(BF)], 1)


def activate_kernel(
    side_ref, pre_ref, ixa_ref, ixb_ref, iya_ref, iyb_ref, rr_ref, cot_ref, pair_ref, w_ref,
    act_ref, grad_ref, xa_ref, xb_ref, ya_ref, yb_ref, dw_ref,
):
    sides = (side_ref[0], side_ref[1])
    arrived = unpack_sides(
        1, sides, CAP + 32, TZ + 16, ixa_ref[...], ixb_ref[...], iya_ref[...], iyb_ref[...]
    )
    sums = [None] * 8
    sources = []
    for number in FACES:
        picked = toward(*DIRECTIONS[number])
        source = arrived[number][:CAP].astype(F32).T.astype(BF)
        sources.append(source)
        gathered = [dot(source, match(row, CAP)).astype(BF) for row in face_rows(arrived[number][CAP:])]
        weight = jnp.concatenate([w_ref[offset] for offset in picked], 0)
        sums[number] = dot(weight, jnp.concatenate(gathered, 0), ((0,), (0,))).T
    edge_source = jnp.concatenate([arrived[n][:TZ] for n in CORNERS], 0).astype(F32).T.astype(BF)
    edge_found = jnp.zeros((16, 4 * TZ), F32)
    for place, number in enumerate(CORNERS):
        rows = arrived[number][TZ:].astype(F32)
        edge_found = jnp.where(inside(place, 1, rows.shape), rows, edge_found)
    gathered = [dot(edge_source, match(edge_found[k : k + 1], 4 * TZ)).astype(BF) for k in range(3)]
    masked = []
    weights = []
    for place, number in enumerate(CORNERS):
        for step in range(3):
            masked.append(jnp.where(inside(place, 1, (C, 4 * TZ)), gathered[step], BF(0)))
            weights.append(w_ref[toward(*DIRECTIONS[number])[step]])
    total = dot(jnp.concatenate(weights, 0), jnp.concatenate(masked, 0), ((0,), (0,))).T
    for place, number in enumerate(CORNERS):
        sums[number] = total[place * TZ : (place + 1) * TZ]

    selector = hot(rr_ref[...], ROWS)
    both = dot(selector, high_low(jnp.concatenate(sums, 0)))
    pre = pre_ref[...] + both[:, :C] + both[:, C:]
    gate = 1.0 / (1.0 + jnp.exp(-pre))
    act_ref[...] = (pre * gate).astype(BF)
    upstream = cot_ref[...].astype(F32) + pair_ref[...].astype(F32)
    grad = upstream * gate * (1.0 + pre * (1.0 - gate))
    grad_ref[...] = grad.astype(BF)
    listed = dot(grad.T.astype(BF), selector).T.astype(BF)
    lists = [listed[start : start + length] for start, length in SPANS]
    pack_sides(lists, -1, sides, xa_ref, xb_ref, ya_ref, yb_ref)

    dw_ref[...] = jnp.zeros_like(dw_ref)
    for source, number in zip(sources, FACES):
        pieces = [
            dot(match(row, CAP), lists[number]).astype(BF) for row in face_rows(arrived[number][CAP:])
        ]
        part = dot(source, jnp.concatenate(pieces, 1))
        for index, offset in enumerate(toward(*DIRECTIONS[number])):
            dw_ref[offset] += part[:, index * C : (index + 1) * C]
    back = jnp.concatenate([lists[n] for n in CORNERS], 0)
    spots = [dot(match(edge_found[k : k + 1], 4 * TZ), back).astype(BF) for k in range(3)]
    pieces = [
        jnp.where(inside(place, 0, (4 * TZ, C)), spots[step], BF(0)) for place in range(4) for step in range(3)
    ]
    part = dot(edge_source, jnp.concatenate(pieces, 1))
    for place, number in enumerate(CORNERS):
        for step in range(3):
            index = 3 * place + step
            dw_ref[toward(*DIRECTIONS[number])[step]] += part[:, index * C : (index + 1) * C]


def weight_kernel(g_ref, grad_ref, x_ref, halo_ref, dw_ref):
    step = pl.program_id(0)

    @pl.when(step == 0)
    def _():
        dw_ref[13] = halo_ref[13] + dot(x_ref[...], grad_ref[...], ((0,), (0,)))

    total = dot(g_ref[...], grad_ref[...])
    dw_ref[pl.ds(14 * step, 13)] = halo_ref[pl.ds(14 * step, 13)] + total.reshape(13, C, C)


def return_kernel(side_ref, ixa_ref, ixb_ref, iya_ref, iyb_ref, face_p_ref, edge_p_ref, w_ref, placed_ref):
    sides = (side_ref[0], side_ref[1])
    returned = unpack_sides(-1, sides, CAP, TZ, ixa_ref[...], ixb_ref[...], iya_ref[...], iyb_ref[...])
    for place, number in enumerate(FACES):
        other, length = SPANS[7 - number]
        pieces = [dot(match(row, CAP), returned[number]).astype(BF) for row in face_rows(face_p_ref[place])]
        weight = jnp.concatenate([w_ref[offset] for offset in toward(*DIRECTIONS[number])], 1)
        placed_ref[other : other + length, :] = dot(jnp.concatenate(pieces, 1), weight, ((1,), (1,)))
    back = jnp.concatenate([returned[n] for n in CORNERS], 0)
    found = edge_p_ref[...].astype(F32)
    spots = [dot(match(found[k : k + 1], 4 * TZ), back).astype(BF) for k in range(3)]
    pieces = []
    weights = []
    for place, number in enumerate(CORNERS):
        for step in range(3):
            pieces.append(jnp.where(inside(place, 0, (4 * TZ, C)), spots[step], BF(0)))
            weights.append(w_ref[toward(*DIRECTIONS[number])[step]])
    result = dot(jnp.concatenate(pieces, 1), jnp.concatenate(weights, 1), ((1,), (1,)))
    for place, number in enumerate(CORNERS):
        other, length = SPANS[7 - number]
        placed_ref[other : other + length, :] = result[place * TZ : (place + 1) * TZ, :]


def backward_kernel(grad_ref, lm_ref, w_ref, out_ref, *, begin):
    size = out_ref.shape[0]
    source = grad_ref[...].astype(F32).T.astype(BF)
    gathered = []
    for k in range(27):
        if k == 13:
            gathered.append(source[:, begin : begin + size])
        else:
            gathered.append(dot(source, hot(lm_ref[26 - k : 27 - k, begin : begin + size], ROWS)).astype(BF))
    weight = jnp.concatenate([w_ref[k] for k in range(27)], 1)
    out_ref[...] = dot(weight, jnp.concatenate(gathered, 0)).T


def final_kernel(*refs):
    placed_ref, rr_ref, act_ref, pair_ref, mixed_ref, out_ref = refs[-6:]
    both = dot(hot(rr_ref[...], ROWS), high_low(placed_ref[...]))
    both = both[:, :C] + both[:, C:]
    size = ROWS // len(refs[:-6])
    for index, ref in enumerate(refs[:-6]):
        rows = slice(index * size, (index + 1) * size)
        out_ref[rows, :] = (ref[...] + both[rows]).astype(BF)
    mixed_ref[...] = (act_ref[...].astype(F32) + pair_ref[...].astype(F32)).astype(BF)


def assemble_kernel(bits_ref, own_ref, one_ref, two_ref, four_ref, out_ref):
    place = bits_ref[0] * 4 + bits_ref[1] * 2 + bits_ref[2]
    blocks = [own_ref[...], one_ref[...]] + [two_ref[i] for i in range(2)] + [four_ref[i] for i in range(4)]
    for distance, block in enumerate(blocks):
        out_ref[place ^ distance] = block.astype(F32)


PARAMS = pltpu.CompilerParams(vmem_limit_bytes=48 * 2**20)


def shape(dims, dtype):
    return jax.ShapeDtypeStruct(dims, dtype)


def whole(dims):
    return pl.BlockSpec(dims, lambda *ids: (0,) * len(dims))


def pairing(axis, which):
    pairs = []
    for tile in range(lax.axis_size("space")):
        at_x, at_y = tile % TILES_X, tile // TILES_X
        tiles_y = lax.axis_size("space") // TILES_X
        if axis == "x":
            move = 1 if (at_x + which) % 2 == 0 else -1
            at_x = (at_x + move) % TILES_X
        else:
            move = 1 if (at_y + which) % 2 == 0 else -1
            at_y = (at_y + move) % tiles_y
        pairs.append((tile, at_y * TILES_X + at_x))
    return pairs


def exchange_x(xa, xb):
    return [lax.ppermute(v, "space", pairing("x", n)) for n, v in enumerate((xa, xb))]


def exchange_y(ya, yb, xa, xb, sides, face, edge):
    sent = []
    for which, own in enumerate((ya, yb)):
        down = sides[1] != which
        corners = [jnp.where(down, v[face : face + edge], v[face + edge :]) for v in (xa, xb)]
        sent.append(jnp.concatenate([own] + corners, 0))
    return [lax.ppermute(v, "space", pairing("y", n)) for n, v in enumerate(sent)]


def swapped(array):
    return lax.ppermute(array, "segment", [(i, i ^ 1) for i in range(lax.axis_size("segment"))])


def xor_send(value, bits):
    return lax.ppermute(value, "space", [(i, i ^ bits) for i in range(lax.axis_size("space"))])


def pick(array, index):
    return lax.dynamic_index_in_dim(array, index, 0, False)


def cost(flops, data):
    return pl.CostEstimate(flops=int(flops), bytes_accessed=int(data), transcendentals=0)


def tie(value, other):
    return lax.optimization_barrier((value, other))[0]


def on_device(features, weights, cotangent, local_map, send_map, recv_map):
    x = features[0]
    w = weights[0]
    cot = cotangent[0]
    lm = local_map.T
    sm = send_map.T
    rr = recv_map.reshape(1, HALO)
    me = lax.axis_index("space")
    sides = jnp.stack([me % 2, me // TILES_X % 2]).astype(jnp.int32)
    smem = pl.BlockSpec(memory_space=pltpu.SMEM)
    vmem = pl.BlockSpec(memory_space=pltpu.VMEM)
    def lists_shape(face, edge):
        return [shape((face + 2 * edge, C), BF)] * 2 + [shape((face, C), BF)] * 2

    xa, xb, ya, yb, face_p, edge_p = pl.pallas_call(
        start_kernel,
        in_specs=[smem] + [vmem] * 3,
        out_shape=lists_shape(CAP + 32, TZ + 16) + [shape((4, 32, C), BF), shape((16, C), BF)],
        compiler_params=PARAMS,
        cost_estimate=cost(2e9, 4e6),
        name="start",
    )(sides, x, rr, sm)
    cot_pair = swapped(cot)
    in_x = exchange_x(xa, xb)
    in_y = exchange_y(ya, yb, *in_x, sides, CAP + 32, TZ + 16)
    gathered, pre = pl.pallas_call(
        functools.partial(forward_kernel, width=512),
        grid=(2,),
        in_specs=[whole((ROWS, C)), whole((27, ROWS)), whole((27, C, C))],
        out_specs=[pl.BlockSpec((13 * C, ROWS), lambda j: (j, 0)), whole((ROWS, C))],
        out_shape=[shape((26 * C, ROWS), BF), shape((ROWS, C), F32)],
        scratch_shapes=[pltpu.VMEM((C, ROWS), BF), pltpu.VMEM((C, ROWS), F32)],
        compiler_params=PARAMS,
        cost_estimate=cost(15e9, 9e6),
        name="forward",
    )(x, lm, w)
    act, grad, xa, xb, ya, yb, dw_halo = pl.pallas_call(
        activate_kernel,
        in_specs=[smem] + [vmem] * 9,
        out_shape=[shape((ROWS, C), BF)] * 2 + lists_shape(CAP, TZ) + [shape((27, C, C), F32)],
        compiler_params=PARAMS,
        cost_estimate=cost(4e9, 3e6),
        name="activate",
    )(sides, pre, *in_x, *in_y, rr, cot, cot_pair, w)
    dw = pl.pallas_call(
        weight_kernel,
        grid=(2,),
        in_specs=[pl.BlockSpec((13 * C, ROWS), lambda j: (j, 0)), whole((ROWS, C)), whole((ROWS, C)), whole((27, C, C))],
        out_specs=whole((27, C, C)),
        out_shape=shape((27, C, C), F32),
        compiler_params=PARAMS,
        cost_estimate=cost(4e9, 9e6),
        name="weight",
    )(gathered, grad, x, dw_halo)

    size = ROWS // 4

    def backward(index, grad):
        return pl.pallas_call(
            functools.partial(backward_kernel, begin=index * size),
            out_shape=shape((size, C), F32),
            compiler_params=PARAMS,
            cost_estimate=cost(3e9, 2e6),
            name="backward",
        )(grad, lm, w)

    bits = [me % 2, me // 2 % 2, me // 8 % 2]
    blocks = dw.reshape(2, 2, 2, -1, C)

    def halve(blocks, stage):
        return pick(blocks, bits[stage]), pick(blocks, 1 - bits[stage]).astype(BF)

    def plus(one, two):
        return one.astype(F32) + two.astype(F32)

    locals_ = []
    kept, sent = halve(blocks, 0)
    got = xor_send(sent, 1)
    kept, sent = halve(plus(kept, got), 1)
    got = xor_send(sent, 2)
    in_x = exchange_x(tie(xa, sent), tie(xb, sent))
    locals_.append(backward(0, tie(grad, sent)))
    kept, sent = halve(plus(kept, tie(got, locals_[0])), 2)
    got = xor_send(sent, 8)
    locals_.append(backward(1, tie(grad, sent)))
    own = plus(kept, tie(got, locals_[1])).astype(BF)
    got = xor_send(own, 4)
    in_y = exchange_y(tie(ya, own), tie(yb, own), *in_x, sides, CAP, TZ)
    locals_.append(backward(2, tie(grad, own)))
    own = plus(own, tie(got, locals_[2])).astype(BF)
    got = xor_send(own, 16)
    act_pair = swapped(tie(act, own))
    placed = pl.pallas_call(
        return_kernel,
        in_specs=[smem] + [vmem] * 7,
        out_shape=shape((HALO, C), F32),
        compiler_params=PARAMS,
        cost_estimate=cost(3e9, 4e6),
        name="returning",
    )(sides, *in_x, *in_y, face_p, edge_p, tie(w, own))
    own = plus(own, tie(got, placed)).astype(BF)
    one = xor_send(own, 8)
    locals_.append(backward(3, tie(grad, own)))
    one = tie(one, locals_[3])
    two = xor_send(jnp.stack([own, one]), 2)
    mixed, input_grad = pl.pallas_call(
        final_kernel,
        out_shape=[shape((ROWS, C), BF), shape((ROWS, C), BF)],
        compiler_params=PARAMS,
        cost_estimate=cost(1e9, 3e6),
        name="final",
    )(*locals_, tie(placed, one), rr, act, act_pair)
    two = tie(two, input_grad)
    four = xor_send(jnp.concatenate([jnp.stack([own, one]), two], 0), 1)
    weight_grad = pl.pallas_call(
        assemble_kernel,
        in_specs=[smem] + [vmem] * 4,
        out_shape=shape((8,) + own.shape, F32),
        compiler_params=PARAMS,
        cost_estimate=cost(1e6, 3e6),
        name="assemble",
    )(jnp.stack(bits).astype(jnp.int32), own, one, two, four)
    return (mixed[None], input_grad[None], weight_grad.reshape(dw.shape)[None])


def solution(mesh):
    in_specs = (
        P("segment", "space", None),
        P("segment", None, None, None),
        P("segment", "space", None),
        P("space", None),
        P("space", None),
        P("space"),
    )
    out_specs = (
        P("segment", "space", None),
        P("segment", "space", None),
        P("segment", None, None, None),
    )
    return jax.shard_map(
        on_device, mesh=mesh, in_specs=in_specs, out_specs=out_specs, check_vma=False
    )
```

```python
import functools

import jax
import jax.numpy as jnp
from jax import lax
from jax.experimental import pallas as pl
from jax.experimental.pallas import tpu as pltpu
from jax.sharding import PartitionSpec as P

TZ = 32
TILES_X = 4
CAP = 256
ROWS = 1024
C = 128
HALO = 1152

DIRECTIONS = ((-1, -1), (-1, 0), (-1, 1), (0, -1), (0, 1), (1, -1), (1, 0), (1, 1))
BF = jnp.bfloat16
F32 = jnp.float32


def spans():
    result = []
    start = 0
    for step_x, step_y in DIRECTIONS:
        length = TZ if step_x != 0 and step_y != 0 else CAP
        result.append((start, length))
        start = start + length
    return result


SPANS = spans()
FACES = [n for n, (a, b) in enumerate(DIRECTIONS) if a == 0 or b == 0]
CORNERS = [n for n, (a, b) in enumerate(DIRECTIONS) if a != 0 and b != 0]


def toward(step_x, step_y):
    picked = []
    for offset in range(27):
        along_x = offset // 9 - 1
        along_y = offset // 3 % 3 - 1
        if (step_x == 0 or along_x == -step_x) and (step_y == 0 or along_y == -step_y):
            picked.append(offset)
    return picked


def dot(a, b, dims=((1,), (0,))):
    return lax.dot_general(a, b, (dims, ((), ())), preferred_element_type=F32)


def hot(row, rows):
    pos = lax.broadcasted_iota(jnp.int32, (256, 128), 0).astype(jnp.int16)
    count = row.shape[1]
    blocks = []
    for base in range(0, rows, 256):
        rel = (row - base).astype(jnp.int16)
        parts = [
            jnp.where(rel[:, t : t + 128] == pos, BF(1), BF(0)) for t in range(0, count, 128)
        ]
        blocks.append(jnp.concatenate(parts, 1))
    return jnp.concatenate(blocks, 0)


def spread(column, count):
    kept = jnp.where(column == ROWS, -1, column)
    return jnp.broadcast_to(kept, (column.shape[0], count)).astype(jnp.int16)


def places_from_one(rows):
    return (lax.broadcasted_iota(jnp.int32, (rows, 128), 0) + 1).astype(BF)


def positions(column, row):
    rows, count = column.shape
    numbers = places_from_one(rows)
    numbers = jnp.concatenate([numbers] * (count // 128), 1)
    found = jnp.where(column == row.astype(jnp.int16), numbers, BF(0))
    while rows > 16:
        rows //= 2
        found = jnp.maximum(found[:rows], found[rows:])
    return jnp.max(found.astype(F32), axis=0, keepdims=True)


def match(row, rows):
    numbers = places_from_one(rows)
    row = row.astype(BF)
    parts = [jnp.where(row[:, t : t + 128] == numbers, BF(1), BF(0)) for t in range(0, row.shape[1], 128)]
    return jnp.concatenate(parts, 1)


def face_rows(block):
    block = block.astype(F32)
    return [jnp.concatenate([block[k : k + 1], block[16 + k : 17 + k]], 1) for k in range(9)]


def column_of(row):
    return jnp.broadcast_to(row.astype(F32), (8, row.shape[1])).T[:, :1].astype(jnp.int32)


def inside(place, axis, dims):
    return (lax.broadcasted_iota(jnp.int32, dims, axis) // TZ) == place


def number_of(step_x, step_y):
    return DIRECTIONS.index((step_x, step_y))


def pack_sides(lists, orient, sides, xa_ref, xb_ref, ya_ref, yb_ref):
    x_odd, y_odd = sides[0] == 1, sides[1] == 1

    def x_side(side):
        picked = [(orient * side, 0), (orient * side, -orient), (orient * side, orient)]
        return jnp.concatenate([lists[number_of(*d)] for d in picked], 0)

    plus, minus = x_side(1), x_side(-1)
    xa_ref[...] = jnp.where(x_odd, minus, plus)
    xb_ref[...] = jnp.where(x_odd, plus, minus)
    plus, minus = lists[number_of(0, orient)], lists[number_of(0, -orient)]
    ya_ref[...] = jnp.where(y_odd, minus, plus)
    yb_ref[...] = jnp.where(y_odd, plus, minus)


def unpack_sides(orient, sides, face, edge, xa, xb, ya, yb):
    x_odd, y_odd = sides[0] == 1, sides[1] == 1

    def of_side(side, odd, a, b):
        return jnp.where(odd, b, a) if side == 1 else jnp.where(odd, a, b)

    lists = []
    for step_x, step_y in DIRECTIONS:
        if step_y == 0:
            lists.append(of_side(-orient * step_x, x_odd, xa[:face], xb[:face]))
        elif step_x == 0:
            lists.append(of_side(-orient * step_y, y_odd, ya[:face], yb[:face]))
        else:
            first = of_side(-orient * step_y, y_odd, ya[face : face + edge], yb[face : face + edge])
            second = of_side(-orient * step_y, y_odd, ya[face + edge :], yb[face + edge :])
            lists.append(of_side(-orient * step_x, x_odd, first, second))
    return lists


def start_kernel(side_ref, x_ref, rr_ref, sm_ref, xa_ref, xb_ref, ya_ref, yb_ref, face_p_ref, edge_p_ref):
    lists = [None] * 8
    row = rr_ref[...]
    column = column_of(row)
    listed = dot(x_ref[...].astype(F32).T.astype(BF), hot(row, ROWS)).T.astype(BF)
    for place, number in enumerate(FACES):
        start, length = SPANS[number]
        other, _ = SPANS[7 - number]
        wide = spread(column[other : other + length], length)
        found = [
            positions(wide, sm_ref[offset : offset + 1, start : start + length])
            for offset in toward(*DIRECTIONS[number])
        ]
        found = jnp.concatenate(found + [jnp.zeros((7, length), F32)], 0)
        found = jnp.concatenate([found[:, :128], found[:, 128:]], 0).astype(BF)
        face_p_ref[place] = found
        lists[number] = jnp.concatenate([listed[other : other + length], found], 0)
    wide = spread(
        jnp.concatenate([column[SPANS[7 - n][0] : SPANS[7 - n][0] + TZ] for n in CORNERS], 0), 4 * TZ
    )
    found = []
    for step in range(3):
        pieces = []
        for number in CORNERS:
            start, length = SPANS[number]
            offset = toward(*DIRECTIONS[number])[step]
            pieces.append(sm_ref[offset : offset + 1, start : start + length])
        found.append(positions(wide, jnp.concatenate(pieces, 1)))
    found = jnp.concatenate(found + [jnp.zeros((13, 4 * TZ), F32)], 0).astype(BF)
    edge_p_ref[...] = found
    for number in CORNERS:
        other, length = SPANS[7 - number]
        lists[number] = jnp.concatenate([listed[other : other + length], found], 0)
    pack_sides(lists, 1, (side_ref[0], side_ref[1]), xa_ref, xb_ref, ya_ref, yb_ref)


def forward_kernel(x_ref, lm_ref, w_ref, g_ref, pre_ref, x_t, total, *, width):
    step = pl.program_id(0)

    @pl.when(step == 0)
    def _():
        x_t[...] = x_ref[...].astype(F32).T.astype(BF)
        total[...] = dot(w_ref[13], x_t[...], ((0,), (0,)))

    source = x_t[...]
    weight = jnp.concatenate([w_ref[14 * step + i] for i in range(13)], 0)
    for begin in range(0, ROWS, width):
        cols = slice(begin, begin + width)
        gathered = [
            dot(source, hot(lm_ref[pl.ds(14 * step + i, 1), cols], ROWS)).astype(BF) for i in range(13)
        ]
        gathered = jnp.concatenate(gathered, 0)
        g_ref[:, cols] = gathered
        total[:, cols] += dot(weight, gathered, ((0,), (0,)))

    @pl.when(step == 1)
    def _():
        pre_ref[...] = total[...].T


def high_low(values):
    high = values.astype(BF)
    return jnp.concatenate([high, (values - high.astype(F32)).astype(BF)], 1)


def activate_kernel(
    side_ref, pre_ref, ixa_ref, ixb_ref, iya_ref, iyb_ref, rr_ref, cot_ref, pair_ref, w_ref,
    act_ref, grad_ref, xa_ref, xb_ref, ya_ref, yb_ref, dw_ref,
):
    sides = (side_ref[0], side_ref[1])
    arrived = unpack_sides(
        1, sides, CAP + 32, TZ + 16, ixa_ref[...], ixb_ref[...], iya_ref[...], iyb_ref[...]
    )
    sums = [None] * 8
    sources = []
    for number in FACES:
        picked = toward(*DIRECTIONS[number])
        source = arrived[number][:CAP].astype(F32).T.astype(BF)
        sources.append(source)
        gathered = [dot(source, match(row, CAP)).astype(BF) for row in face_rows(arrived[number][CAP:])]
        weight = jnp.concatenate([w_ref[offset] for offset in picked], 0)
        sums[number] = dot(weight, jnp.concatenate(gathered, 0), ((0,), (0,))).T
    edge_source = jnp.concatenate([arrived[n][:TZ] for n in CORNERS], 0).astype(F32).T.astype(BF)
    edge_found = jnp.zeros((16, 4 * TZ), F32)
    for place, number in enumerate(CORNERS):
        rows = arrived[number][TZ:].astype(F32)
        edge_found = jnp.where(inside(place, 1, rows.shape), rows, edge_found)
    gathered = [dot(edge_source, match(edge_found[k : k + 1], 4 * TZ)).astype(BF) for k in range(3)]
    masked = []
    weights = []
    for place, number in enumerate(CORNERS):
        for step in range(3):
            masked.append(jnp.where(inside(place, 1, (C, 4 * TZ)), gathered[step], BF(0)))
            weights.append(w_ref[toward(*DIRECTIONS[number])[step]])
    total = dot(jnp.concatenate(weights, 0), jnp.concatenate(masked, 0), ((0,), (0,))).T
    for place, number in enumerate(CORNERS):
        sums[number] = total[place * TZ : (place + 1) * TZ]

    selector = hot(rr_ref[...], ROWS)
    both = dot(selector, high_low(jnp.concatenate(sums, 0)))
    pre = pre_ref[...] + both[:, :C] + both[:, C:]
    gate = 1.0 / (1.0 + jnp.exp(-pre))
    act_ref[...] = (pre * gate).astype(BF)
    upstream = cot_ref[...].astype(F32) + pair_ref[...].astype(F32)
    grad = upstream * gate * (1.0 + pre * (1.0 - gate))
    grad_ref[...] = grad.astype(BF)
    listed = dot(grad.T.astype(BF), selector).T.astype(BF)
    lists = [listed[start : start + length] for start, length in SPANS]
    pack_sides(lists, -1, sides, xa_ref, xb_ref, ya_ref, yb_ref)

    dw_ref[...] = jnp.zeros_like(dw_ref)
    for source, number in zip(sources, FACES):
        pieces = [
            dot(match(row, CAP), lists[number]).astype(BF) for row in face_rows(arrived[number][CAP:])
        ]
        part = dot(source, jnp.concatenate(pieces, 1))
        for index, offset in enumerate(toward(*DIRECTIONS[number])):
            dw_ref[offset] += part[:, index * C : (index + 1) * C]
    back = jnp.concatenate([lists[n] for n in CORNERS], 0)
    spots = [dot(match(edge_found[k : k + 1], 4 * TZ), back).astype(BF) for k in range(3)]
    pieces = [
        jnp.where(inside(place, 0, (4 * TZ, C)), spots[step], BF(0)) for place in range(4) for step in range(3)
    ]
    part = dot(edge_source, jnp.concatenate(pieces, 1))
    for place, number in enumerate(CORNERS):
        for step in range(3):
            index = 3 * place + step
            dw_ref[toward(*DIRECTIONS[number])[step]] += part[:, index * C : (index + 1) * C]


def weight_kernel(side_ref, g_ref, grad_ref, x_ref, halo_ref, kept_ref, sent_ref, total):
    step = pl.program_id(0)

    @pl.when(step == 0)
    def _():
        middle = halo_ref[13] + dot(x_ref[...], grad_ref[...], ((0,), (0,)))
        total[13 * C : 14 * C, :] = middle

    part = dot(g_ref[...], grad_ref[...]) + halo_ref[pl.ds(14 * step, 13)].reshape(13 * C, C)
    total[pl.ds(pl.multiple_of(14 * C * step, 8), 13 * C), :] = part

    @pl.when(step == 1)
    def _():
        half = kept_ref.shape[0]
        kept_ref[...] = total[pl.ds(pl.multiple_of(side_ref[2] * half, 8), half), :]
        sent_ref[...] = total[pl.ds(pl.multiple_of((1 - side_ref[2]) * half, 8), half), :].astype(BF)


def return_kernel(side_ref, ixa_ref, ixb_ref, iya_ref, iyb_ref, face_p_ref, edge_p_ref, w_ref, placed_ref):
    sides = (side_ref[0], side_ref[1])
    returned = unpack_sides(-1, sides, CAP, TZ, ixa_ref[...], ixb_ref[...], iya_ref[...], iyb_ref[...])
    for place, number in enumerate(FACES):
        other, length = SPANS[7 - number]
        pieces = [dot(match(row, CAP), returned[number]).astype(BF) for row in face_rows(face_p_ref[place])]
        weight = jnp.concatenate([w_ref[offset] for offset in toward(*DIRECTIONS[number])], 1)
        placed_ref[other : other + length, :] = dot(jnp.concatenate(pieces, 1), weight, ((1,), (1,)))
    back = jnp.concatenate([returned[n] for n in CORNERS], 0)
    found = edge_p_ref[...].astype(F32)
    spots = [dot(match(found[k : k + 1], 4 * TZ), back).astype(BF) for k in range(3)]
    pieces = []
    weights = []
    for place, number in enumerate(CORNERS):
        for step in range(3):
            pieces.append(jnp.where(inside(place, 0, (4 * TZ, C)), spots[step], BF(0)))
            weights.append(w_ref[toward(*DIRECTIONS[number])[step]])
    result = dot(jnp.concatenate(pieces, 1), jnp.concatenate(weights, 1), ((1,), (1,)))
    for place, number in enumerate(CORNERS):
        other, length = SPANS[7 - number]
        placed_ref[other : other + length, :] = result[place * TZ : (place + 1) * TZ, :]


def backward_kernel(grad_ref, lm_ref, w_ref, out_ref, *, begin):
    size = out_ref.shape[0]
    source = grad_ref[...].astype(F32).T.astype(BF)
    gathered = []
    for k in range(27):
        if k == 13:
            gathered.append(source[:, begin : begin + size])
        else:
            gathered.append(dot(source, hot(lm_ref[26 - k : 27 - k, begin : begin + size], ROWS)).astype(BF))
    weight = jnp.concatenate([w_ref[k] for k in range(27)], 1)
    out_ref[...] = dot(weight, jnp.concatenate(gathered, 0)).T


def final_kernel(*refs):
    placed_ref, rr_ref, act_ref, pair_ref, mixed_ref, out_ref = refs[-6:]
    both = dot(hot(rr_ref[...], ROWS), high_low(placed_ref[...]))
    both = both[:, :C] + both[:, C:]
    size = ROWS // len(refs[:-6])
    for index, ref in enumerate(refs[:-6]):
        rows = slice(index * size, (index + 1) * size)
        out_ref[rows, :] = (ref[...] + both[rows]).astype(BF)
    mixed_ref[...] = (act_ref[...].astype(F32) + pair_ref[...].astype(F32)).astype(BF)


def assemble_kernel(bits_ref, own_ref, one_ref, two_ref, four_ref, out_ref):
    place = bits_ref[0] * 4 + bits_ref[1] * 2 + bits_ref[2]
    blocks = [own_ref[...], one_ref[...]] + [two_ref[i] for i in range(2)] + [four_ref[i] for i in range(4)]
    for distance, block in enumerate(blocks):
        out_ref[place ^ distance] = block.astype(F32)


PARAMS = pltpu.CompilerParams(vmem_limit_bytes=48 * 2**20)


def shape(dims, dtype):
    return jax.ShapeDtypeStruct(dims, dtype)


def whole(dims):
    return pl.BlockSpec(dims, lambda *ids: (0,) * len(dims))


def pairing(axis, which):
    pairs = []
    for tile in range(lax.axis_size("space")):
        at_x, at_y = tile % TILES_X, tile // TILES_X
        tiles_y = lax.axis_size("space") // TILES_X
        if axis == "x":
            move = 1 if (at_x + which) % 2 == 0 else -1
            at_x = (at_x + move) % TILES_X
        else:
            move = 1 if (at_y + which) % 2 == 0 else -1
            at_y = (at_y + move) % tiles_y
        pairs.append((tile, at_y * TILES_X + at_x))
    return pairs


def exchange_x(xa, xb):
    return [lax.ppermute(v, "space", pairing("x", n)) for n, v in enumerate((xa, xb))]


def exchange_y(ya, yb, xa, xb, sides, face, edge):
    sent = []
    for which, own in enumerate((ya, yb)):
        down = sides[1] != which
        corners = [jnp.where(down, v[face : face + edge], v[face + edge :]) for v in (xa, xb)]
        sent.append(jnp.concatenate([own] + corners, 0))
    return [lax.ppermute(v, "space", pairing("y", n)) for n, v in enumerate(sent)]


def swapped(array):
    return lax.ppermute(array, "segment", [(i, i ^ 1) for i in range(lax.axis_size("segment"))])


def xor_send(value, bits):
    return lax.ppermute(value, "space", [(i, i ^ bits) for i in range(lax.axis_size("space"))])


def pick(array, index):
    return lax.dynamic_index_in_dim(array, index, 0, False)


def cost(flops, data):
    return pl.CostEstimate(flops=int(flops), bytes_accessed=int(data), transcendentals=0)


def tie(value, other):
    return lax.optimization_barrier((value, other))[0]


def on_device(features, weights, cotangent, local_map, send_map, recv_map):
    x = features[0]
    w = weights[0]
    cot = cotangent[0]
    lm = local_map.T
    sm = send_map.T
    rr = recv_map.reshape(1, HALO)
    me = lax.axis_index("space")
    sides = jnp.stack([me % 2, me // TILES_X % 2, me % 2]).astype(jnp.int32)
    smem = pl.BlockSpec(memory_space=pltpu.SMEM)
    vmem = pl.BlockSpec(memory_space=pltpu.VMEM)
    def lists_shape(face, edge):
        return [shape((face + 2 * edge, C), BF)] * 2 + [shape((face, C), BF)] * 2

    xa, xb, ya, yb, face_p, edge_p = pl.pallas_call(
        start_kernel,
        in_specs=[smem] + [vmem] * 3,
        out_shape=lists_shape(CAP + 32, TZ + 16) + [shape((4, 32, C), BF), shape((16, C), BF)],
        compiler_params=PARAMS,
        cost_estimate=cost(2e9, 4e6),
        name="start",
    )(sides, x, rr, sm)
    cot_pair = swapped(cot)
    in_x = exchange_x(xa, xb)
    in_y = exchange_y(ya, yb, *in_x, sides, CAP + 32, TZ + 16)
    gathered, pre = pl.pallas_call(
        functools.partial(forward_kernel, width=512),
        grid=(2,),
        in_specs=[whole((ROWS, C)), whole((27, ROWS)), whole((27, C, C))],
        out_specs=[pl.BlockSpec((13 * C, ROWS), lambda j: (j, 0)), whole((ROWS, C))],
        out_shape=[shape((26 * C, ROWS), BF), shape((ROWS, C), F32)],
        scratch_shapes=[pltpu.VMEM((C, ROWS), BF), pltpu.VMEM((C, ROWS), F32)],
        compiler_params=PARAMS,
        cost_estimate=cost(15e9, 9e6),
        name="forward",
    )(x, lm, w)
    act, grad, xa, xb, ya, yb, dw_halo = pl.pallas_call(
        activate_kernel,
        in_specs=[smem] + [vmem] * 9,
        out_shape=[shape((ROWS, C), BF)] * 2 + lists_shape(CAP, TZ) + [shape((27, C, C), F32)],
        compiler_params=PARAMS,
        cost_estimate=cost(4e9, 3e6),
        name="activate",
    )(sides, pre, *in_x, *in_y, rr, cot, cot_pair, w)
    half = 27 * C // 2
    kept, sent = pl.pallas_call(
        weight_kernel,
        grid=(2,),
        in_specs=[smem, pl.BlockSpec((13 * C, ROWS), lambda j: (j, 0)), whole((ROWS, C)), whole((ROWS, C)), whole((27, C, C))],
        out_specs=[whole((half, C)), whole((half, C))],
        out_shape=[shape((half, C), F32), shape((half, C), BF)],
        scratch_shapes=[pltpu.VMEM((27 * C, C), F32)],
        compiler_params=PARAMS,
        cost_estimate=cost(4e9, 9e6),
        name="weight",
    )(sides, gathered, grad, x, dw_halo)

    size = ROWS // 4

    def backward(index, grad):
        return pl.pallas_call(
            functools.partial(backward_kernel, begin=index * size),
            out_shape=shape((size, C), F32),
            compiler_params=PARAMS,
            cost_estimate=cost(3e9, 2e6),
            name="backward",
        )(grad, lm, w)

    bits = [me % 2, (me // 2 + me // 4) % 2, (me // 8 + me // 16) % 2]

    def halve(blocks, stage):
        return pick(blocks, bits[stage]), pick(blocks, 1 - bits[stage]).astype(BF)

    def plus(one, two):
        return one.astype(F32) + two.astype(F32)

    locals_ = []
    got = xor_send(sent, 1)
    kept, sent = halve(plus(kept, got).reshape(2, 2, -1, C), 1)
    got = xor_send(sent, 2)
    locals_.append(backward(0, tie(grad, sent)))
    locals_.append(backward(1, tie(grad, locals_[0])))
    kept, sent = halve(plus(kept, tie(got, locals_[1])), 2)
    got = xor_send(sent, 8)
    in_x = exchange_x(tie(xa, sent), tie(xb, sent))
    own = plus(kept, got).astype(BF)
    got = xor_send(own, 6)
    act_pair = swapped(tie(act, own))
    locals_.append(backward(2, tie(grad, own)))
    own = plus(own, tie(got, locals_[2])).astype(BF)
    got = xor_send(own, 24)
    in_y = exchange_y(tie(ya, own), tie(yb, own), *[tie(v, own) for v in in_x], sides, CAP, TZ)
    locals_.append(backward(3, tie(grad, own)))
    own = plus(own, tie(got, locals_[3])).astype(BF)
    one = xor_send(own, 8)
    placed = pl.pallas_call(
        return_kernel,
        in_specs=[smem] + [vmem] * 7,
        out_shape=shape((HALO, C), F32),
        compiler_params=PARAMS,
        cost_estimate=cost(3e9, 4e6),
        name="returning",
    )(sides, *in_x, *in_y, face_p, edge_p, tie(w, own))
    one = tie(one, placed)
    two = xor_send(jnp.stack([own, one]), 2)
    mixed, input_grad = pl.pallas_call(
        final_kernel,
        out_shape=[shape((ROWS, C), BF), shape((ROWS, C), BF)],
        compiler_params=PARAMS,
        cost_estimate=cost(1e9, 3e6),
        name="final",
    )(*locals_, tie(placed, one), rr, act, act_pair)
    two = tie(two, input_grad)
    four = xor_send(jnp.concatenate([jnp.stack([own, one]), two], 0), 1)
    weight_grad = pl.pallas_call(
        assemble_kernel,
        in_specs=[smem] + [vmem] * 4,
        out_shape=shape((8,) + own.shape, F32),
        compiler_params=PARAMS,
        cost_estimate=cost(1e6, 3e6),
        name="assemble",
    )(jnp.stack(bits).astype(jnp.int32), own, one, two, four)
    return (mixed[None], input_grad[None], weight_grad.reshape(w.shape)[None])


def solution(mesh):
    in_specs = (
        P("segment", "space", None),
        P("segment", None, None, None),
        P("segment", "space", None),
        P("space", None),
        P("space", None),
        P("space"),
    )
    out_specs = (
        P("segment", "space", None),
        P("segment", "space", None),
        P("segment", None, None, None),
    )
    return jax.shard_map(
        on_device, mesh=mesh, in_specs=in_specs, out_specs=out_specs, check_vma=False
    )
```

```python
import functools

import jax
import jax.numpy as jnp
from jax import lax
from jax.experimental import pallas as pl
from jax.experimental.pallas import tpu as pltpu
from jax.sharding import PartitionSpec as P

TZ = 32
TILES_X = 4
CAP = 256
ROWS = 1024
C = 128
HALO = 1152

DIRECTIONS = ((-1, -1), (-1, 0), (-1, 1), (0, -1), (0, 1), (1, -1), (1, 0), (1, 1))
BF = jnp.bfloat16
F32 = jnp.float32


def spans():
    result = []
    start = 0
    for step_x, step_y in DIRECTIONS:
        length = TZ if step_x != 0 and step_y != 0 else CAP
        result.append((start, length))
        start = start + length
    return result


SPANS = spans()
FACES = [n for n, (a, b) in enumerate(DIRECTIONS) if a == 0 or b == 0]
CORNERS = [n for n, (a, b) in enumerate(DIRECTIONS) if a != 0 and b != 0]


def toward(step_x, step_y):
    picked = []
    for offset in range(27):
        along_x = offset // 9 - 1
        along_y = offset // 3 % 3 - 1
        if (step_x == 0 or along_x == -step_x) and (step_y == 0 or along_y == -step_y):
            picked.append(offset)
    return picked


def dot(a, b, dims=((1,), (0,))):
    return lax.dot_general(a, b, (dims, ((), ())), preferred_element_type=F32)


def hot(row, rows):
    pos = lax.broadcasted_iota(jnp.int32, (256, 128), 0).astype(jnp.int16)
    count = row.shape[1]
    blocks = []
    for base in range(0, rows, 256):
        rel = (row - base).astype(jnp.int16)
        parts = [
            jnp.where(rel[:, t : t + 128] == pos, BF(1), BF(0)) for t in range(0, count, 128)
        ]
        blocks.append(jnp.concatenate(parts, 1))
    return jnp.concatenate(blocks, 0)


def spread(column, count):
    kept = jnp.where(column == ROWS, -1, column)
    return jnp.broadcast_to(kept, (column.shape[0], count)).astype(jnp.int16)


def places_from_one(rows):
    return (lax.broadcasted_iota(jnp.int32, (rows, 128), 0) + 1).astype(BF)


def positions(column, row):
    rows, count = column.shape
    numbers = places_from_one(rows)
    numbers = jnp.concatenate([numbers] * (count // 128), 1)
    found = jnp.where(column == row.astype(jnp.int16), numbers, BF(0))
    while rows > 16:
        rows //= 2
        found = jnp.maximum(found[:rows], found[rows:])
    return jnp.max(found.astype(F32), axis=0, keepdims=True)


def match(row, rows):
    numbers = places_from_one(rows)
    row = row.astype(BF)
    parts = [jnp.where(row[:, t : t + 128] == numbers, BF(1), BF(0)) for t in range(0, row.shape[1], 128)]
    return jnp.concatenate(parts, 1)


def face_rows(block):
    block = block.astype(F32)
    return [jnp.concatenate([block[k : k + 1], block[16 + k : 17 + k]], 1) for k in range(9)]


def column_of(row):
    return jnp.broadcast_to(row.astype(F32), (8, row.shape[1])).T[:, :1].astype(jnp.int32)


def inside(place, axis, dims):
    return (lax.broadcasted_iota(jnp.int32, dims, axis) // TZ) == place


def number_of(step_x, step_y):
    return DIRECTIONS.index((step_x, step_y))


def pack_sides(lists, orient, sides, xa_ref, xb_ref, ya_ref, yb_ref):
    x_odd, y_odd = sides[0] == 1, sides[1] == 1

    def x_side(side):
        picked = [(orient * side, 0), (orient * side, -orient), (orient * side, orient)]
        return jnp.concatenate([lists[number_of(*d)] for d in picked], 0)

    plus, minus = x_side(1), x_side(-1)
    xa_ref[...] = jnp.where(x_odd, minus, plus)
    xb_ref[...] = jnp.where(x_odd, plus, minus)
    plus, minus = lists[number_of(0, orient)], lists[number_of(0, -orient)]
    ya_ref[...] = jnp.where(y_odd, minus, plus)
    yb_ref[...] = jnp.where(y_odd, plus, minus)


def unpack_sides(orient, sides, face, edge, xa, xb, ya, yb):
    x_odd, y_odd = sides[0] == 1, sides[1] == 1

    def of_side(side, odd, a, b):
        return jnp.where(odd, b, a) if side == 1 else jnp.where(odd, a, b)

    lists = []
    for step_x, step_y in DIRECTIONS:
        if step_y == 0:
            lists.append(of_side(-orient * step_x, x_odd, xa[:face], xb[:face]))
        elif step_x == 0:
            lists.append(of_side(-orient * step_y, y_odd, ya[:face], yb[:face]))
        else:
            first = of_side(-orient * step_y, y_odd, ya[face : face + edge], yb[face : face + edge])
            second = of_side(-orient * step_y, y_odd, ya[face + edge :], yb[face + edge :])
            lists.append(of_side(-orient * step_x, x_odd, first, second))
    return lists


def start_kernel(side_ref, x_ref, rr_ref, sm_ref, xa_ref, xb_ref, ya_ref, yb_ref, face_p_ref, edge_p_ref):
    lists = [None] * 8
    row = rr_ref[...]
    column = column_of(row)
    listed = dot(x_ref[...].astype(F32).T.astype(BF), hot(row, ROWS)).T.astype(BF)
    for place, number in enumerate(FACES):
        start, length = SPANS[number]
        other, _ = SPANS[7 - number]
        wide = spread(column[other : other + length], length)
        found = [
            positions(wide, sm_ref[offset : offset + 1, start : start + length])
            for offset in toward(*DIRECTIONS[number])
        ]
        found = jnp.concatenate(found + [jnp.zeros((7, length), F32)], 0)
        found = jnp.concatenate([found[:, :128], found[:, 128:]], 0).astype(BF)
        face_p_ref[place] = found
        lists[number] = jnp.concatenate([listed[other : other + length], found], 0)
    wide = spread(
        jnp.concatenate([column[SPANS[7 - n][0] : SPANS[7 - n][0] + TZ] for n in CORNERS], 0), 4 * TZ
    )
    found = []
    for step in range(3):
        pieces = []
        for number in CORNERS:
            start, length = SPANS[number]
            offset = toward(*DIRECTIONS[number])[step]
            pieces.append(sm_ref[offset : offset + 1, start : start + length])
        found.append(positions(wide, jnp.concatenate(pieces, 1)))
    found = jnp.concatenate(found + [jnp.zeros((13, 4 * TZ), F32)], 0).astype(BF)
    edge_p_ref[...] = found
    for number in CORNERS:
        other, length = SPANS[7 - number]
        lists[number] = jnp.concatenate([listed[other : other + length], found], 0)
    pack_sides(lists, 1, (side_ref[0], side_ref[1]), xa_ref, xb_ref, ya_ref, yb_ref)


def forward_kernel(x_ref, lm_ref, w_ref, *refs, width, first):
    g_ref, sum_ref = refs[-2:]
    source = x_ref[...].astype(F32).T.astype(BF)
    offsets = range(first, first + 13)
    weight = jnp.concatenate([w_ref[k] for k in offsets], 0)
    for begin in range(0, ROWS, width):
        cols = slice(begin, begin + width)
        gathered = [dot(source, hot(lm_ref[k : k + 1, cols], ROWS)).astype(BF) for k in offsets]
        gathered = jnp.concatenate(gathered, 0)
        g_ref[:, cols] = gathered
        part = dot(weight, gathered, ((0,), (0,)))
        if first == 0:
            sum_ref[:, cols] = part + dot(w_ref[13], source[:, cols], ((0,), (0,)))
        else:
            sum_ref[cols, :] = (part + refs[0][:, cols]).T


def high_low(values):
    high = values.astype(BF)
    return jnp.concatenate([high, (values - high.astype(F32)).astype(BF)], 1)


def activate_kernel(
    side_ref, pre_ref, ixa_ref, ixb_ref, iya_ref, iyb_ref, rr_ref, cot_ref, pair_ref, w_ref,
    act_ref, grad_ref, xa_ref, xb_ref, ya_ref, yb_ref, dw_ref,
):
    sides = (side_ref[0], side_ref[1])
    arrived = unpack_sides(
        1, sides, CAP + 32, TZ + 16, ixa_ref[...], ixb_ref[...], iya_ref[...], iyb_ref[...]
    )
    sums = [None] * 8
    sources = []
    for number in FACES:
        picked = toward(*DIRECTIONS[number])
        source = arrived[number][:CAP].astype(F32).T.astype(BF)
        sources.append(source)
        gathered = [dot(source, match(row, CAP)).astype(BF) for row in face_rows(arrived[number][CAP:])]
        weight = jnp.concatenate([w_ref[offset] for offset in picked], 0)
        sums[number] = dot(weight, jnp.concatenate(gathered, 0), ((0,), (0,))).T
    edge_source = jnp.concatenate([arrived[n][:TZ] for n in CORNERS], 0).astype(F32).T.astype(BF)
    edge_found = jnp.zeros((16, 4 * TZ), F32)
    for place, number in enumerate(CORNERS):
        rows = arrived[number][TZ:].astype(F32)
        edge_found = jnp.where(inside(place, 1, rows.shape), rows, edge_found)
    gathered = [dot(edge_source, match(edge_found[k : k + 1], 4 * TZ)).astype(BF) for k in range(3)]
    masked = []
    weights = []
    for place, number in enumerate(CORNERS):
        for step in range(3):
            masked.append(jnp.where(inside(place, 1, (C, 4 * TZ)), gathered[step], BF(0)))
            weights.append(w_ref[toward(*DIRECTIONS[number])[step]])
    total = dot(jnp.concatenate(weights, 0), jnp.concatenate(masked, 0), ((0,), (0,))).T
    for place, number in enumerate(CORNERS):
        sums[number] = total[place * TZ : (place + 1) * TZ]

    selector = hot(rr_ref[...], ROWS)
    both = dot(selector, high_low(jnp.concatenate(sums, 0)))
    pre = pre_ref[...] + both[:, :C] + both[:, C:]
    gate = 1.0 / (1.0 + jnp.exp(-pre))
    act_ref[...] = (pre * gate).astype(BF)
    upstream = cot_ref[...].astype(F32) + pair_ref[...].astype(F32)
    grad = upstream * gate * (1.0 + pre * (1.0 - gate))
    grad_ref[...] = grad.astype(BF)
    listed = dot(grad.T.astype(BF), selector).T.astype(BF)
    lists = [listed[start : start + length] for start, length in SPANS]
    pack_sides(lists, -1, sides, xa_ref, xb_ref, ya_ref, yb_ref)

    dw_ref[...] = jnp.zeros_like(dw_ref)
    for source, number in zip(sources, FACES):
        pieces = [
            dot(match(row, CAP), lists[number]).astype(BF) for row in face_rows(arrived[number][CAP:])
        ]
        part = dot(source, jnp.concatenate(pieces, 1))
        for index, offset in enumerate(toward(*DIRECTIONS[number])):
            dw_ref[offset] += part[:, index * C : (index + 1) * C]
    back = jnp.concatenate([lists[n] for n in CORNERS], 0)
    spots = [dot(match(edge_found[k : k + 1], 4 * TZ), back).astype(BF) for k in range(3)]
    pieces = [
        jnp.where(inside(place, 0, (4 * TZ, C)), spots[step], BF(0)) for place in range(4) for step in range(3)
    ]
    part = dot(edge_source, jnp.concatenate(pieces, 1))
    for place, number in enumerate(CORNERS):
        for step in range(3):
            index = 3 * place + step
            dw_ref[toward(*DIRECTIONS[number])[step]] += part[:, index * C : (index + 1) * C]


def weight_first_kernel(g_ref, grad_ref, x_ref, halo_ref, dw_ref):
    grad = grad_ref[...]
    dw_ref[: 13 * C, :] = dot(g_ref[...], grad) + halo_ref[:13].reshape(13 * C, C)
    dw_ref[13 * C :, :] = dot(x_ref[...], grad, ((0,), (0,))) + halo_ref[13]


def weight_second_kernel(side_ref, g_ref, grad_ref, first_ref, halo_ref, kept_ref, sent_ref, total):
    total[: 14 * C, :] = first_ref[...]
    total[14 * C :, :] = dot(g_ref[...], grad_ref[...]) + halo_ref[14:].reshape(13 * C, C)
    half = kept_ref.shape[0]
    kept_ref[...] = total[pl.ds(pl.multiple_of(side_ref[2] * half, 8), half), :]
    sent_ref[...] = total[pl.ds(pl.multiple_of((1 - side_ref[2]) * half, 8), half), :].astype(BF)


def return_kernel(side_ref, ixa_ref, ixb_ref, iya_ref, iyb_ref, face_p_ref, edge_p_ref, w_ref, placed_ref):
    sides = (side_ref[0], side_ref[1])
    returned = unpack_sides(-1, sides, CAP, TZ, ixa_ref[...], ixb_ref[...], iya_ref[...], iyb_ref[...])
    for place, number in enumerate(FACES):
        other, length = SPANS[7 - number]
        pieces = [dot(match(row, CAP), returned[number]).astype(BF) for row in face_rows(face_p_ref[place])]
        weight = jnp.concatenate([w_ref[offset] for offset in toward(*DIRECTIONS[number])], 1)
        placed_ref[other : other + length, :] = dot(jnp.concatenate(pieces, 1), weight, ((1,), (1,)))
    back = jnp.concatenate([returned[n] for n in CORNERS], 0)
    found = edge_p_ref[...].astype(F32)
    spots = [dot(match(found[k : k + 1], 4 * TZ), back).astype(BF) for k in range(3)]
    pieces = []
    weights = []
    for place, number in enumerate(CORNERS):
        for step in range(3):
            pieces.append(jnp.where(inside(place, 0, (4 * TZ, C)), spots[step], BF(0)))
            weights.append(w_ref[toward(*DIRECTIONS[number])[step]])
    result = dot(jnp.concatenate(pieces, 1), jnp.concatenate(weights, 1), ((1,), (1,)))
    for place, number in enumerate(CORNERS):
        other, length = SPANS[7 - number]
        placed_ref[other : other + length, :] = result[place * TZ : (place + 1) * TZ, :]


def backward_kernel(grad_ref, lm_ref, w_ref, out_ref, *, begin):
    size = out_ref.shape[0]
    source = grad_ref[...].astype(F32).T.astype(BF)
    gathered = []
    for k in range(27):
        if k == 13:
            gathered.append(source[:, begin : begin + size])
        else:
            gathered.append(dot(source, hot(lm_ref[26 - k : 27 - k, begin : begin + size], ROWS)).astype(BF))
    weight = jnp.concatenate([w_ref[k] for k in range(27)], 1)
    out_ref[...] = dot(weight, jnp.concatenate(gathered, 0)).T


def final_kernel(*refs):
    placed_ref, rr_ref, act_ref, pair_ref, mixed_ref, out_ref = refs[-6:]
    both = dot(hot(rr_ref[...], ROWS), high_low(placed_ref[...]))
    both = both[:, :C] + both[:, C:]
    size = ROWS // len(refs[:-6])
    for index, ref in enumerate(refs[:-6]):
        rows = slice(index * size, (index + 1) * size)
        out_ref[rows, :] = (ref[...] + both[rows]).astype(BF)
    mixed_ref[...] = (act_ref[...].astype(F32) + pair_ref[...].astype(F32)).astype(BF)


def assemble_kernel(bits_ref, own_ref, one_ref, two_ref, four_ref, out_ref):
    place = bits_ref[0] * 4 + bits_ref[1] * 2 + bits_ref[2]
    blocks = [own_ref[...], one_ref[...]] + [two_ref[i] for i in range(2)] + [four_ref[i] for i in range(4)]
    for distance, block in enumerate(blocks):
        out_ref[place ^ distance] = block.astype(F32)


PARAMS = pltpu.CompilerParams(vmem_limit_bytes=30 * 2**20)


def shape(dims, dtype):
    return jax.ShapeDtypeStruct(dims, dtype)


def whole(dims):
    return pl.BlockSpec(dims, lambda *ids: (0,) * len(dims))


def pairing(axis, which):
    pairs = []
    for tile in range(lax.axis_size("space")):
        at_x, at_y = tile % TILES_X, tile // TILES_X
        tiles_y = lax.axis_size("space") // TILES_X
        if axis == "x":
            move = 1 if (at_x + which) % 2 == 0 else -1
            at_x = (at_x + move) % TILES_X
        else:
            move = 1 if (at_y + which) % 2 == 0 else -1
            at_y = (at_y + move) % tiles_y
        pairs.append((tile, at_y * TILES_X + at_x))
    return pairs


def exchange_x(xa, xb):
    return [lax.ppermute(v, "space", pairing("x", n)) for n, v in enumerate((xa, xb))]


def second_phase(ya, yb, xa, xb, sides, face, edge):
    sent = []
    for which, own in enumerate((ya, yb)):
        down = sides[1] != which
        corners = [jnp.where(down, v[face : face + edge], v[face + edge :]) for v in (xa, xb)]
        sent.append(jnp.concatenate([own] + corners, 0))
    return sent


def exchange_y(sent):
    return [lax.ppermute(v, "space", pairing("y", n)) for n, v in enumerate(sent)]


def swapped(array):
    return lax.ppermute(array, "segment", [(i, i ^ 1) for i in range(lax.axis_size("segment"))])


def xor_send(value, bits):
    return lax.ppermute(value, "space", [(i, i ^ bits) for i in range(lax.axis_size("space"))])


def pick(array, index):
    return lax.dynamic_index_in_dim(array, index, 0, False)


def cost(flops, data):
    return pl.CostEstimate(flops=int(flops), bytes_accessed=int(data), transcendentals=0)


def tie(value, other):
    return lax.optimization_barrier((value, other))[0]


def on_device(features, weights, cotangent, local_map, send_map, recv_map):
    x = features[0]
    w = weights[0]
    cot = cotangent[0]
    lm = local_map.T
    sm = send_map.T
    rr = recv_map.reshape(1, HALO)
    me = lax.axis_index("space")
    sides = jnp.stack([me % 2, me // TILES_X % 2, me % 2]).astype(jnp.int32)
    smem = pl.BlockSpec(memory_space=pltpu.SMEM)
    vmem = pl.BlockSpec(memory_space=pltpu.VMEM)
    def lists_shape(face, edge):
        return [shape((face + 2 * edge, C), BF)] * 2 + [shape((face, C), BF)] * 2

    xa, xb, ya, yb, face_p, edge_p = pl.pallas_call(
        start_kernel,
        in_specs=[smem] + [vmem] * 3,
        out_shape=lists_shape(CAP + 32, TZ + 16) + [shape((4, 32, C), BF), shape((16, C), BF)],
        compiler_params=PARAMS,
        cost_estimate=cost(2e9, 4e6),
        name="start",
    )(sides, x, rr, sm)
    cot_pair = swapped(cot)
    in_x = exchange_x(xa, xb)

    def forward(first, dims, x, *before):
        return pl.pallas_call(
            functools.partial(forward_kernel, width=512, first=first),
            out_shape=[shape((13 * C, ROWS), BF), shape(dims, F32)],
            compiler_params=PARAMS,
            cost_estimate=cost(7e9, 5e6),
            name="forward",
        )(x, lm, w, *before)

    g0, pre = forward(0, (C, ROWS), x)
    in_x = [tie(v, pre) for v in in_x]
    sent = second_phase(ya, yb, *in_x, sides, CAP + 32, TZ + 16)
    in_y = exchange_y(sent)
    g1, pre = forward(14, (ROWS, C), tie(x, sent[0]), pre)
    in_y = [tie(v, pre) for v in in_y]
    act, grad, xa, xb, ya, yb, dw_halo = pl.pallas_call(
        activate_kernel,
        in_specs=[smem] + [vmem] * 9,
        out_shape=[shape((ROWS, C), BF)] * 2 + lists_shape(CAP, TZ) + [shape((27, C, C), F32)],
        compiler_params=PARAMS,
        cost_estimate=cost(4e9, 3e6),
        name="activate",
    )(sides, pre, *in_x, *in_y, rr, cot, cot_pair, w)
    half = 27 * C // 2
    in_x = exchange_x(xa, xb)
    first = pl.pallas_call(
        weight_first_kernel,
        out_shape=shape((14 * C, C), F32),
        compiler_params=PARAMS,
        cost_estimate=cost(4e9, 5e6),
        name="weight_first",
    )(g0, grad, x, dw_halo)
    sent = second_phase(*[tie(v, first) for v in (ya, yb, *in_x)], sides, CAP, TZ)
    in_y = exchange_y(sent)
    kept, sent = pl.pallas_call(
        weight_second_kernel,
        in_specs=[smem] + [vmem] * 4,
        out_shape=[shape((half, C), F32), shape((half, C), BF)],
        scratch_shapes=[pltpu.VMEM((27 * C, C), F32)],
        compiler_params=PARAMS,
        cost_estimate=cost(4e9, 5e6),
        name="weight_second",
    )(sides, g1, tie(grad, tuple(sent)), first, dw_halo)

    size = ROWS // 4

    def backward(index, grad):
        return pl.pallas_call(
            functools.partial(backward_kernel, begin=index * size),
            out_shape=shape((size, C), F32),
            compiler_params=PARAMS,
            cost_estimate=cost(3e9, 2e6),
            name="backward",
        )(grad, lm, w)

    bits = [me % 2, (me // 2 + me // 4) % 2, (me // 8 + me // 16) % 2]

    def halve(blocks, stage):
        return pick(blocks, bits[stage]), pick(blocks, 1 - bits[stage]).astype(BF)

    def plus(one, two):
        return one.astype(F32) + two.astype(F32)

    locals_ = []
    got = xor_send(sent, 1)
    kept, sent = halve(plus(kept, got).reshape(2, 2, -1, C), 1)
    got = xor_send(sent, 2)
    locals_.append(backward(0, tie(grad, sent)))
    placed = pl.pallas_call(
        return_kernel,
        in_specs=[smem] + [vmem] * 7,
        out_shape=shape((HALO, C), F32),
        compiler_params=PARAMS,
        cost_estimate=cost(3e9, 4e6),
        name="returning",
    )(sides, *in_x, *in_y, face_p, edge_p, tie(w, locals_[0]))
    kept, sent = halve(plus(kept, tie(got, placed)), 2)
    got = xor_send(sent, 8)
    locals_.append(backward(1, tie(grad, sent)))
    own = plus(kept, tie(got, locals_[1])).astype(BF)
    got = xor_send(own, 6)
    act_pair = swapped(tie(act, own))
    locals_.append(backward(2, tie(grad, own)))
    own = plus(own, tie(got, locals_[2])).astype(BF)
    got = xor_send(own, 24)
    locals_.append(backward(3, tie(grad, own)))
    own = plus(own, tie(got, locals_[3])).astype(BF)
    one = xor_send(own, 8)
    mixed, input_grad = pl.pallas_call(
        final_kernel,
        out_shape=[shape((ROWS, C), BF), shape((ROWS, C), BF)],
        compiler_params=PARAMS,
        cost_estimate=cost(1e9, 3e6),
        name="final",
    )(*locals_, tie(placed, own), rr, act, act_pair)
    one = tie(one, input_grad)
    two = xor_send(jnp.stack([own, one]), 2)
    four = xor_send(jnp.concatenate([jnp.stack([own, one]), two], 0), 1)
    weight_grad = pl.pallas_call(
        assemble_kernel,
        in_specs=[smem] + [vmem] * 4,
        out_shape=shape((8,) + own.shape, F32),
        compiler_params=PARAMS,
        cost_estimate=cost(1e6, 3e6),
        name="assemble",
    )(jnp.stack(bits).astype(jnp.int32), own, one, two, four)
    return (mixed[None], input_grad[None], weight_grad.reshape(w.shape)[None])


def solution(mesh):
    in_specs = (
        P("segment", "space", None),
        P("segment", None, None, None),
        P("segment", "space", None),
        P("space", None),
        P("space", None),
        P("space"),
    )
    out_specs = (
        P("segment", "space", None),
        P("segment", "space", None),
        P("segment", None, None, None),
    )
    return jax.shard_map(
        on_device, mesh=mesh, in_specs=in_specs, out_specs=out_specs, check_vma=False
    )
```

```python
import functools

import jax
import jax.numpy as jnp
from jax import lax
from jax.experimental import pallas as pl
from jax.experimental.pallas import tpu as pltpu
from jax.sharding import PartitionSpec as P

TZ = 32
TILES_X = 4
CAP = 256
ROWS = 1024
C = 128
HALO = 1152

DIRECTIONS = ((-1, -1), (-1, 0), (-1, 1), (0, -1), (0, 1), (1, -1), (1, 0), (1, 1))
BF = jnp.bfloat16
F32 = jnp.float32


def spans():
    result = []
    start = 0
    for step_x, step_y in DIRECTIONS:
        length = TZ if step_x != 0 and step_y != 0 else CAP
        result.append((start, length))
        start = start + length
    return result


SPANS = spans()
FACES = [n for n, (a, b) in enumerate(DIRECTIONS) if a == 0 or b == 0]
CORNERS = [n for n, (a, b) in enumerate(DIRECTIONS) if a != 0 and b != 0]


def toward(step_x, step_y):
    picked = []
    for offset in range(27):
        along_x = offset // 9 - 1
        along_y = offset // 3 % 3 - 1
        if (step_x == 0 or along_x == -step_x) and (step_y == 0 or along_y == -step_y):
            picked.append(offset)
    return picked


def dot(a, b, dims=((1,), (0,))):
    return lax.dot_general(a, b, (dims, ((), ())), preferred_element_type=F32)


def hot(row, rows):
    pos = lax.broadcasted_iota(jnp.int32, (256, 128), 0).astype(jnp.int16)
    count = row.shape[1]
    blocks = []
    for base in range(0, rows, 256):
        rel = (row - base).astype(jnp.int16)
        parts = [
            jnp.where(rel[:, t : t + 128] == pos, BF(1), BF(0)) for t in range(0, count, 128)
        ]
        blocks.append(jnp.concatenate(parts, 1))
    return jnp.concatenate(blocks, 0)


def spread(column, count):
    kept = jnp.where(column == ROWS, -1, column)
    return jnp.broadcast_to(kept, (column.shape[0], count)).astype(jnp.int16)


def places_from_one(rows):
    return (lax.broadcasted_iota(jnp.int32, (rows, 128), 0) + 1).astype(BF)


def positions(column, row):
    rows, count = column.shape
    numbers = places_from_one(rows)
    numbers = jnp.concatenate([numbers] * (count // 128), 1)
    found = jnp.where(column == row.astype(jnp.int16), numbers, BF(0))
    while rows > 16:
        rows //= 2
        found = jnp.maximum(found[:rows], found[rows:])
    return jnp.max(found.astype(F32), axis=0, keepdims=True)


def match(row, rows):
    numbers = places_from_one(rows)
    row = row.astype(BF)
    parts = [jnp.where(row[:, t : t + 128] == numbers, BF(1), BF(0)) for t in range(0, row.shape[1], 128)]
    return jnp.concatenate(parts, 1)


def face_rows(block):
    block = block.astype(F32)
    return [jnp.concatenate([block[k : k + 1], block[16 + k : 17 + k]], 1) for k in range(9)]


def column_of(row):
    return jnp.broadcast_to(row.astype(F32), (8, row.shape[1])).T[:, :1].astype(jnp.int32)


def inside(place, axis, dims):
    return (lax.broadcasted_iota(jnp.int32, dims, axis) // TZ) == place


def number_of(step_x, step_y):
    return DIRECTIONS.index((step_x, step_y))


def pack_sides(lists, orient, sides, xa_ref, xb_ref, ya_ref, yb_ref):
    x_odd, y_odd = sides[0] == 1, sides[1] == 1

    def x_side(side):
        picked = [(orient * side, 0), (orient * side, -orient), (orient * side, orient)]
        return jnp.concatenate([lists[number_of(*d)] for d in picked], 0)

    plus, minus = x_side(1), x_side(-1)
    xa_ref[...] = jnp.where(x_odd, minus, plus)
    xb_ref[...] = jnp.where(x_odd, plus, minus)
    plus, minus = lists[number_of(0, orient)], lists[number_of(0, -orient)]
    ya_ref[...] = jnp.where(y_odd, minus, plus)
    yb_ref[...] = jnp.where(y_odd, plus, minus)


def unpack_sides(orient, sides, face, edge, xa, xb, ya, yb):
    x_odd, y_odd = sides[0] == 1, sides[1] == 1

    def of_side(side, odd, a, b):
        return jnp.where(odd, b, a) if side == 1 else jnp.where(odd, a, b)

    lists = []
    for step_x, step_y in DIRECTIONS:
        if step_y == 0:
            lists.append(of_side(-orient * step_x, x_odd, xa[:face], xb[:face]))
        elif step_x == 0:
            lists.append(of_side(-orient * step_y, y_odd, ya[:face], yb[:face]))
        else:
            first = of_side(-orient * step_y, y_odd, ya[face : face + edge], yb[face : face + edge])
            second = of_side(-orient * step_y, y_odd, ya[face + edge :], yb[face + edge :])
            lists.append(of_side(-orient * step_x, x_odd, first, second))
    return lists


def start_kernel(side_ref, x_ref, rr_ref, sm_ref, xa_ref, xb_ref, ya_ref, yb_ref, face_p_ref, edge_p_ref):
    lists = [None] * 8
    row = rr_ref[...]
    column = column_of(row)
    listed = dot(x_ref[...].astype(F32).T.astype(BF), hot(row, ROWS)).T.astype(BF)
    for place, number in enumerate(FACES):
        start, length = SPANS[number]
        other, _ = SPANS[7 - number]
        wide = spread(column[other : other + length], length)
        found = [
            positions(wide, sm_ref[offset : offset + 1, start : start + length])
            for offset in toward(*DIRECTIONS[number])
        ]
        found = jnp.concatenate(found + [jnp.zeros((7, length), F32)], 0)
        found = jnp.concatenate([found[:, :128], found[:, 128:]], 0).astype(BF)
        face_p_ref[place] = found
        lists[number] = jnp.concatenate([listed[other : other + length], found], 0)
    wide = spread(
        jnp.concatenate([column[SPANS[7 - n][0] : SPANS[7 - n][0] + TZ] for n in CORNERS], 0), 4 * TZ
    )
    found = []
    for step in range(3):
        pieces = []
        for number in CORNERS:
            start, length = SPANS[number]
            offset = toward(*DIRECTIONS[number])[step]
            pieces.append(sm_ref[offset : offset + 1, start : start + length])
        found.append(positions(wide, jnp.concatenate(pieces, 1)))
    found = jnp.concatenate(found + [jnp.zeros((13, 4 * TZ), F32)], 0).astype(BF)
    edge_p_ref[...] = found
    for number in CORNERS:
        other, length = SPANS[7 - number]
        lists[number] = jnp.concatenate([listed[other : other + length], found], 0)
    pack_sides(lists, 1, (side_ref[0], side_ref[1]), xa_ref, xb_ref, ya_ref, yb_ref)


def forward_kernel(x_ref, lm_ref, w_ref, *refs, width, first):
    g_ref, sum_ref = refs[-2:]
    source = x_ref[...].astype(F32).T.astype(BF)
    offsets = range(first, first + 13)
    weight = jnp.concatenate([w_ref[k] for k in offsets], 0)
    for begin in range(0, ROWS, width):
        cols = slice(begin, begin + width)
        gathered = [dot(source, hot(lm_ref[k : k + 1, cols], ROWS)).astype(BF) for k in offsets]
        gathered = jnp.concatenate(gathered, 0)
        g_ref[:, cols] = gathered
        part = dot(weight, gathered, ((0,), (0,)))
        if first == 0:
            sum_ref[:, cols] = part + dot(w_ref[13], source[:, cols], ((0,), (0,)))
        else:
            sum_ref[cols, :] = (part + refs[0][:, cols]).T


def high_low(values):
    high = values.astype(BF)
    return jnp.concatenate([high, (values - high.astype(F32)).astype(BF)], 1)


def activate_kernel(
    side_ref, pre_ref, ixa_ref, ixb_ref, iya_ref, iyb_ref, rr_ref, cot_ref, pair_ref, w_ref,
    act_ref, grad_ref, xa_ref, xb_ref, ya_ref, yb_ref, dw_ref,
):
    sides = (side_ref[0], side_ref[1])
    arrived = unpack_sides(
        1, sides, CAP + 32, TZ + 16, ixa_ref[...], ixb_ref[...], iya_ref[...], iyb_ref[...]
    )
    sums = [None] * 8
    sources = []
    for number in FACES:
        picked = toward(*DIRECTIONS[number])
        source = arrived[number][:CAP].astype(F32).T.astype(BF)
        sources.append(source)
        gathered = [dot(source, match(row, CAP)).astype(BF) for row in face_rows(arrived[number][CAP:])]
        weight = jnp.concatenate([w_ref[offset] for offset in picked], 0)
        sums[number] = dot(weight, jnp.concatenate(gathered, 0), ((0,), (0,))).T
    edge_source = jnp.concatenate([arrived[n][:TZ] for n in CORNERS], 0).astype(F32).T.astype(BF)
    edge_found = jnp.zeros((16, 4 * TZ), F32)
    for place, number in enumerate(CORNERS):
        rows = arrived[number][TZ:].astype(F32)
        edge_found = jnp.where(inside(place, 1, rows.shape), rows, edge_found)
    gathered = [dot(edge_source, match(edge_found[k : k + 1], 4 * TZ)).astype(BF) for k in range(3)]
    masked = []
    weights = []
    for place, number in enumerate(CORNERS):
        for step in range(3):
            masked.append(jnp.where(inside(place, 1, (C, 4 * TZ)), gathered[step], BF(0)))
            weights.append(w_ref[toward(*DIRECTIONS[number])[step]])
    total = dot(jnp.concatenate(weights, 0), jnp.concatenate(masked, 0), ((0,), (0,))).T
    for place, number in enumerate(CORNERS):
        sums[number] = total[place * TZ : (place + 1) * TZ]

    selector = hot(rr_ref[...], ROWS)
    both = dot(selector, high_low(jnp.concatenate(sums, 0)))
    pre = pre_ref[...] + both[:, :C] + both[:, C:]
    gate = 1.0 / (1.0 + jnp.exp(-pre))
    act_ref[...] = (pre * gate).astype(BF)
    upstream = cot_ref[...].astype(F32) + pair_ref[...].astype(F32)
    grad = upstream * gate * (1.0 + pre * (1.0 - gate))
    grad_ref[...] = grad.astype(BF)
    listed = dot(grad.T.astype(BF), selector).T.astype(BF)
    lists = [listed[start : start + length] for start, length in SPANS]
    pack_sides(lists, -1, sides, xa_ref, xb_ref, ya_ref, yb_ref)

    dw_ref[...] = jnp.zeros_like(dw_ref)
    for source, number in zip(sources, FACES):
        pieces = [
            dot(match(row, CAP), lists[number]).astype(BF) for row in face_rows(arrived[number][CAP:])
        ]
        part = dot(source, jnp.concatenate(pieces, 1))
        for index, offset in enumerate(toward(*DIRECTIONS[number])):
            dw_ref[offset] += part[:, index * C : (index + 1) * C]
    back = jnp.concatenate([lists[n] for n in CORNERS], 0)
    spots = [dot(match(edge_found[k : k + 1], 4 * TZ), back).astype(BF) for k in range(3)]
    pieces = [
        jnp.where(inside(place, 0, (4 * TZ, C)), spots[step], BF(0)) for place in range(4) for step in range(3)
    ]
    part = dot(edge_source, jnp.concatenate(pieces, 1))
    for place, number in enumerate(CORNERS):
        for step in range(3):
            index = 3 * place + step
            dw_ref[toward(*DIRECTIONS[number])[step]] += part[:, index * C : (index + 1) * C]


def weight_first_kernel(g_ref, grad_ref, x_ref, halo_ref, dw_ref):
    grad = grad_ref[...]
    dw_ref[: 13 * C, :] = dot(g_ref[...], grad) + halo_ref[:13].reshape(13 * C, C)
    dw_ref[13 * C :, :] = dot(x_ref[...], grad, ((0,), (0,))) + halo_ref[13]


def weight_second_kernel(side_ref, g_ref, grad_ref, first_ref, halo_ref, kept_ref, sent_ref, total):
    total[: 14 * C, :] = first_ref[...]
    total[14 * C :, :] = dot(g_ref[...], grad_ref[...]) + halo_ref[14:].reshape(13 * C, C)
    half = kept_ref.shape[0]
    kept_ref[...] = total[pl.ds(pl.multiple_of(side_ref[2] * half, 8), half), :]
    sent_ref[...] = total[pl.ds(pl.multiple_of((1 - side_ref[2]) * half, 8), half), :].astype(BF)


def return_kernel(side_ref, ixa_ref, ixb_ref, iya_ref, iyb_ref, face_p_ref, edge_p_ref, w_ref, placed_ref):
    sides = (side_ref[0], side_ref[1])
    returned = unpack_sides(-1, sides, CAP, TZ, ixa_ref[...], ixb_ref[...], iya_ref[...], iyb_ref[...])
    for place, number in enumerate(FACES):
        other, length = SPANS[7 - number]
        pieces = [dot(match(row, CAP), returned[number]).astype(BF) for row in face_rows(face_p_ref[place])]
        weight = jnp.concatenate([w_ref[offset] for offset in toward(*DIRECTIONS[number])], 1)
        placed_ref[other : other + length, :] = dot(jnp.concatenate(pieces, 1), weight, ((1,), (1,)))
    back = jnp.concatenate([returned[n] for n in CORNERS], 0)
    found = edge_p_ref[...].astype(F32)
    spots = [dot(match(found[k : k + 1], 4 * TZ), back).astype(BF) for k in range(3)]
    pieces = []
    weights = []
    for place, number in enumerate(CORNERS):
        for step in range(3):
            pieces.append(jnp.where(inside(place, 0, (4 * TZ, C)), spots[step], BF(0)))
            weights.append(w_ref[toward(*DIRECTIONS[number])[step]])
    result = dot(jnp.concatenate(pieces, 1), jnp.concatenate(weights, 1), ((1,), (1,)))
    for place, number in enumerate(CORNERS):
        other, length = SPANS[7 - number]
        placed_ref[other : other + length, :] = result[place * TZ : (place + 1) * TZ, :]


def backward_kernel(grad_ref, lm_ref, w_ref, out_ref, *, begin):
    size = out_ref.shape[0]
    source = grad_ref[...].astype(F32).T.astype(BF)
    gathered = []
    for k in range(27):
        if k == 13:
            gathered.append(source[:, begin : begin + size])
        else:
            gathered.append(dot(source, hot(lm_ref[26 - k : 27 - k, begin : begin + size], ROWS)).astype(BF))
    weight = jnp.concatenate([w_ref[k] for k in range(27)], 1)
    out_ref[...] = dot(weight, jnp.concatenate(gathered, 0)).T


def final_kernel(*refs):
    placed_ref, rr_ref, act_ref, pair_ref, mixed_ref, out_ref = refs[-6:]
    both = dot(hot(rr_ref[...], ROWS), high_low(placed_ref[...]))
    both = both[:, :C] + both[:, C:]
    size = ROWS // len(refs[:-6])
    for index, ref in enumerate(refs[:-6]):
        rows = slice(index * size, (index + 1) * size)
        out_ref[rows, :] = (ref[...] + both[rows]).astype(BF)
    mixed_ref[...] = (act_ref[...].astype(F32) + pair_ref[...].astype(F32)).astype(BF)


def assemble_kernel(bits_ref, own_ref, one_ref, two_ref, four_ref, out_ref):
    place = bits_ref[0] * 4 + bits_ref[1] * 2 + bits_ref[2]
    blocks = [own_ref[...], one_ref[...]] + [two_ref[i] for i in range(2)] + [four_ref[i] for i in range(4)]
    for distance, block in enumerate(blocks):
        out_ref[place ^ distance] = block.astype(F32)


PARAMS = pltpu.CompilerParams(vmem_limit_bytes=30 * 2**20)


def shape(dims, dtype):
    return jax.ShapeDtypeStruct(dims, dtype)


def whole(dims):
    return pl.BlockSpec(dims, lambda *ids: (0,) * len(dims))


def pairing(axis, which):
    pairs = []
    for tile in range(lax.axis_size("space")):
        at_x, at_y = tile % TILES_X, tile // TILES_X
        tiles_y = lax.axis_size("space") // TILES_X
        if axis == "x":
            move = 1 if (at_x + which) % 2 == 0 else -1
            at_x = (at_x + move) % TILES_X
        else:
            move = 1 if (at_y + which) % 2 == 0 else -1
            at_y = (at_y + move) % tiles_y
        pairs.append((tile, at_y * TILES_X + at_x))
    return pairs


def exchange_x(xa, xb):
    return [lax.ppermute(v, "space", pairing("x", n)) for n, v in enumerate((xa, xb))]


def second_phase(ya, yb, xa, xb, sides, face, edge):
    sent = []
    for which, own in enumerate((ya, yb)):
        down = sides[1] != which
        corners = [jnp.where(down, v[face : face + edge], v[face + edge :]) for v in (xa, xb)]
        sent.append(jnp.concatenate([own] + corners, 0))
    return sent


def exchange_y(sent):
    return [lax.ppermute(v, "space", pairing("y", n)) for n, v in enumerate(sent)]


def swapped(array):
    return lax.ppermute(array, "segment", [(i, i ^ 1) for i in range(lax.axis_size("segment"))])


def xor_send(value, bits):
    return lax.ppermute(value, "space", [(i, i ^ bits) for i in range(lax.axis_size("space"))])


def pick(array, index):
    return lax.dynamic_index_in_dim(array, index, 0, False)


def cost(flops, data):
    return pl.CostEstimate(flops=int(flops), bytes_accessed=int(data), transcendentals=0)


def tie(value, other):
    return lax.optimization_barrier((value, other))[0]


def on_device(features, weights, cotangent, local_map, send_map, recv_map):
    x = features[0]
    w = weights[0]
    cot = cotangent[0]
    lm = local_map.T
    sm = send_map.T
    rr = recv_map.reshape(1, HALO)
    me = lax.axis_index("space")
    sides = jnp.stack([me % 2, me // TILES_X % 2, me % 2]).astype(jnp.int32)
    smem = pl.BlockSpec(memory_space=pltpu.SMEM)
    vmem = pl.BlockSpec(memory_space=pltpu.VMEM)
    def lists_shape(face, edge):
        return [shape((face + 2 * edge, C), BF)] * 2 + [shape((face, C), BF)] * 2

    xa, xb, ya, yb, face_p, edge_p = pl.pallas_call(
        start_kernel,
        in_specs=[smem] + [vmem] * 3,
        out_shape=lists_shape(CAP + 32, TZ + 16) + [shape((4, 32, C), BF), shape((16, C), BF)],
        compiler_params=PARAMS,
        cost_estimate=cost(2e9, 4e6),
        name="start",
    )(sides, x, rr, sm)
    cot_pair = swapped(cot)
    in_x = exchange_x(xa, xb)

    def forward(first, dims, x, *before):
        return pl.pallas_call(
            functools.partial(forward_kernel, width=512, first=first),
            out_shape=[shape((13 * C, ROWS), BF), shape(dims, F32)],
            compiler_params=PARAMS,
            cost_estimate=cost(7e9, 5e6),
            name="forward",
        )(x, lm, w, *before)

    g0, pre = forward(0, (C, ROWS), x)
    in_x = [tie(v, pre) for v in in_x]
    sent = second_phase(ya, yb, *in_x, sides, CAP + 32, TZ + 16)
    in_y = exchange_y(sent)
    g1, pre = forward(14, (ROWS, C), tie(x, sent[0]), pre)
    in_y = [tie(v, pre) for v in in_y]
    act, grad, xa, xb, ya, yb, dw_halo = pl.pallas_call(
        activate_kernel,
        in_specs=[smem] + [vmem] * 9,
        out_shape=[shape((ROWS, C), BF)] * 2 + lists_shape(CAP, TZ) + [shape((27, C, C), F32)],
        compiler_params=PARAMS,
        cost_estimate=cost(4e9, 3e6),
        name="activate",
    )(sides, pre, *in_x, *in_y, rr, cot, cot_pair, w)
    half = 27 * C // 2
    in_x = exchange_x(xa, xb)
    first = pl.pallas_call(
        weight_first_kernel,
        out_shape=shape((14 * C, C), F32),
        compiler_params=PARAMS,
        cost_estimate=cost(4e9, 5e6),
        name="weight_first",
    )(g0, grad, x, dw_halo)
    kept, sent = pl.pallas_call(
        weight_second_kernel,
        in_specs=[smem] + [vmem] * 4,
        out_shape=[shape((half, C), F32), shape((half, C), BF)],
        scratch_shapes=[pltpu.VMEM((27 * C, C), F32)],
        compiler_params=PARAMS,
        cost_estimate=cost(4e9, 5e6),
        name="weight_second",
    )(sides, g1, grad, first, dw_halo)

    size = ROWS // 4

    def backward(index, grad):
        return pl.pallas_call(
            functools.partial(backward_kernel, begin=index * size),
            out_shape=shape((size, C), F32),
            compiler_params=PARAMS,
            cost_estimate=cost(3e9, 2e6),
            name="backward",
        )(grad, lm, w)

    bits = [me % 2, (me // 2 + me // 4) % 2, (me // 8 + me // 16) % 2]

    def halve(blocks, stage):
        return pick(blocks, bits[stage]), pick(blocks, 1 - bits[stage]).astype(BF)

    def plus(one, two):
        return one.astype(F32) + two.astype(F32)

    locals_ = []
    got = xor_send(sent, 1)
    kept, sent = halve(plus(kept, got).reshape(2, 2, -1, C), 1)
    sent, in_x = lax.optimization_barrier((sent, in_x))
    got = xor_send(sent, 2)
    locals_.append(backward(0, tie(grad, sent)))
    locals_.append(backward(1, tie(grad, locals_[0])))
    kept, sent = halve(plus(kept, tie(got, locals_[1])), 2)
    got = xor_send(sent, 8)
    in_y = exchange_y(second_phase(*[tie(v, sent) for v in (ya, yb, *in_x)], sides, CAP, TZ))
    own = plus(kept, got).astype(BF)
    got = xor_send(own, 6)
    act_pair = swapped(tie(act, own))
    locals_.append(backward(2, tie(grad, own)))
    own = plus(own, tie(got, locals_[2])).astype(BF)
    got = xor_send(own, 24)
    placed = pl.pallas_call(
        return_kernel,
        in_specs=[smem] + [vmem] * 7,
        out_shape=shape((HALO, C), F32),
        compiler_params=PARAMS,
        cost_estimate=cost(3e9, 4e6),
        name="returning",
    )(sides, *in_x, *in_y, face_p, edge_p, tie(w, own))
    own = plus(own, tie(got, placed)).astype(BF)
    one = xor_send(own, 8)
    locals_.append(backward(3, tie(grad, own)))
    one = tie(one, locals_[3])
    two = xor_send(jnp.stack([own, one]), 2)
    mixed, input_grad = pl.pallas_call(
        final_kernel,
        out_shape=[shape((ROWS, C), BF), shape((ROWS, C), BF)],
        compiler_params=PARAMS,
        cost_estimate=cost(1e9, 3e6),
        name="final",
    )(*locals_, tie(placed, one), rr, act, act_pair)
    two = tie(two, input_grad)
    four = xor_send(jnp.concatenate([jnp.stack([own, one]), two], 0), 1)
    weight_grad = pl.pallas_call(
        assemble_kernel,
        in_specs=[smem] + [vmem] * 4,
        out_shape=shape((8,) + own.shape, F32),
        compiler_params=PARAMS,
        cost_estimate=cost(1e6, 3e6),
        name="assemble",
    )(jnp.stack(bits).astype(jnp.int32), own, one, two, four)
    return (mixed[None], input_grad[None], weight_grad.reshape(w.shape)[None])


def solution(mesh):
    in_specs = (
        P("segment", "space", None),
        P("segment", None, None, None),
        P("segment", "space", None),
        P("space", None),
        P("space", None),
        P("space"),
    )
    out_specs = (
        P("segment", "space", None),
        P("segment", "space", None),
        P("segment", None, None, None),
    )
    return jax.shard_map(
        on_device, mesh=mesh, in_specs=in_specs, out_specs=out_specs, check_vma=False
    )
```

```python
import functools

import jax
import jax.numpy as jnp
from jax import lax
from jax.experimental import pallas as pl
from jax.experimental.pallas import tpu as pltpu
from jax.sharding import PartitionSpec as P

TZ = 32
TILES_X = 4
CAP = 256
ROWS = 1024
C = 128
HALO = 1152

DIRECTIONS = ((-1, -1), (-1, 0), (-1, 1), (0, -1), (0, 1), (1, -1), (1, 0), (1, 1))
BF = jnp.bfloat16
F32 = jnp.float32


def spans():
    result = []
    start = 0
    for step_x, step_y in DIRECTIONS:
        length = TZ if step_x != 0 and step_y != 0 else CAP
        result.append((start, length))
        start = start + length
    return result


SPANS = spans()
FACES = [n for n, (a, b) in enumerate(DIRECTIONS) if a == 0 or b == 0]
CORNERS = [n for n, (a, b) in enumerate(DIRECTIONS) if a != 0 and b != 0]


def toward(step_x, step_y):
    picked = []
    for offset in range(27):
        along_x = offset // 9 - 1
        along_y = offset // 3 % 3 - 1
        if (step_x == 0 or along_x == -step_x) and (step_y == 0 or along_y == -step_y):
            picked.append(offset)
    return picked


def dot(a, b, dims=((1,), (0,))):
    return lax.dot_general(a, b, (dims, ((), ())), preferred_element_type=F32)


def hot(row, rows):
    pos = lax.broadcasted_iota(jnp.int32, (256, 128), 0).astype(jnp.int16)
    count = row.shape[1]
    blocks = []
    for base in range(0, rows, 256):
        rel = (row - base).astype(jnp.int16)
        parts = [
            jnp.where(rel[:, t : t + 128] == pos, BF(1), BF(0)) for t in range(0, count, 128)
        ]
        blocks.append(jnp.concatenate(parts, 1))
    return jnp.concatenate(blocks, 0)


def spread(column, count):
    kept = jnp.where(column == ROWS, -1, column)
    return jnp.broadcast_to(kept, (column.shape[0], count)).astype(jnp.int16)


def places_from_one(rows):
    return (lax.broadcasted_iota(jnp.int32, (rows, 128), 0) + 1).astype(BF)


def positions(column, row):
    rows, count = column.shape
    numbers = places_from_one(rows)
    numbers = jnp.concatenate([numbers] * (count // 128), 1)
    found = jnp.where(column == row.astype(jnp.int16), numbers, BF(0))
    while rows > 16:
        rows //= 2
        found = jnp.maximum(found[:rows], found[rows:])
    return jnp.max(found.astype(F32), axis=0, keepdims=True)


def match(row, rows):
    numbers = places_from_one(rows)
    row = row.astype(BF)
    parts = [jnp.where(row[:, t : t + 128] == numbers, BF(1), BF(0)) for t in range(0, row.shape[1], 128)]
    return jnp.concatenate(parts, 1)


def face_rows(block):
    block = block.astype(F32)
    return [jnp.concatenate([block[k : k + 1], block[16 + k : 17 + k]], 1) for k in range(9)]


def column_of(row):
    return jnp.broadcast_to(row.astype(F32), (8, row.shape[1])).T[:, :1].astype(jnp.int32)


def inside(place, axis, dims):
    return (lax.broadcasted_iota(jnp.int32, dims, axis) // TZ) == place


def number_of(step_x, step_y):
    return DIRECTIONS.index((step_x, step_y))


def pack_sides(lists, orient, sides, xa_ref, xb_ref, ya_ref, yb_ref):
    x_odd, y_odd = sides[0] == 1, sides[1] == 1

    def x_side(side):
        picked = [(orient * side, 0), (orient * side, -orient), (orient * side, orient)]
        return jnp.concatenate([lists[number_of(*d)] for d in picked], 0)

    plus, minus = x_side(1), x_side(-1)
    xa_ref[...] = jnp.where(x_odd, minus, plus)
    xb_ref[...] = jnp.where(x_odd, plus, minus)
    plus, minus = lists[number_of(0, orient)], lists[number_of(0, -orient)]
    ya_ref[...] = jnp.where(y_odd, minus, plus)
    yb_ref[...] = jnp.where(y_odd, plus, minus)


def unpack_sides(orient, sides, face, edge, xa, xb, ya, yb):
    x_odd, y_odd = sides[0] == 1, sides[1] == 1

    def of_side(side, odd, a, b):
        return jnp.where(odd, b, a) if side == 1 else jnp.where(odd, a, b)

    lists = []
    for step_x, step_y in DIRECTIONS:
        if step_y == 0:
            lists.append(of_side(-orient * step_x, x_odd, xa[:face], xb[:face]))
        elif step_x == 0:
            lists.append(of_side(-orient * step_y, y_odd, ya[:face], yb[:face]))
        else:
            first = of_side(-orient * step_y, y_odd, ya[face : face + edge], yb[face : face + edge])
            second = of_side(-orient * step_y, y_odd, ya[face + edge :], yb[face + edge :])
            lists.append(of_side(-orient * step_x, x_odd, first, second))
    return lists


def start_kernel(side_ref, x_ref, rr_ref, sm_ref, xa_ref, xb_ref, ya_ref, yb_ref, face_p_ref, edge_p_ref):
    lists = [None] * 8
    row = rr_ref[...].reshape(1, HALO)
    column = column_of(row)
    listed = dot(x_ref[...].astype(F32).T.astype(BF), hot(row, ROWS)).T.astype(BF)
    for place, number in enumerate(FACES):
        start, length = SPANS[number]
        other, _ = SPANS[7 - number]
        wide = spread(column[other : other + length], length)
        found = [
            positions(wide, sm_ref[offset : offset + 1, start : start + length])
            for offset in toward(*DIRECTIONS[number])
        ]
        found = jnp.concatenate(found + [jnp.zeros((7, length), F32)], 0)
        found = jnp.concatenate([found[:, :128], found[:, 128:]], 0).astype(BF)
        face_p_ref[place] = found
        lists[number] = jnp.concatenate([listed[other : other + length], found], 0)
    wide = spread(
        jnp.concatenate([column[SPANS[7 - n][0] : SPANS[7 - n][0] + TZ] for n in CORNERS], 0), 4 * TZ
    )
    found = []
    for step in range(3):
        pieces = []
        for number in CORNERS:
            start, length = SPANS[number]
            offset = toward(*DIRECTIONS[number])[step]
            pieces.append(sm_ref[offset : offset + 1, start : start + length])
        found.append(positions(wide, jnp.concatenate(pieces, 1)))
    found = jnp.concatenate(found + [jnp.zeros((13, 4 * TZ), F32)], 0).astype(BF)
    edge_p_ref[...] = found
    for number in CORNERS:
        other, length = SPANS[7 - number]
        lists[number] = jnp.concatenate([listed[other : other + length], found], 0)
    pack_sides(lists, 1, (side_ref[0], side_ref[1]), xa_ref, xb_ref, ya_ref, yb_ref)


def forward_kernel(x_ref, lm_ref, w_ref, *refs, width, first):
    g_ref, sum_ref = refs[-2:]
    source = x_ref[...].astype(F32).T.astype(BF)
    offsets = range(first, first + 13)
    weight = jnp.concatenate([w_ref[k] for k in offsets], 0)
    for begin in range(0, ROWS, width):
        cols = slice(begin, begin + width)
        gathered = [dot(source, hot(lm_ref[k : k + 1, cols], ROWS)).astype(BF) for k in offsets]
        gathered = jnp.concatenate(gathered, 0)
        g_ref[:, cols] = gathered
        part = dot(weight, gathered, ((0,), (0,)))
        if first == 0:
            sum_ref[:, cols] = part + dot(w_ref[13], source[:, cols], ((0,), (0,)))
        else:
            sum_ref[cols, :] = (part + refs[0][:, cols]).T


def high_low(values):
    high = values.astype(BF)
    return jnp.concatenate([high, (values - high.astype(F32)).astype(BF)], 1)


def activate_kernel(
    side_ref, pre_ref, ixa_ref, ixb_ref, iya_ref, iyb_ref, rr_ref, cot_ref, pair_ref, w_ref,
    act_ref, grad_ref, xa_ref, xb_ref, ya_ref, yb_ref, dw_ref,
):
    sides = (side_ref[0], side_ref[1])
    arrived = unpack_sides(
        1, sides, CAP + 32, TZ + 16, ixa_ref[...], ixb_ref[...], iya_ref[...], iyb_ref[...]
    )
    sums = [None] * 8
    sources = []
    for number in FACES:
        picked = toward(*DIRECTIONS[number])
        source = arrived[number][:CAP].astype(F32).T.astype(BF)
        sources.append(source)
        gathered = [dot(source, match(row, CAP)).astype(BF) for row in face_rows(arrived[number][CAP:])]
        weight = jnp.concatenate([w_ref[offset] for offset in picked], 0)
        sums[number] = dot(weight, jnp.concatenate(gathered, 0), ((0,), (0,))).T
    edge_source = jnp.concatenate([arrived[n][:TZ] for n in CORNERS], 0).astype(F32).T.astype(BF)
    edge_found = jnp.zeros((16, 4 * TZ), F32)
    for place, number in enumerate(CORNERS):
        rows = arrived[number][TZ:].astype(F32)
        edge_found = jnp.where(inside(place, 1, rows.shape), rows, edge_found)
    gathered = [dot(edge_source, match(edge_found[k : k + 1], 4 * TZ)).astype(BF) for k in range(3)]
    masked = []
    weights = []
    for place, number in enumerate(CORNERS):
        for step in range(3):
            masked.append(jnp.where(inside(place, 1, (C, 4 * TZ)), gathered[step], BF(0)))
            weights.append(w_ref[toward(*DIRECTIONS[number])[step]])
    total = dot(jnp.concatenate(weights, 0), jnp.concatenate(masked, 0), ((0,), (0,))).T
    for place, number in enumerate(CORNERS):
        sums[number] = total[place * TZ : (place + 1) * TZ]

    selector = hot(rr_ref[...].reshape(1, HALO), ROWS)
    both = dot(selector, high_low(jnp.concatenate(sums, 0)))
    pre = pre_ref[...] + both[:, :C] + both[:, C:]
    gate = 1.0 / (1.0 + jnp.exp(-pre))
    act_ref[...] = (pre * gate).astype(BF)
    upstream = cot_ref[...].astype(F32) + pair_ref[...].astype(F32)
    grad = upstream * gate * (1.0 + pre * (1.0 - gate))
    grad_ref[...] = grad.astype(BF)
    listed = dot(grad.T.astype(BF), selector).T.astype(BF)
    lists = [listed[start : start + length] for start, length in SPANS]
    pack_sides(lists, -1, sides, xa_ref, xb_ref, ya_ref, yb_ref)

    dw_ref[...] = jnp.zeros_like(dw_ref)
    for source, number in zip(sources, FACES):
        pieces = [
            dot(match(row, CAP), lists[number]).astype(BF) for row in face_rows(arrived[number][CAP:])
        ]
        part = dot(source, jnp.concatenate(pieces, 1))
        for index, offset in enumerate(toward(*DIRECTIONS[number])):
            dw_ref[offset] += part[:, index * C : (index + 1) * C]
    back = jnp.concatenate([lists[n] for n in CORNERS], 0)
    spots = [dot(match(edge_found[k : k + 1], 4 * TZ), back).astype(BF) for k in range(3)]
    pieces = [
        jnp.where(inside(place, 0, (4 * TZ, C)), spots[step], BF(0)) for place in range(4) for step in range(3)
    ]
    part = dot(edge_source, jnp.concatenate(pieces, 1))
    for place, number in enumerate(CORNERS):
        for step in range(3):
            index = 3 * place + step
            dw_ref[toward(*DIRECTIONS[number])[step]] += part[:, index * C : (index + 1) * C]


def weight_first_kernel(g_ref, grad_ref, x_ref, halo_ref, dw_ref):
    grad = grad_ref[...]
    dw_ref[: 13 * C, :] = dot(g_ref[...], grad) + halo_ref[:13].reshape(13 * C, C)
    dw_ref[13 * C :, :] = dot(x_ref[...], grad, ((0,), (0,))) + halo_ref[13]


def weight_second_kernel(side_ref, g_ref, grad_ref, first_ref, halo_ref, kept_ref, sent_ref, total):
    total[: 14 * C, :] = first_ref[...]
    total[14 * C :, :] = dot(g_ref[...], grad_ref[...]) + halo_ref[14:].reshape(13 * C, C)
    half = kept_ref.shape[0]
    kept_ref[...] = total[pl.ds(pl.multiple_of(side_ref[2] * half, 8), half), :]
    sent_ref[...] = total[pl.ds(pl.multiple_of((1 - side_ref[2]) * half, 8), half), :].astype(BF)


def return_kernel(side_ref, ixa_ref, ixb_ref, iya_ref, iyb_ref, face_p_ref, edge_p_ref, w_ref, placed_ref):
    sides = (side_ref[0], side_ref[1])
    returned = unpack_sides(-1, sides, CAP, TZ, ixa_ref[...], ixb_ref[...], iya_ref[...], iyb_ref[...])
    for place, number in enumerate(FACES):
        other, length = SPANS[7 - number]
        pieces = [dot(match(row, CAP), returned[number]).astype(BF) for row in face_rows(face_p_ref[place])]
        weight = jnp.concatenate([w_ref[offset] for offset in toward(*DIRECTIONS[number])], 1)
        placed_ref[other : other + length, :] = dot(jnp.concatenate(pieces, 1), weight, ((1,), (1,)))
    back = jnp.concatenate([returned[n] for n in CORNERS], 0)
    found = edge_p_ref[...].astype(F32)
    spots = [dot(match(found[k : k + 1], 4 * TZ), back).astype(BF) for k in range(3)]
    pieces = []
    weights = []
    for place, number in enumerate(CORNERS):
        for step in range(3):
            pieces.append(jnp.where(inside(place, 0, (4 * TZ, C)), spots[step], BF(0)))
            weights.append(w_ref[toward(*DIRECTIONS[number])[step]])
    result = dot(jnp.concatenate(pieces, 1), jnp.concatenate(weights, 1), ((1,), (1,)))
    for place, number in enumerate(CORNERS):
        other, length = SPANS[7 - number]
        placed_ref[other : other + length, :] = result[place * TZ : (place + 1) * TZ, :]


def backward_kernel(grad_ref, lm_ref, w_ref, out_ref, *, begin):
    size = out_ref.shape[0]
    source = grad_ref[...].astype(F32).T.astype(BF)
    gathered = []
    for k in range(27):
        if k == 13:
            gathered.append(source[:, begin : begin + size])
        else:
            gathered.append(dot(source, hot(lm_ref[26 - k : 27 - k, begin : begin + size], ROWS)).astype(BF))
    weight = jnp.concatenate([w_ref[k] for k in range(27)], 1)
    out_ref[...] = dot(weight, jnp.concatenate(gathered, 0)).T


def final_kernel(*refs):
    placed_ref, rr_ref, act_ref, pair_ref, mixed_ref, out_ref = refs[-6:]
    both = dot(hot(rr_ref[...].reshape(1, HALO), ROWS), high_low(placed_ref[...]))
    both = both[:, :C] + both[:, C:]
    size = ROWS // len(refs[:-6])
    for index, ref in enumerate(refs[:-6]):
        rows = slice(index * size, (index + 1) * size)
        out_ref[rows, :] = (ref[...] + both[rows]).astype(BF)
    mixed_ref[...] = (act_ref[...].astype(F32) + pair_ref[...].astype(F32)).astype(BF)


def assemble_kernel(bits_ref, low_ref, high_ref, *refs, distances):
    out_ref, held, sems = refs[-3:]
    place = bits_ref[0] * 4 + bits_ref[1] * 2 + bits_ref[2]
    copies = []
    for index, distance in enumerate(distances):
        held[index] = (low_ref if index < 2 else high_ref)[index % 2].astype(F32)
        copies.append(pltpu.make_async_copy(held.at[index], out_ref.at[place ^ distance], sems.at[index]))
        copies[-1].start()
    for copy in copies:
        copy.wait()


PARAMS = pltpu.CompilerParams(vmem_limit_bytes=30 * 2**20)


def shape(dims, dtype):
    return jax.ShapeDtypeStruct(dims, dtype)


def whole(dims):
    return pl.BlockSpec(dims, lambda *ids: (0,) * len(dims))


def pairing(axis, which):
    pairs = []
    for tile in range(lax.axis_size("space")):
        at_x, at_y = tile % TILES_X, tile // TILES_X
        tiles_y = lax.axis_size("space") // TILES_X
        if axis == "x":
            move = 1 if (at_x + which) % 2 == 0 else -1
            at_x = (at_x + move) % TILES_X
        else:
            move = 1 if (at_y + which) % 2 == 0 else -1
            at_y = (at_y + move) % tiles_y
        pairs.append((tile, at_y * TILES_X + at_x))
    return pairs


def exchange_x(xa, xb):
    return [lax.ppermute(v, "space", pairing("x", n)) for n, v in enumerate((xa, xb))]


def second_phase(ya, yb, xa, xb, sides, face, edge):
    sent = []
    for which, own in enumerate((ya, yb)):
        down = sides[1] != which
        corners = [jnp.where(down, v[face : face + edge], v[face + edge :]) for v in (xa, xb)]
        sent.append(jnp.concatenate([own] + corners, 0))
    return sent


def exchange_y(sent):
    return [lax.ppermute(v, "space", pairing("y", n)) for n, v in enumerate(sent)]


def swapped(array):
    return lax.ppermute(array, "segment", [(i, i ^ 1) for i in range(lax.axis_size("segment"))])


def xor_send(value, bits):
    return lax.ppermute(value, "space", [(i, i ^ bits) for i in range(lax.axis_size("space"))])


def pick(array, index):
    return lax.dynamic_index_in_dim(array, index, 0, False)


def cost(flops, data):
    return pl.CostEstimate(flops=int(flops), bytes_accessed=int(data), transcendentals=0)


def tie(value, other):
    return lax.optimization_barrier((value, other))[0]


def on_device(features, weights, cotangent, local_map, send_map, recv_map):
    x = features[0]
    w = weights[0]
    cot = cotangent[0]
    lm = local_map.T
    sm = send_map.T
    rr = recv_map
    me = lax.axis_index("space")
    sides = jnp.stack([me % 2, me // TILES_X % 2, me % 2]).astype(jnp.int32)
    smem = pl.BlockSpec(memory_space=pltpu.SMEM)
    vmem = pl.BlockSpec(memory_space=pltpu.VMEM)
    def lists_shape(face, edge):
        return [shape((face + 2 * edge, C), BF)] * 2 + [shape((face, C), BF)] * 2

    xa, xb, ya, yb, face_p, edge_p = pl.pallas_call(
        start_kernel,
        in_specs=[smem] + [vmem] * 3,
        out_shape=lists_shape(CAP + 32, TZ + 16) + [shape((4, 32, C), BF), shape((16, C), BF)],
        compiler_params=PARAMS,
        cost_estimate=cost(2e9, 4e6),
        name="start",
    )(sides, x, rr, sm)
    cot_pair = swapped(cot)
    in_x = exchange_x(xa, xb)

    def forward(first, dims, x, *before):
        return pl.pallas_call(
            functools.partial(forward_kernel, width=512, first=first),
            out_shape=[shape((13 * C, ROWS), BF), shape(dims, F32)],
            compiler_params=PARAMS,
            cost_estimate=cost(7e9, 5e6),
            name="forward",
        )(x, lm, w, *before)

    g0, pre = forward(0, (C, ROWS), x)
    in_x = [tie(v, pre) for v in in_x]
    sent = second_phase(ya, yb, *in_x, sides, CAP + 32, TZ + 16)
    in_y = exchange_y(sent)
    g1, pre = forward(14, (ROWS, C), tie(x, sent[0]), pre)
    in_y = [tie(v, pre) for v in in_y]
    act, grad, xa, xb, ya, yb, dw_halo = pl.pallas_call(
        activate_kernel,
        in_specs=[smem] + [vmem] * 9,
        out_shape=[shape((ROWS, C), BF)] * 2 + lists_shape(CAP, TZ) + [shape((27, C, C), F32)],
        compiler_params=PARAMS,
        cost_estimate=cost(4e9, 3e6),
        name="activate",
    )(sides, pre, *in_x, *in_y, rr, cot, cot_pair, w)
    half = 27 * C // 2
    in_x = exchange_x(xa, xb)
    first = pl.pallas_call(
        weight_first_kernel,
        out_shape=shape((14 * C, C), F32),
        compiler_params=PARAMS,
        cost_estimate=cost(4e9, 5e6),
        name="weight_first",
    )(g0, grad, x, dw_halo)
    kept, sent = pl.pallas_call(
        weight_second_kernel,
        in_specs=[smem] + [vmem] * 4,
        out_shape=[shape((half, C), F32), shape((half, C), BF)],
        scratch_shapes=[pltpu.VMEM((27 * C, C), F32)],
        compiler_params=PARAMS,
        cost_estimate=cost(4e9, 5e6),
        name="weight_second",
    )(sides, g1, grad, first, dw_halo)

    size = ROWS // 4

    def backward(index, grad):
        return pl.pallas_call(
            functools.partial(backward_kernel, begin=index * size),
            out_shape=shape((size, C), F32),
            compiler_params=PARAMS,
            cost_estimate=cost(3e9, 2e6),
            name="backward",
        )(grad, lm, w)

    bits = [me % 2, (me // 2 + me // 4) % 2, (me // 8 + me // 16) % 2]

    def halve(blocks, stage):
        return pick(blocks, bits[stage]), pick(blocks, 1 - bits[stage]).astype(BF)

    def plus(one, two):
        return one.astype(F32) + two.astype(F32)

    locals_ = []
    got = xor_send(sent, 1)
    kept, sent = halve(plus(kept, got).reshape(2, 2, -1, C), 1)
    sent, in_x = lax.optimization_barrier((sent, in_x))
    got = xor_send(sent, 2)
    locals_.append(backward(0, tie(grad, sent)))
    locals_.append(backward(1, tie(grad, locals_[0])))
    kept, sent = halve(plus(kept, tie(got, locals_[1])), 2)
    got = xor_send(sent, 8)
    in_y = exchange_y(second_phase(*[tie(v, sent) for v in (ya, yb, *in_x)], sides, CAP, TZ))
    own = plus(kept, got).astype(BF)
    got = xor_send(own, 6)
    act_pair = swapped(tie(act, own))
    locals_.append(backward(2, tie(grad, own)))
    own = plus(own, tie(got, locals_[2])).astype(BF)
    got = xor_send(own, 24)
    placed = pl.pallas_call(
        return_kernel,
        in_specs=[smem] + [vmem] * 7,
        out_shape=shape((HALO, C), F32),
        compiler_params=PARAMS,
        cost_estimate=cost(3e9, 4e6),
        name="returning",
    )(sides, *in_x, *in_y, face_p, edge_p, tie(w, own))
    own = plus(own, tie(got, placed)).astype(BF)
    one = xor_send(own, 8)
    locals_.append(backward(3, tie(grad, own)))
    one = tie(one, locals_[3])
    pair = jnp.stack([own, one])
    two = xor_send(pair, 2)
    cross = xor_send(pair, 1)
    mixed, input_grad = pl.pallas_call(
        final_kernel,
        out_shape=[shape((ROWS, C), BF), shape((ROWS, C), BF)],
        compiler_params=PARAMS,
        cost_estimate=cost(1e9, 3e6),
        name="final",
    )(*locals_, tie(placed, one), rr, act, act_pair)

    def assemble(low, high, distances, *before):
        hbm = pl.BlockSpec(memory_space=pltpu.HBM)
        return pl.pallas_call(
            functools.partial(assemble_kernel, distances=distances),
            in_specs=[smem, vmem, vmem] + [hbm] * len(before),
            out_specs=hbm,
            out_shape=shape((8,) + own.shape, F32),
            input_output_aliases={3: 0} if before else {},
            scratch_shapes=[pltpu.VMEM((4,) + own.shape, F32), pltpu.SemaphoreType.DMA((4,))],
            compiler_params=PARAMS,
            cost_estimate=cost(1e6, 3e6),
            name="assemble",
        )(jnp.stack(bits).astype(jnp.int32), low, high, *before)

    near = assemble(pair, cross, (0, 1, 4, 5))
    two = tie(two, (input_grad, near))
    far = xor_send(two, 1)
    weight_grad = assemble(two, far, (2, 3, 6, 7), near)
    weight_grad = weight_grad.reshape(w.shape)
    return (mixed[None], input_grad[None], weight_grad[None])


def solution(mesh):
    in_specs = (
        P("segment", "space", None),
        P("segment", None, None, None),
        P("segment", "space", None),
        P("space", None),
        P("space", None),
        P("space"),
    )
    out_specs = (
        P("segment", "space", None),
        P("segment", "space", None),
        P("segment", None, None, None),
    )
    return jax.shard_map(
        on_device, mesh=mesh, in_specs=in_specs, out_specs=out_specs, check_vma=False
    )
```

```python
import functools

import jax
import jax.numpy as jnp
from jax import lax
from jax.experimental import pallas as pl
from jax.experimental.pallas import tpu as pltpu
from jax.sharding import PartitionSpec as P

TZ = 32
TILES_X = 4
CAP = 256
ROWS = 1024
C = 128
HALO = 1152

DIRECTIONS = ((-1, -1), (-1, 0), (-1, 1), (0, -1), (0, 1), (1, -1), (1, 0), (1, 1))
BF = jnp.bfloat16
F32 = jnp.float32


def spans():
    result = []
    start = 0
    for step_x, step_y in DIRECTIONS:
        length = TZ if step_x != 0 and step_y != 0 else CAP
        result.append((start, length))
        start = start + length
    return result


SPANS = spans()
FACES = [n for n, (a, b) in enumerate(DIRECTIONS) if a == 0 or b == 0]
CORNERS = [n for n, (a, b) in enumerate(DIRECTIONS) if a != 0 and b != 0]


def toward(step_x, step_y):
    picked = []
    for offset in range(27):
        along_x = offset // 9 - 1
        along_y = offset // 3 % 3 - 1
        if (step_x == 0 or along_x == -step_x) and (step_y == 0 or along_y == -step_y):
            picked.append(offset)
    return picked


def dot(a, b, dims=((1,), (0,))):
    return lax.dot_general(a, b, (dims, ((), ())), preferred_element_type=F32)


def hot(row, rows):
    pos = lax.broadcasted_iota(jnp.int32, (256, 128), 0).astype(jnp.int16)
    count = row.shape[1]
    blocks = []
    for base in range(0, rows, 256):
        rel = (row - base).astype(jnp.int16)
        parts = [
            jnp.where(rel[:, t : t + 128] == pos, BF(1), BF(0)) for t in range(0, count, 128)
        ]
        blocks.append(jnp.concatenate(parts, 1))
    return jnp.concatenate(blocks, 0)


def spread(column, count):
    kept = jnp.where(column == ROWS, -1, column)
    return jnp.broadcast_to(kept, (column.shape[0], count)).astype(jnp.int16)


def places_from_one(rows):
    return (lax.broadcasted_iota(jnp.int32, (rows, 128), 0) + 1).astype(BF)


def positions(column, row):
    rows, count = column.shape
    numbers = places_from_one(rows)
    numbers = jnp.concatenate([numbers] * (count // 128), 1)
    found = jnp.where(column == row.astype(jnp.int16), numbers, BF(0))
    while rows > 16:
        rows //= 2
        found = jnp.maximum(found[:rows], found[rows:])
    return jnp.max(found.astype(F32), axis=0, keepdims=True)


def match(row, rows):
    numbers = places_from_one(rows)
    row = row.astype(BF)
    parts = [jnp.where(row[:, t : t + 128] == numbers, BF(1), BF(0)) for t in range(0, row.shape[1], 128)]
    return jnp.concatenate(parts, 1)


def face_rows(block):
    block = block.astype(F32)
    return [jnp.concatenate([block[k : k + 1], block[16 + k : 17 + k]], 1) for k in range(9)]


def column_of(row):
    return jnp.broadcast_to(row.astype(F32), (8, row.shape[1])).T[:, :1].astype(jnp.int32)


def inside(place, axis, dims):
    return (lax.broadcasted_iota(jnp.int32, dims, axis) // TZ) == place


def number_of(step_x, step_y):
    return DIRECTIONS.index((step_x, step_y))


def pack_sides(lists, orient, sides, xa_ref, xb_ref, ya_ref, yb_ref):
    x_odd, y_odd = sides[0] == 1, sides[1] == 1

    def x_side(side):
        picked = [(orient * side, 0), (orient * side, -orient), (orient * side, orient)]
        return jnp.concatenate([lists[number_of(*d)] for d in picked], 0)

    plus, minus = x_side(1), x_side(-1)
    xa_ref[...] = jnp.where(x_odd, minus, plus)
    xb_ref[...] = jnp.where(x_odd, plus, minus)
    plus, minus = lists[number_of(0, orient)], lists[number_of(0, -orient)]
    ya_ref[...] = jnp.where(y_odd, minus, plus)
    yb_ref[...] = jnp.where(y_odd, plus, minus)


def unpack_sides(orient, sides, face, edge, xa, xb, ya, yb):
    x_odd, y_odd = sides[0] == 1, sides[1] == 1

    def of_side(side, odd, a, b):
        return jnp.where(odd, b, a) if side == 1 else jnp.where(odd, a, b)

    lists = []
    for step_x, step_y in DIRECTIONS:
        if step_y == 0:
            lists.append(of_side(-orient * step_x, x_odd, xa[:face], xb[:face]))
        elif step_x == 0:
            lists.append(of_side(-orient * step_y, y_odd, ya[:face], yb[:face]))
        else:
            first = of_side(-orient * step_y, y_odd, ya[face : face + edge], yb[face : face + edge])
            second = of_side(-orient * step_y, y_odd, ya[face + edge :], yb[face + edge :])
            lists.append(of_side(-orient * step_x, x_odd, first, second))
    return lists


def start_kernel(side_ref, x_ref, rr_ref, sm_ref, xa_ref, xb_ref, ya_ref, yb_ref, face_p_ref, edge_p_ref):
    lists = [None] * 8
    row = rr_ref[...]
    column = column_of(row)
    listed = dot(x_ref[...].astype(F32).T.astype(BF), hot(row, ROWS)).T.astype(BF)
    for place, number in enumerate(FACES):
        start, length = SPANS[number]
        other, _ = SPANS[7 - number]
        wide = spread(column[other : other + length], length)
        found = [
            positions(wide, sm_ref[offset : offset + 1, start : start + length])
            for offset in toward(*DIRECTIONS[number])
        ]
        found = jnp.concatenate(found + [jnp.zeros((7, length), F32)], 0)
        found = jnp.concatenate([found[:, :128], found[:, 128:]], 0).astype(BF)
        face_p_ref[place] = found
        lists[number] = jnp.concatenate([listed[other : other + length], found], 0)
    wide = spread(
        jnp.concatenate([column[SPANS[7 - n][0] : SPANS[7 - n][0] + TZ] for n in CORNERS], 0), 4 * TZ
    )
    found = []
    for step in range(3):
        pieces = []
        for number in CORNERS:
            start, length = SPANS[number]
            offset = toward(*DIRECTIONS[number])[step]
            pieces.append(sm_ref[offset : offset + 1, start : start + length])
        found.append(positions(wide, jnp.concatenate(pieces, 1)))
    found = jnp.concatenate(found + [jnp.zeros((13, 4 * TZ), F32)], 0).astype(BF)
    edge_p_ref[...] = found
    for number in CORNERS:
        other, length = SPANS[7 - number]
        lists[number] = jnp.concatenate([listed[other : other + length], found], 0)
    pack_sides(lists, 1, (side_ref[0], side_ref[1]), xa_ref, xb_ref, ya_ref, yb_ref)


def forward_kernel(x_ref, lm_ref, w_ref, *refs, width, first):
    g_ref, sum_ref = refs[-2:]
    source = x_ref[...].astype(F32).T.astype(BF)
    offsets = range(first, first + 13)
    weight = jnp.concatenate([w_ref[k] for k in offsets], 0)
    for begin in range(0, ROWS, width):
        cols = slice(begin, begin + width)
        gathered = [dot(source, hot(lm_ref[k : k + 1, cols], ROWS)).astype(BF) for k in offsets]
        gathered = jnp.concatenate(gathered, 0)
        g_ref[:, cols] = gathered
        part = dot(weight, gathered, ((0,), (0,)))
        if first == 0:
            sum_ref[:, cols] = part + dot(w_ref[13], source[:, cols], ((0,), (0,)))
        else:
            sum_ref[cols, :] = (part + refs[0][:, cols]).T


def high_low(values):
    high = values.astype(BF)
    return jnp.concatenate([high, (values - high.astype(F32)).astype(BF)], 1)


def activate_kernel(
    side_ref, pre_ref, ixa_ref, ixb_ref, iya_ref, iyb_ref, rr_ref, cot_ref, pair_ref, w_ref,
    act_ref, grad_ref, xa_ref, xb_ref, ya_ref, yb_ref, dw_ref,
):
    sides = (side_ref[0], side_ref[1])
    arrived = unpack_sides(
        1, sides, CAP + 32, TZ + 16, ixa_ref[...], ixb_ref[...], iya_ref[...], iyb_ref[...]
    )
    sums = [None] * 8
    sources = []
    for number in FACES:
        picked = toward(*DIRECTIONS[number])
        source = arrived[number][:CAP].astype(F32).T.astype(BF)
        sources.append(source)
        gathered = [dot(source, match(row, CAP)).astype(BF) for row in face_rows(arrived[number][CAP:])]
        weight = jnp.concatenate([w_ref[offset] for offset in picked], 0)
        sums[number] = dot(weight, jnp.concatenate(gathered, 0), ((0,), (0,))).T
    edge_source = jnp.concatenate([arrived[n][:TZ] for n in CORNERS], 0).astype(F32).T.astype(BF)
    edge_found = jnp.zeros((16, 4 * TZ), F32)
    for place, number in enumerate(CORNERS):
        rows = arrived[number][TZ:].astype(F32)
        edge_found = jnp.where(inside(place, 1, rows.shape), rows, edge_found)
    gathered = [dot(edge_source, match(edge_found[k : k + 1], 4 * TZ)).astype(BF) for k in range(3)]
    masked = []
    weights = []
    for place, number in enumerate(CORNERS):
        for step in range(3):
            masked.append(jnp.where(inside(place, 1, (C, 4 * TZ)), gathered[step], BF(0)))
            weights.append(w_ref[toward(*DIRECTIONS[number])[step]])
    total = dot(jnp.concatenate(weights, 0), jnp.concatenate(masked, 0), ((0,), (0,))).T
    for place, number in enumerate(CORNERS):
        sums[number] = total[place * TZ : (place + 1) * TZ]

    selector = hot(rr_ref[...], ROWS)
    both = dot(selector, high_low(jnp.concatenate(sums, 0)))
    pre = pre_ref[...] + both[:, :C] + both[:, C:]
    gate = 1.0 / (1.0 + jnp.exp(-pre))
    act_ref[...] = (pre * gate).astype(BF)
    upstream = cot_ref[...].astype(F32) + pair_ref[...].astype(F32)
    grad = upstream * gate * (1.0 + pre * (1.0 - gate))
    grad_ref[...] = grad.astype(BF)
    listed = dot(grad.T.astype(BF), selector).T.astype(BF)
    lists = [listed[start : start + length] for start, length in SPANS]
    pack_sides(lists, -1, sides, xa_ref, xb_ref, ya_ref, yb_ref)

    dw_ref[...] = jnp.zeros_like(dw_ref)
    for source, number in zip(sources, FACES):
        pieces = [
            dot(match(row, CAP), lists[number]).astype(BF) for row in face_rows(arrived[number][CAP:])
        ]
        part = dot(source, jnp.concatenate(pieces, 1))
        for index, offset in enumerate(toward(*DIRECTIONS[number])):
            dw_ref[offset] += part[:, index * C : (index + 1) * C]
    back = jnp.concatenate([lists[n] for n in CORNERS], 0)
    spots = [dot(match(edge_found[k : k + 1], 4 * TZ), back).astype(BF) for k in range(3)]
    pieces = [
        jnp.where(inside(place, 0, (4 * TZ, C)), spots[step], BF(0)) for place in range(4) for step in range(3)
    ]
    part = dot(edge_source, jnp.concatenate(pieces, 1))
    for place, number in enumerate(CORNERS):
        for step in range(3):
            index = 3 * place + step
            dw_ref[toward(*DIRECTIONS[number])[step]] += part[:, index * C : (index + 1) * C]


def weight_first_kernel(g_ref, grad_ref, x_ref, halo_ref, dw_ref):
    grad = grad_ref[...]
    dw_ref[: 13 * C, :] = dot(g_ref[...], grad) + halo_ref[:13].reshape(13 * C, C)
    dw_ref[13 * C :, :] = dot(x_ref[...], grad, ((0,), (0,))) + halo_ref[13]


def weight_second_kernel(side_ref, g_ref, grad_ref, first_ref, halo_ref, kept_ref, sent_ref, total):
    total[: 14 * C, :] = first_ref[...]
    total[14 * C :, :] = dot(g_ref[...], grad_ref[...]) + halo_ref[14:].reshape(13 * C, C)
    half = kept_ref.shape[0]
    kept_ref[...] = total[pl.ds(pl.multiple_of(side_ref[2] * half, 8), half), :]
    sent_ref[...] = total[pl.ds(pl.multiple_of((1 - side_ref[2]) * half, 8), half), :].astype(BF)


def return_kernel(side_ref, ixa_ref, ixb_ref, iya_ref, iyb_ref, face_p_ref, edge_p_ref, w_ref, placed_ref):
    sides = (side_ref[0], side_ref[1])
    returned = unpack_sides(-1, sides, CAP, TZ, ixa_ref[...], ixb_ref[...], iya_ref[...], iyb_ref[...])
    for place, number in enumerate(FACES):
        other, length = SPANS[7 - number]
        pieces = [dot(match(row, CAP), returned[number]).astype(BF) for row in face_rows(face_p_ref[place])]
        weight = jnp.concatenate([w_ref[offset] for offset in toward(*DIRECTIONS[number])], 1)
        placed_ref[other : other + length, :] = dot(jnp.concatenate(pieces, 1), weight, ((1,), (1,)))
    back = jnp.concatenate([returned[n] for n in CORNERS], 0)
    found = edge_p_ref[...].astype(F32)
    spots = [dot(match(found[k : k + 1], 4 * TZ), back).astype(BF) for k in range(3)]
    pieces = []
    weights = []
    for place, number in enumerate(CORNERS):
        for step in range(3):
            pieces.append(jnp.where(inside(place, 0, (4 * TZ, C)), spots[step], BF(0)))
            weights.append(w_ref[toward(*DIRECTIONS[number])[step]])
    result = dot(jnp.concatenate(pieces, 1), jnp.concatenate(weights, 1), ((1,), (1,)))
    for place, number in enumerate(CORNERS):
        other, length = SPANS[7 - number]
        placed_ref[other : other + length, :] = result[place * TZ : (place + 1) * TZ, :]


def backward_kernel(grad_ref, lm_ref, w_ref, out_ref, *, begin):
    size = out_ref.shape[0]
    source = grad_ref[...].astype(F32).T.astype(BF)
    gathered = []
    for k in range(27):
        if k == 13:
            gathered.append(source[:, begin : begin + size])
        else:
            gathered.append(dot(source, hot(lm_ref[26 - k : 27 - k, begin : begin + size], ROWS)).astype(BF))
    weight = jnp.concatenate([w_ref[k] for k in range(27)], 1)
    out_ref[...] = dot(weight, jnp.concatenate(gathered, 0)).T


def final_kernel(*refs):
    placed_ref, rr_ref, act_ref, pair_ref, mixed_ref, out_ref = refs[-6:]
    both = dot(hot(rr_ref[...], ROWS), high_low(placed_ref[...]))
    both = both[:, :C] + both[:, C:]
    size = ROWS // len(refs[:-6])
    for index, ref in enumerate(refs[:-6]):
        rows = slice(index * size, (index + 1) * size)
        out_ref[rows, :] = (ref[...] + both[rows]).astype(BF)
    mixed_ref[...] = (act_ref[...].astype(F32) + pair_ref[...].astype(F32)).astype(BF)


def assemble_kernel(bits_ref, own_ref, one_ref, two_ref, four_ref, out_ref):
    place = bits_ref[0] * 4 + bits_ref[1] * 2 + bits_ref[2]
    blocks = [own_ref[...], one_ref[...]] + [two_ref[i] for i in range(2)] + [four_ref[i] for i in range(4)]
    for distance, block in enumerate(blocks):
        out_ref[place ^ distance] = block.astype(F32)


PARAMS = pltpu.CompilerParams(vmem_limit_bytes=30 * 2**20)


def shape(dims, dtype):
    return jax.ShapeDtypeStruct(dims, dtype)


def whole(dims):
    return pl.BlockSpec(dims, lambda *ids: (0,) * len(dims))


def pairing(axis, which):
    pairs = []
    for tile in range(lax.axis_size("space")):
        at_x, at_y = tile % TILES_X, tile // TILES_X
        tiles_y = lax.axis_size("space") // TILES_X
        if axis == "x":
            move = 1 if (at_x + which) % 2 == 0 else -1
            at_x = (at_x + move) % TILES_X
        else:
            move = 1 if (at_y + which) % 2 == 0 else -1
            at_y = (at_y + move) % tiles_y
        pairs.append((tile, at_y * TILES_X + at_x))
    return pairs


def exchange_x(xa, xb):
    return [lax.ppermute(v, "space", pairing("x", n)) for n, v in enumerate((xa, xb))]


def second_phase(ya, yb, xa, xb, sides, face, edge):
    sent = []
    for which, own in enumerate((ya, yb)):
        down = sides[1] != which
        corners = [jnp.where(down, v[face : face + edge], v[face + edge :]) for v in (xa, xb)]
        sent.append(jnp.concatenate([own] + corners, 0))
    return sent


def exchange_y(sent):
    return [lax.ppermute(v, "space", pairing("y", n)) for n, v in enumerate(sent)]


def swapped(array):
    return lax.ppermute(array, "segment", [(i, i ^ 1) for i in range(lax.axis_size("segment"))])


def xor_send(value, bits):
    return lax.ppermute(value, "space", [(i, i ^ bits) for i in range(lax.axis_size("space"))])


def pick(array, index):
    return lax.dynamic_index_in_dim(array, index, 0, False)


def cost(flops, data):
    return pl.CostEstimate(flops=int(flops), bytes_accessed=int(data), transcendentals=0)


def tie(value, other):
    return lax.optimization_barrier((value, other))[0]


def on_device(features, weights, cotangent, local_map, send_map, recv_map):
    x = features[0]
    w = weights[0]
    cot = cotangent[0]
    lm = local_map.T
    sm = send_map.T
    rr = recv_map.reshape(1, HALO)
    me = lax.axis_index("space")
    sides = jnp.stack([me % 2, me // TILES_X % 2, me % 2]).astype(jnp.int32)
    smem = pl.BlockSpec(memory_space=pltpu.SMEM)
    vmem = pl.BlockSpec(memory_space=pltpu.VMEM)
    def lists_shape(face, edge):
        return [shape((face + 2 * edge, C), BF)] * 2 + [shape((face, C), BF)] * 2

    xa, xb, ya, yb, face_p, edge_p = pl.pallas_call(
        start_kernel,
        in_specs=[smem] + [vmem] * 3,
        out_shape=lists_shape(CAP + 32, TZ + 16) + [shape((4, 32, C), BF), shape((16, C), BF)],
        compiler_params=PARAMS,
        cost_estimate=cost(2e9, 4e6),
        name="start",
    )(sides, x, rr, sm)
    cot_pair = swapped(cot)
    in_x = exchange_x(xa, xb)

    def forward(first, dims, x, *before):
        return pl.pallas_call(
            functools.partial(forward_kernel, width=512, first=first),
            out_shape=[shape((13 * C, ROWS), BF), shape(dims, F32)],
            compiler_params=PARAMS,
            cost_estimate=cost(7e9, 5e6),
            name="forward",
        )(x, lm, w, *before)

    g0, pre = forward(0, (C, ROWS), x)
    in_x = [tie(v, pre) for v in in_x]
    sent = second_phase(ya, yb, *in_x, sides, CAP + 32, TZ + 16)
    in_y = exchange_y(sent)
    g1, pre = forward(14, (ROWS, C), tie(x, sent[0]), pre)
    in_y = [tie(v, pre) for v in in_y]
    act, grad, xa, xb, ya, yb, dw_halo = pl.pallas_call(
        activate_kernel,
        in_specs=[smem] + [vmem] * 9,
        out_shape=[shape((ROWS, C), BF)] * 2 + lists_shape(CAP, TZ) + [shape((27, C, C), F32)],
        compiler_params=PARAMS,
        cost_estimate=cost(4e9, 3e6),
        name="activate",
    )(sides, pre, *in_x, *in_y, rr, cot, cot_pair, w)
    half = 27 * C // 2
    first = pl.pallas_call(
        weight_first_kernel,
        out_shape=shape((14 * C, C), F32),
        compiler_params=PARAMS,
        cost_estimate=cost(4e9, 5e6),
        name="weight_first",
    )(g0, grad, x, dw_halo)
    kept, sent = pl.pallas_call(
        weight_second_kernel,
        in_specs=[smem] + [vmem] * 4,
        out_shape=[shape((half, C), F32), shape((half, C), BF)],
        scratch_shapes=[pltpu.VMEM((27 * C, C), F32)],
        compiler_params=PARAMS,
        cost_estimate=cost(4e9, 5e6),
        name="weight_second",
    )(sides, g1, grad, first, dw_halo)

    size = ROWS // 4

    def backward(index, grad):
        return pl.pallas_call(
            functools.partial(backward_kernel, begin=index * size),
            out_shape=shape((size, C), F32),
            compiler_params=PARAMS,
            cost_estimate=cost(3e9, 2e6),
            name="backward",
        )(grad, lm, w)

    bits = [me % 2, (me // 2 + me // 4) % 2, (me // 8 + me // 16) % 2]

    def halve(blocks, stage):
        return pick(blocks, bits[stage]), pick(blocks, 1 - bits[stage]).astype(BF)

    def plus(one, two):
        return one.astype(F32) + two.astype(F32)

    locals_ = []
    got = xor_send(sent, 1)
    kept, sent = halve(plus(kept, got).reshape(2, 2, -1, C), 1)
    got = xor_send(sent, 2)
    act_pair = swapped(tie(act, sent))
    locals_.append(backward(0, tie(grad, sent)))
    locals_.append(backward(1, tie(grad, locals_[0])))
    kept, sent = halve(plus(kept, tie(got, locals_[1])), 2)
    got = xor_send(sent, 8)
    in_x = exchange_x(tie(xa, sent), tie(xb, sent))
    own = plus(kept, got).astype(BF)
    got = xor_send(own, 6)
    in_y = exchange_y(second_phase(*[tie(v, own) for v in (ya, yb, *in_x)], sides, CAP, TZ))
    locals_.append(backward(2, tie(grad, own)))
    own = plus(own, tie(got, locals_[2])).astype(BF)
    got = xor_send(own, 24)
    placed = pl.pallas_call(
        return_kernel,
        in_specs=[smem] + [vmem] * 7,
        out_shape=shape((HALO, C), F32),
        compiler_params=PARAMS,
        cost_estimate=cost(3e9, 4e6),
        name="returning",
    )(sides, *in_x, *in_y, face_p, edge_p, tie(w, own))
    own = plus(own, tie(got, placed)).astype(BF)
    one = xor_send(own, 8)
    locals_.append(backward(3, tie(grad, own)))
    one = tie(one, locals_[3])
    two = xor_send(jnp.stack([own, one]), 2)
    mixed, input_grad = pl.pallas_call(
        final_kernel,
        out_shape=[shape((ROWS, C), BF), shape((ROWS, C), BF)],
        compiler_params=PARAMS,
        cost_estimate=cost(1e9, 3e6),
        name="final",
    )(*locals_, tie(placed, one), rr, act, act_pair)
    two = tie(two, input_grad)
    four = xor_send(jnp.concatenate([jnp.stack([own, one]), two], 0), 1)
    weight_grad = pl.pallas_call(
        assemble_kernel,
        in_specs=[smem] + [vmem] * 4,
        out_shape=shape((8,) + own.shape, F32),
        compiler_params=PARAMS,
        cost_estimate=cost(1e6, 3e6),
        name="assemble",
    )(jnp.stack(bits).astype(jnp.int32), own, one, two, four)
    return (mixed[None], input_grad[None], weight_grad.reshape(w.shape)[None])


def solution(mesh):
    in_specs = (
        P("segment", "space", None),
        P("segment", None, None, None),
        P("segment", "space", None),
        P("space", None),
        P("space", None),
        P("space"),
    )
    out_specs = (
        P("segment", "space", None),
        P("segment", "space", None),
        P("segment", None, None, None),
    )
    return jax.shard_map(
        on_device, mesh=mesh, in_specs=in_specs, out_specs=out_specs, check_vma=False
    )
```

```python
import functools

import jax
import jax.numpy as jnp
from jax import lax
from jax.experimental import pallas as pl
from jax.experimental.pallas import tpu as pltpu
from jax.sharding import PartitionSpec as P

TZ = 32
TILES_X = 4
CAP = 256
ROWS = 1024
C = 128
HALO = 1152

DIRECTIONS = ((-1, -1), (-1, 0), (-1, 1), (0, -1), (0, 1), (1, -1), (1, 0), (1, 1))
BF = jnp.bfloat16
F32 = jnp.float32


def spans():
    result = []
    start = 0
    for step_x, step_y in DIRECTIONS:
        length = TZ if step_x != 0 and step_y != 0 else CAP
        result.append((start, length))
        start = start + length
    return result


SPANS = spans()
FACES = [n for n, (a, b) in enumerate(DIRECTIONS) if a == 0 or b == 0]
CORNERS = [n for n, (a, b) in enumerate(DIRECTIONS) if a != 0 and b != 0]


def toward(step_x, step_y):
    picked = []
    for offset in range(27):
        along_x = offset // 9 - 1
        along_y = offset // 3 % 3 - 1
        if (step_x == 0 or along_x == -step_x) and (step_y == 0 or along_y == -step_y):
            picked.append(offset)
    return picked


def dot(a, b, dims=((1,), (0,))):
    return lax.dot_general(a, b, (dims, ((), ())), preferred_element_type=F32)


def hot(row, rows):
    pos = lax.broadcasted_iota(jnp.int32, (256, 128), 0).astype(jnp.int16)
    count = row.shape[1]
    blocks = []
    for base in range(0, rows, 256):
        rel = (row - base).astype(jnp.int16)
        parts = [
            jnp.where(rel[:, t : t + 128] == pos, BF(1), BF(0)) for t in range(0, count, 128)
        ]
        blocks.append(jnp.concatenate(parts, 1))
    return jnp.concatenate(blocks, 0)


def spread(column, count):
    kept = jnp.where(column == ROWS, -1, column)
    return jnp.broadcast_to(kept, (column.shape[0], count)).astype(jnp.int16)


def places_from_one(rows):
    return (lax.broadcasted_iota(jnp.int32, (rows, 128), 0) + 1).astype(BF)


def positions(column, row):
    rows, count = column.shape
    numbers = places_from_one(rows)
    numbers = jnp.concatenate([numbers] * (count // 128), 1)
    found = jnp.where(column == row.astype(jnp.int16), numbers, BF(0))
    while rows > 16:
        rows //= 2
        found = jnp.maximum(found[:rows], found[rows:])
    return jnp.max(found.astype(F32), axis=0, keepdims=True)


def match(row, rows):
    numbers = places_from_one(rows)
    row = row.astype(BF)
    parts = [jnp.where(row[:, t : t + 128] == numbers, BF(1), BF(0)) for t in range(0, row.shape[1], 128)]
    return jnp.concatenate(parts, 1)


def face_rows(block):
    block = block.astype(F32)
    return [jnp.concatenate([block[k : k + 1], block[16 + k : 17 + k]], 1) for k in range(9)]


def column_of(row):
    return jnp.broadcast_to(row.astype(F32), (8, row.shape[1])).T[:, :1].astype(jnp.int32)


def inside(place, axis, dims):
    return (lax.broadcasted_iota(jnp.int32, dims, axis) // TZ) == place


def number_of(step_x, step_y):
    return DIRECTIONS.index((step_x, step_y))


def pack_sides(lists, orient, sides, xa_ref, xb_ref, ya_ref, yb_ref):
    x_odd, y_odd = sides[0] == 1, sides[1] == 1

    def x_side(side):
        picked = [(orient * side, 0), (orient * side, -orient), (orient * side, orient)]
        return jnp.concatenate([lists[number_of(*d)] for d in picked], 0)

    plus, minus = x_side(1), x_side(-1)
    xa_ref[...] = jnp.where(x_odd, minus, plus)
    xb_ref[...] = jnp.where(x_odd, plus, minus)
    plus, minus = lists[number_of(0, orient)], lists[number_of(0, -orient)]
    ya_ref[...] = jnp.where(y_odd, minus, plus)
    yb_ref[...] = jnp.where(y_odd, plus, minus)


def unpack_sides(orient, sides, face, edge, xa, xb, ya, yb):
    x_odd, y_odd = sides[0] == 1, sides[1] == 1

    def of_side(side, odd, a, b):
        return jnp.where(odd, b, a) if side == 1 else jnp.where(odd, a, b)

    lists = []
    for step_x, step_y in DIRECTIONS:
        if step_y == 0:
            lists.append(of_side(-orient * step_x, x_odd, xa[:face], xb[:face]))
        elif step_x == 0:
            lists.append(of_side(-orient * step_y, y_odd, ya[:face], yb[:face]))
        else:
            first = of_side(-orient * step_y, y_odd, ya[face : face + edge], yb[face : face + edge])
            second = of_side(-orient * step_y, y_odd, ya[face + edge :], yb[face + edge :])
            lists.append(of_side(-orient * step_x, x_odd, first, second))
    return lists


def start_kernel(side_ref, x_ref, rr_ref, sm_ref, xa_ref, xb_ref, ya_ref, yb_ref, face_p_ref, edge_p_ref):
    lists = [None] * 8
    row = rr_ref[...]
    column = column_of(row)
    listed = dot(x_ref[...].astype(F32).T.astype(BF), hot(row, ROWS)).T.astype(BF)
    for place, number in enumerate(FACES):
        start, length = SPANS[number]
        other, _ = SPANS[7 - number]
        wide = spread(column[other : other + length], length)
        found = [
            positions(wide, sm_ref[offset : offset + 1, start : start + length])
            for offset in toward(*DIRECTIONS[number])
        ]
        found = jnp.concatenate(found + [jnp.zeros((7, length), F32)], 0)
        found = jnp.concatenate([found[:, :128], found[:, 128:]], 0).astype(BF)
        face_p_ref[place] = found
        lists[number] = jnp.concatenate([listed[other : other + length], found], 0)
    wide = spread(
        jnp.concatenate([column[SPANS[7 - n][0] : SPANS[7 - n][0] + TZ] for n in CORNERS], 0), 4 * TZ
    )
    found = []
    for step in range(3):
        pieces = []
        for number in CORNERS:
            start, length = SPANS[number]
            offset = toward(*DIRECTIONS[number])[step]
            pieces.append(sm_ref[offset : offset + 1, start : start + length])
        found.append(positions(wide, jnp.concatenate(pieces, 1)))
    found = jnp.concatenate(found + [jnp.zeros((13, 4 * TZ), F32)], 0).astype(BF)
    edge_p_ref[...] = found
    for number in CORNERS:
        other, length = SPANS[7 - number]
        lists[number] = jnp.concatenate([listed[other : other + length], found], 0)
    pack_sides(lists, 1, (side_ref[0], side_ref[1]), xa_ref, xb_ref, ya_ref, yb_ref)


def forward_kernel(x_ref, lm_ref, w_ref, *refs, width, first):
    g_ref, sum_ref = refs[-2:]
    source = x_ref[...].astype(F32).T.astype(BF)
    offsets = range(first, first + 13)
    weight = jnp.concatenate([w_ref[k] for k in offsets], 0)
    for begin in range(0, ROWS, width):
        cols = slice(begin, begin + width)
        gathered = [dot(source, hot(lm_ref[k : k + 1, cols], ROWS)).astype(BF) for k in offsets]
        gathered = jnp.concatenate(gathered, 0)
        g_ref[:, cols] = gathered
        part = dot(weight, gathered, ((0,), (0,)))
        if first == 0:
            sum_ref[:, cols] = part + dot(w_ref[13], source[:, cols], ((0,), (0,)))
        else:
            sum_ref[cols, :] = (part + refs[0][:, cols]).T


def high_low(values):
    high = values.astype(BF)
    return jnp.concatenate([high, (values - high.astype(F32)).astype(BF)], 1)


def activate_kernel(
    side_ref, pre_ref, ixa_ref, ixb_ref, iya_ref, iyb_ref, rr_ref, cot_ref, pair_ref, w_ref,
    act_ref, grad_ref, xa_ref, xb_ref, ya_ref, yb_ref, dw_ref,
):
    sides = (side_ref[0], side_ref[1])
    arrived = unpack_sides(
        1, sides, CAP + 32, TZ + 16, ixa_ref[...], ixb_ref[...], iya_ref[...], iyb_ref[...]
    )
    sums = [None] * 8
    sources = []
    for number in FACES:
        picked = toward(*DIRECTIONS[number])
        source = arrived[number][:CAP].astype(F32).T.astype(BF)
        sources.append(source)
        gathered = [dot(source, match(row, CAP)).astype(BF) for row in face_rows(arrived[number][CAP:])]
        weight = jnp.concatenate([w_ref[offset] for offset in picked], 0)
        sums[number] = dot(weight, jnp.concatenate(gathered, 0), ((0,), (0,))).T
    edge_source = jnp.concatenate([arrived[n][:TZ] for n in CORNERS], 0).astype(F32).T.astype(BF)
    edge_found = jnp.zeros((16, 4 * TZ), F32)
    for place, number in enumerate(CORNERS):
        rows = arrived[number][TZ:].astype(F32)
        edge_found = jnp.where(inside(place, 1, rows.shape), rows, edge_found)
    gathered = [dot(edge_source, match(edge_found[k : k + 1], 4 * TZ)).astype(BF) for k in range(3)]
    masked = []
    weights = []
    for place, number in enumerate(CORNERS):
        for step in range(3):
            masked.append(jnp.where(inside(place, 1, (C, 4 * TZ)), gathered[step], BF(0)))
            weights.append(w_ref[toward(*DIRECTIONS[number])[step]])
    total = dot(jnp.concatenate(weights, 0), jnp.concatenate(masked, 0), ((0,), (0,))).T
    for place, number in enumerate(CORNERS):
        sums[number] = total[place * TZ : (place + 1) * TZ]

    selector = hot(rr_ref[...], ROWS)
    both = dot(selector, high_low(jnp.concatenate(sums, 0)))
    pre = pre_ref[...] + both[:, :C] + both[:, C:]
    gate = 1.0 / (1.0 + jnp.exp(-pre))
    act_ref[...] = (pre * gate).astype(BF)
    upstream = cot_ref[...].astype(F32) + pair_ref[...].astype(F32)
    grad = upstream * gate * (1.0 + pre * (1.0 - gate))
    grad_ref[...] = grad.astype(BF)
    listed = dot(grad.T.astype(BF), selector).T.astype(BF)
    lists = [listed[start : start + length] for start, length in SPANS]
    pack_sides(lists, -1, sides, xa_ref, xb_ref, ya_ref, yb_ref)

    dw_ref[...] = jnp.zeros_like(dw_ref)
    for source, number in zip(sources, FACES):
        pieces = [
            dot(match(row, CAP), lists[number]).astype(BF) for row in face_rows(arrived[number][CAP:])
        ]
        part = dot(source, jnp.concatenate(pieces, 1))
        for index, offset in enumerate(toward(*DIRECTIONS[number])):
            dw_ref[offset] += part[:, index * C : (index + 1) * C]
    back = jnp.concatenate([lists[n] for n in CORNERS], 0)
    spots = [dot(match(edge_found[k : k + 1], 4 * TZ), back).astype(BF) for k in range(3)]
    pieces = [
        jnp.where(inside(place, 0, (4 * TZ, C)), spots[step], BF(0)) for place in range(4) for step in range(3)
    ]
    part = dot(edge_source, jnp.concatenate(pieces, 1))
    for place, number in enumerate(CORNERS):
        for step in range(3):
            index = 3 * place + step
            dw_ref[toward(*DIRECTIONS[number])[step]] += part[:, index * C : (index + 1) * C]


def weight_first_kernel(g_ref, grad_ref, x_ref, halo_ref, dw_ref):
    grad = grad_ref[...]
    dw_ref[: 13 * C, :] = dot(g_ref[...], grad) + halo_ref[:13].reshape(13 * C, C)
    dw_ref[13 * C :, :] = dot(x_ref[...], grad, ((0,), (0,))) + halo_ref[13]


def weight_second_kernel(side_ref, g_ref, grad_ref, first_ref, halo_ref, kept_ref, sent_ref, total):
    total[: 14 * C, :] = first_ref[...]
    total[14 * C :, :] = dot(g_ref[...], grad_ref[...]) + halo_ref[14:].reshape(13 * C, C)
    half = kept_ref.shape[0]
    kept_ref[...] = total[pl.ds(pl.multiple_of(side_ref[2] * half, 8), half), :]
    sent_ref[...] = total[pl.ds(pl.multiple_of((1 - side_ref[2]) * half, 8), half), :].astype(BF)


def return_kernel(side_ref, ixa_ref, ixb_ref, iya_ref, iyb_ref, face_p_ref, edge_p_ref, w_ref, placed_ref):
    sides = (side_ref[0], side_ref[1])
    returned = unpack_sides(-1, sides, CAP, TZ, ixa_ref[...], ixb_ref[...], iya_ref[...], iyb_ref[...])
    for place, number in enumerate(FACES):
        other, length = SPANS[7 - number]
        pieces = [dot(match(row, CAP), returned[number]).astype(BF) for row in face_rows(face_p_ref[place])]
        weight = jnp.concatenate([w_ref[offset] for offset in toward(*DIRECTIONS[number])], 1)
        placed_ref[other : other + length, :] = dot(jnp.concatenate(pieces, 1), weight, ((1,), (1,)))
    back = jnp.concatenate([returned[n] for n in CORNERS], 0)
    found = edge_p_ref[...].astype(F32)
    spots = [dot(match(found[k : k + 1], 4 * TZ), back).astype(BF) for k in range(3)]
    pieces = []
    weights = []
    for place, number in enumerate(CORNERS):
        for step in range(3):
            pieces.append(jnp.where(inside(place, 0, (4 * TZ, C)), spots[step], BF(0)))
            weights.append(w_ref[toward(*DIRECTIONS[number])[step]])
    result = dot(jnp.concatenate(pieces, 1), jnp.concatenate(weights, 1), ((1,), (1,)))
    for place, number in enumerate(CORNERS):
        other, length = SPANS[7 - number]
        placed_ref[other : other + length, :] = result[place * TZ : (place + 1) * TZ, :]


def backward_kernel(grad_ref, lm_ref, w_ref, out_ref, *, begin):
    size = out_ref.shape[0]
    source = grad_ref[...].astype(F32).T.astype(BF)
    gathered = []
    for k in range(27):
        if k == 13:
            gathered.append(source[:, begin : begin + size])
        else:
            gathered.append(dot(source, hot(lm_ref[26 - k : 27 - k, begin : begin + size], ROWS)).astype(BF))
    weight = jnp.concatenate([w_ref[k] for k in range(27)], 1)
    out_ref[...] = dot(weight, jnp.concatenate(gathered, 0)).T


def final_kernel(*refs):
    placed_ref, rr_ref, act_ref, pair_ref, mixed_ref, out_ref = refs[-6:]
    both = dot(hot(rr_ref[...], ROWS), high_low(placed_ref[...]))
    both = both[:, :C] + both[:, C:]
    size = ROWS // len(refs[:-6])
    for index, ref in enumerate(refs[:-6]):
        rows = slice(index * size, (index + 1) * size)
        out_ref[rows, :] = (ref[...] + both[rows]).astype(BF)
    mixed_ref[...] = (act_ref[...].astype(F32) + pair_ref[...].astype(F32)).astype(BF)


def assemble_kernel(bits_ref, own_ref, one_ref, two_ref, four_ref, out_ref):
    place = bits_ref[0] * 4 + bits_ref[1] * 2 + bits_ref[2]
    blocks = [own_ref[...], one_ref[...]] + [two_ref[i] for i in range(2)] + [four_ref[i] for i in range(4)]
    for distance, block in enumerate(blocks):
        out_ref[place ^ distance] = block.astype(F32)


PARAMS = pltpu.CompilerParams(vmem_limit_bytes=30 * 2**20)


def shape(dims, dtype):
    return jax.ShapeDtypeStruct(dims, dtype)


def whole(dims):
    return pl.BlockSpec(dims, lambda *ids: (0,) * len(dims))


def pairing(axis, which):
    pairs = []
    for tile in range(lax.axis_size("space")):
        at_x, at_y = tile % TILES_X, tile // TILES_X
        tiles_y = lax.axis_size("space") // TILES_X
        if axis == "x":
            move = 1 if (at_x + which) % 2 == 0 else -1
            at_x = (at_x + move) % TILES_X
        else:
            move = 1 if (at_y + which) % 2 == 0 else -1
            at_y = (at_y + move) % tiles_y
        pairs.append((tile, at_y * TILES_X + at_x))
    return pairs


def exchange_x(xa, xb):
    return [lax.ppermute(v, "space", pairing("x", n)) for n, v in enumerate((xa, xb))]


def second_phase(ya, yb, xa, xb, sides, face, edge):
    sent = []
    for which, own in enumerate((ya, yb)):
        down = sides[1] != which
        corners = [jnp.where(down, v[face : face + edge], v[face + edge :]) for v in (xa, xb)]
        sent.append(jnp.concatenate([own] + corners, 0))
    return sent


def exchange_y(sent):
    return [lax.ppermute(v, "space", pairing("y", n)) for n, v in enumerate(sent)]


def swapped(array):
    return lax.ppermute(array, "segment", [(i, i ^ 1) for i in range(lax.axis_size("segment"))])


def xor_send(value, bits):
    return lax.ppermute(value, "space", [(i, i ^ bits) for i in range(lax.axis_size("space"))])


def pick(array, index):
    return lax.dynamic_index_in_dim(array, index, 0, False)


def cost(flops, data):
    return pl.CostEstimate(flops=int(flops), bytes_accessed=int(data), transcendentals=0)


def tie(value, other):
    return lax.optimization_barrier((value, other))[0]


def on_device(features, weights, cotangent, local_map, send_map, recv_map):
    x = features[0]
    w = weights[0]
    cot = cotangent[0]
    lm = local_map.T
    sm = send_map.T
    rr = recv_map.reshape(1, HALO)
    me = lax.axis_index("space")
    sides = jnp.stack([me % 2, me // TILES_X % 2, me % 2]).astype(jnp.int32)
    smem = pl.BlockSpec(memory_space=pltpu.SMEM)
    vmem = pl.BlockSpec(memory_space=pltpu.VMEM)
    def lists_shape(face, edge):
        return [shape((face + 2 * edge, C), BF)] * 2 + [shape((face, C), BF)] * 2

    xa, xb, ya, yb, face_p, edge_p = pl.pallas_call(
        start_kernel,
        in_specs=[smem] + [vmem] * 3,
        out_shape=lists_shape(CAP + 32, TZ + 16) + [shape((4, 32, C), BF), shape((16, C), BF)],
        compiler_params=PARAMS,
        cost_estimate=cost(2e9, 4e6),
        name="start",
    )(sides, x, rr, sm)
    cot_pair = swapped(cot)
    in_x = exchange_x(xa, xb)

    def forward(first, dims, x, *before):
        return pl.pallas_call(
            functools.partial(forward_kernel, width=512, first=first),
            out_shape=[shape((13 * C, ROWS), BF), shape(dims, F32)],
            compiler_params=PARAMS,
            cost_estimate=cost(7e9, 5e6),
            name="forward",
        )(x, lm, w, *before)

    g0, pre = forward(0, (C, ROWS), x)
    in_x = [tie(v, pre) for v in in_x]
    sent = second_phase(ya, yb, *in_x, sides, CAP + 32, TZ + 16)
    in_y = exchange_y(sent)
    g1, pre = forward(14, (ROWS, C), tie(x, sent[0]), pre)
    in_y = [tie(v, pre) for v in in_y]
    act, grad, xa, xb, ya, yb, dw_halo = pl.pallas_call(
        activate_kernel,
        in_specs=[smem] + [vmem] * 9,
        out_shape=[shape((ROWS, C), BF)] * 2 + lists_shape(CAP, TZ) + [shape((27, C, C), F32)],
        compiler_params=PARAMS,
        cost_estimate=cost(4e9, 3e6),
        name="activate",
    )(sides, pre, *in_x, *in_y, rr, cot, cot_pair, w)
    half = 27 * C // 2
    in_x = exchange_x(xa, xb)
    first = pl.pallas_call(
        weight_first_kernel,
        out_shape=shape((14 * C, C), F32),
        compiler_params=PARAMS,
        cost_estimate=cost(4e9, 5e6),
        name="weight_first",
    )(g0, grad, x, dw_halo)
    kept, sent = pl.pallas_call(
        weight_second_kernel,
        in_specs=[smem] + [vmem] * 4,
        out_shape=[shape((half, C), F32), shape((half, C), BF)],
        scratch_shapes=[pltpu.VMEM((27 * C, C), F32)],
        compiler_params=PARAMS,
        cost_estimate=cost(4e9, 5e6),
        name="weight_second",
    )(sides, g1, grad, first, dw_halo)

    size = ROWS // 4

    def backward(index, grad):
        return pl.pallas_call(
            functools.partial(backward_kernel, begin=index * size),
            out_shape=shape((size, C), F32),
            compiler_params=PARAMS,
            cost_estimate=cost(3e9, 2e6),
            name="backward",
        )(grad, lm, w)

    bits = [me % 2, (me // 2 + me // 4) % 2, (me // 8 + me // 16) % 2]

    def halve(one, two, stage):
        kept, sent = [plus(pick(one, at), pick(two, at)) for at in (bits[stage], 1 - bits[stage])]
        return kept, sent.astype(BF)

    def plus(one, two):
        return one.astype(F32) + two.astype(F32)

    locals_ = []
    got = xor_send(sent, 1)
    kept, sent = halve(kept.reshape(2, 2, -1, C), got.reshape(2, 2, -1, C), 1)
    sent, in_x = lax.optimization_barrier((sent, in_x))
    got = xor_send(sent, 2)
    locals_.append(backward(0, tie(grad, sent)))
    locals_.append(backward(1, tie(grad, locals_[0])))
    kept, sent = halve(kept, tie(got, locals_[1]), 2)
    got = xor_send(sent, 8)
    in_y = exchange_y(second_phase(*[tie(v, sent) for v in (ya, yb, *in_x)], sides, CAP, TZ))
    own = plus(kept, got).astype(BF)
    got = xor_send(own, 6)
    act_pair = swapped(tie(act, own))
    locals_.append(backward(2, tie(grad, own)))
    own = plus(own, tie(got, locals_[2])).astype(BF)
    got = xor_send(own, 24)
    placed = pl.pallas_call(
        return_kernel,
        in_specs=[smem] + [vmem] * 7,
        out_shape=shape((HALO, C), F32),
        compiler_params=PARAMS,
        cost_estimate=cost(3e9, 4e6),
        name="returning",
    )(sides, *in_x, *in_y, face_p, edge_p, tie(w, own))
    own = plus(own, tie(got, placed)).astype(BF)
    one = xor_send(own, 8)
    locals_.append(backward(3, tie(grad, own)))
    one = tie(one, locals_[3])
    two = xor_send(jnp.stack([own, one]), 2)
    mixed, input_grad = pl.pallas_call(
        final_kernel,
        out_shape=[shape((ROWS, C), BF), shape((ROWS, C), BF)],
        compiler_params=PARAMS,
        cost_estimate=cost(1e9, 3e6),
        name="final",
    )(*locals_, tie(placed, one), rr, act, act_pair)
    two = tie(two, input_grad)
    four = xor_send(jnp.concatenate([jnp.stack([own, one]), two], 0), 1)
    weight_grad = pl.pallas_call(
        assemble_kernel,
        in_specs=[smem] + [vmem] * 4,
        out_shape=shape((8,) + own.shape, F32),
        compiler_params=PARAMS,
        cost_estimate=cost(1e6, 3e6),
        name="assemble",
    )(jnp.stack(bits).astype(jnp.int32), own, one, two, four)
    return (mixed[None], input_grad[None], weight_grad.reshape(w.shape)[None])


def solution(mesh):
    in_specs = (
        P("segment", "space", None),
        P("segment", None, None, None),
        P("segment", "space", None),
        P("space", None),
        P("space", None),
        P("space"),
    )
    out_specs = (
        P("segment", "space", None),
        P("segment", "space", None),
        P("segment", None, None, None),
    )
    return jax.shard_map(
        on_device, mesh=mesh, in_specs=in_specs, out_specs=out_specs, check_vma=False
    )
```

```python
import functools

import jax
import jax.numpy as jnp
from jax import lax
from jax.experimental import pallas as pl
from jax.experimental.pallas import tpu as pltpu
from jax.sharding import PartitionSpec as P

TZ = 32
TILES_X = 4
CAP = 256
ROWS = 1024
C = 128
HALO = 1152

DIRECTIONS = ((-1, -1), (-1, 0), (-1, 1), (0, -1), (0, 1), (1, -1), (1, 0), (1, 1))
BF = jnp.bfloat16
F32 = jnp.float32


def spans():
    result = []
    start = 0
    for step_x, step_y in DIRECTIONS:
        length = TZ if step_x != 0 and step_y != 0 else CAP
        result.append((start, length))
        start = start + length
    return result


SPANS = spans()
FACES = [n for n, (a, b) in enumerate(DIRECTIONS) if a == 0 or b == 0]
CORNERS = [n for n, (a, b) in enumerate(DIRECTIONS) if a != 0 and b != 0]


def toward(step_x, step_y):
    picked = []
    for offset in range(27):
        along_x = offset // 9 - 1
        along_y = offset // 3 % 3 - 1
        if (step_x == 0 or along_x == -step_x) and (step_y == 0 or along_y == -step_y):
            picked.append(offset)
    return picked


def dot(a, b, dims=((1,), (0,))):
    return lax.dot_general(a, b, (dims, ((), ())), preferred_element_type=F32)


def hot(row, rows):
    pos = lax.broadcasted_iota(jnp.int32, (256, 128), 0).astype(jnp.int16)
    count = row.shape[1]
    blocks = []
    for base in range(0, rows, 256):
        rel = (row - base).astype(jnp.int16)
        parts = [
            jnp.where(rel[:, t : t + 128] == pos, BF(1), BF(0)) for t in range(0, count, 128)
        ]
        blocks.append(jnp.concatenate(parts, 1))
    return jnp.concatenate(blocks, 0)


def spread(column, count):
    kept = jnp.where(column == ROWS, -1, column)
    return jnp.broadcast_to(kept, (column.shape[0], count)).astype(jnp.int16)


def places_from_one(rows):
    return (lax.broadcasted_iota(jnp.int32, (rows, 128), 0) + 1).astype(BF)


def positions(column, row):
    rows, count = column.shape
    numbers = places_from_one(rows)
    numbers = jnp.concatenate([numbers] * (count // 128), 1)
    found = jnp.where(column == row.astype(jnp.int16), numbers, BF(0))
    while rows > 16:
        rows //= 2
        found = jnp.maximum(found[:rows], found[rows:])
    return jnp.max(found.astype(F32), axis=0, keepdims=True)


def match(row, rows):
    numbers = places_from_one(rows)
    row = row.astype(BF)
    parts = [jnp.where(row[:, t : t + 128] == numbers, BF(1), BF(0)) for t in range(0, row.shape[1], 128)]
    return jnp.concatenate(parts, 1)


def face_rows(block):
    block = block.astype(F32)
    return [jnp.concatenate([block[k : k + 1], block[16 + k : 17 + k]], 1) for k in range(9)]


def column_of(row):
    return jnp.broadcast_to(row.astype(F32), (8, row.shape[1])).T[:, :1].astype(jnp.int32)


def inside(place, axis, dims):
    return (lax.broadcasted_iota(jnp.int32, dims, axis) // TZ) == place


def number_of(step_x, step_y):
    return DIRECTIONS.index((step_x, step_y))


def pack_sides(lists, orient, sides, xa_ref, xb_ref, ya_ref, yb_ref):
    x_odd, y_odd = sides[0] == 1, sides[1] == 1

    def x_side(side):
        picked = [(orient * side, 0), (orient * side, -orient), (orient * side, orient)]
        return jnp.concatenate([lists[number_of(*d)] for d in picked], 0)

    plus, minus = x_side(1), x_side(-1)
    xa_ref[...] = jnp.where(x_odd, minus, plus)
    xb_ref[...] = jnp.where(x_odd, plus, minus)
    plus, minus = lists[number_of(0, orient)], lists[number_of(0, -orient)]
    ya_ref[...] = jnp.where(y_odd, minus, plus)
    yb_ref[...] = jnp.where(y_odd, plus, minus)


def unpack_sides(orient, sides, face, edge, xa, xb, ya, yb):
    x_odd, y_odd = sides[0] == 1, sides[1] == 1

    def of_side(side, odd, a, b):
        return jnp.where(odd, b, a) if side == 1 else jnp.where(odd, a, b)

    lists = []
    for step_x, step_y in DIRECTIONS:
        if step_y == 0:
            lists.append(of_side(-orient * step_x, x_odd, xa[:face], xb[:face]))
        elif step_x == 0:
            lists.append(of_side(-orient * step_y, y_odd, ya[:face], yb[:face]))
        else:
            first = of_side(-orient * step_y, y_odd, ya[face : face + edge], yb[face : face + edge])
            second = of_side(-orient * step_y, y_odd, ya[face + edge :], yb[face + edge :])
            lists.append(of_side(-orient * step_x, x_odd, first, second))
    return lists


def start_kernel(side_ref, x_ref, rr_ref, sm_ref, xa_ref, xb_ref, ya_ref, yb_ref, face_p_ref, edge_p_ref):
    lists = [None] * 8
    row = rr_ref[...]
    column = column_of(row)
    listed = dot(x_ref[...].astype(F32).T.astype(BF), hot(row, ROWS)).T.astype(BF)
    for place, number in enumerate(FACES):
        start, length = SPANS[number]
        other, _ = SPANS[7 - number]
        wide = spread(column[other : other + length], length)
        found = [
            positions(wide, sm_ref[offset : offset + 1, start : start + length])
            for offset in toward(*DIRECTIONS[number])
        ]
        found = jnp.concatenate(found + [jnp.zeros((7, length), F32)], 0)
        found = jnp.concatenate([found[:, :128], found[:, 128:]], 0).astype(BF)
        face_p_ref[place] = found
        lists[number] = jnp.concatenate([listed[other : other + length], found], 0)
    wide = spread(
        jnp.concatenate([column[SPANS[7 - n][0] : SPANS[7 - n][0] + TZ] for n in CORNERS], 0), 4 * TZ
    )
    found = []
    for step in range(3):
        pieces = []
        for number in CORNERS:
            start, length = SPANS[number]
            offset = toward(*DIRECTIONS[number])[step]
            pieces.append(sm_ref[offset : offset + 1, start : start + length])
        found.append(positions(wide, jnp.concatenate(pieces, 1)))
    found = jnp.concatenate(found + [jnp.zeros((13, 4 * TZ), F32)], 0).astype(BF)
    edge_p_ref[...] = found
    for number in CORNERS:
        other, length = SPANS[7 - number]
        lists[number] = jnp.concatenate([listed[other : other + length], found], 0)
    pack_sides(lists, 1, (side_ref[0], side_ref[1]), xa_ref, xb_ref, ya_ref, yb_ref)


def forward_kernel(x_ref, lm_ref, w_ref, *refs, width, first):
    g_ref, sum_ref = refs[-2:]
    source = x_ref[...].astype(F32).T.astype(BF)
    offsets = range(first, first + 13)
    weight = jnp.concatenate([w_ref[k] for k in offsets], 0)
    for begin in range(0, ROWS, width):
        cols = slice(begin, begin + width)
        gathered = [dot(source, hot(lm_ref[k : k + 1, cols], ROWS)).astype(BF) for k in offsets]
        gathered = jnp.concatenate(gathered, 0)
        g_ref[:, cols] = gathered
        part = dot(weight, gathered, ((0,), (0,)))
        if first == 0:
            sum_ref[:, cols] = part + dot(w_ref[13], source[:, cols], ((0,), (0,)))
        else:
            sum_ref[cols, :] = (part + refs[0][:, cols]).T


def high_low(values):
    high = values.astype(BF)
    return jnp.concatenate([high, (values - high.astype(F32)).astype(BF)], 1)


def activate_kernel(
    side_ref, pre_ref, ixa_ref, ixb_ref, iya_ref, iyb_ref, rr_ref, cot_ref, pair_ref, w_ref,
    act_ref, grad_ref, xa_ref, xb_ref, ya_ref, yb_ref, dw_ref,
):
    sides = (side_ref[0], side_ref[1])
    arrived = unpack_sides(
        1, sides, CAP + 32, TZ + 16, ixa_ref[...], ixb_ref[...], iya_ref[...], iyb_ref[...]
    )
    sums = [None] * 8
    sources = []
    for number in FACES:
        picked = toward(*DIRECTIONS[number])
        source = arrived[number][:CAP].astype(F32).T.astype(BF)
        sources.append(source)
        gathered = [dot(source, match(row, CAP)).astype(BF) for row in face_rows(arrived[number][CAP:])]
        weight = jnp.concatenate([w_ref[offset] for offset in picked], 0)
        sums[number] = dot(weight, jnp.concatenate(gathered, 0), ((0,), (0,))).T
    edge_source = jnp.concatenate([arrived[n][:TZ] for n in CORNERS], 0).astype(F32).T.astype(BF)
    edge_found = jnp.zeros((16, 4 * TZ), F32)
    for place, number in enumerate(CORNERS):
        rows = arrived[number][TZ:].astype(F32)
        edge_found = jnp.where(inside(place, 1, rows.shape), rows, edge_found)
    gathered = [dot(edge_source, match(edge_found[k : k + 1], 4 * TZ)).astype(BF) for k in range(3)]
    masked = []
    weights = []
    for place, number in enumerate(CORNERS):
        for step in range(3):
            masked.append(jnp.where(inside(place, 1, (C, 4 * TZ)), gathered[step], BF(0)))
            weights.append(w_ref[toward(*DIRECTIONS[number])[step]])
    total = dot(jnp.concatenate(weights, 0), jnp.concatenate(masked, 0), ((0,), (0,))).T
    for place, number in enumerate(CORNERS):
        sums[number] = total[place * TZ : (place + 1) * TZ]

    selector = hot(rr_ref[...], ROWS)
    both = dot(selector, high_low(jnp.concatenate(sums, 0)))
    pre = pre_ref[...] + both[:, :C] + both[:, C:]
    gate = 1.0 / (1.0 + jnp.exp(-pre))
    act_ref[...] = (pre * gate).astype(BF)
    upstream = cot_ref[...].astype(F32) + pair_ref[...].astype(F32)
    grad = upstream * gate * (1.0 + pre * (1.0 - gate))
    grad_ref[...] = grad.astype(BF)
    listed = dot(grad.T.astype(BF), selector).T.astype(BF)
    lists = [listed[start : start + length] for start, length in SPANS]
    pack_sides(lists, -1, sides, xa_ref, xb_ref, ya_ref, yb_ref)

    dw_ref[...] = jnp.zeros_like(dw_ref)
    for source, number in zip(sources, FACES):
        pieces = [
            dot(match(row, CAP), lists[number]).astype(BF) for row in face_rows(arrived[number][CAP:])
        ]
        part = dot(source, jnp.concatenate(pieces, 1))
        for index, offset in enumerate(toward(*DIRECTIONS[number])):
            dw_ref[offset] += part[:, index * C : (index + 1) * C]
    back = jnp.concatenate([lists[n] for n in CORNERS], 0)
    spots = [dot(match(edge_found[k : k + 1], 4 * TZ), back).astype(BF) for k in range(3)]
    pieces = [
        jnp.where(inside(place, 0, (4 * TZ, C)), spots[step], BF(0)) for place in range(4) for step in range(3)
    ]
    part = dot(edge_source, jnp.concatenate(pieces, 1))
    for place, number in enumerate(CORNERS):
        for step in range(3):
            index = 3 * place + step
            dw_ref[toward(*DIRECTIONS[number])[step]] += part[:, index * C : (index + 1) * C]


def weight_first_kernel(g_ref, grad_ref, x_ref, halo_ref, dw_ref):
    grad = grad_ref[...]
    dw_ref[: 13 * C, :] = dot(g_ref[...], grad) + halo_ref[:13].reshape(13 * C, C)
    dw_ref[13 * C :, :] = dot(x_ref[...], grad, ((0,), (0,))) + halo_ref[13]


def weight_second_kernel(side_ref, g_ref, grad_ref, first_ref, halo_ref, kept_ref, sent_ref, total):
    total[: 14 * C, :] = first_ref[...]
    total[14 * C :, :] = dot(g_ref[...], grad_ref[...]) + halo_ref[14:].reshape(13 * C, C)
    half = kept_ref.shape[0]
    kept_ref[...] = total[pl.ds(pl.multiple_of(side_ref[2] * half, 8), half), :]
    sent_ref[...] = total[pl.ds(pl.multiple_of((1 - side_ref[2]) * half, 8), half), :].astype(BF)


def return_kernel(side_ref, ixa_ref, ixb_ref, iya_ref, iyb_ref, face_p_ref, edge_p_ref, w_ref, placed_ref):
    sides = (side_ref[0], side_ref[1])
    returned = unpack_sides(-1, sides, CAP, TZ, ixa_ref[...], ixb_ref[...], iya_ref[...], iyb_ref[...])
    for place, number in enumerate(FACES):
        other, length = SPANS[7 - number]
        pieces = [dot(match(row, CAP), returned[number]).astype(BF) for row in face_rows(face_p_ref[place])]
        weight = jnp.concatenate([w_ref[offset] for offset in toward(*DIRECTIONS[number])], 1)
        placed_ref[other : other + length, :] = dot(jnp.concatenate(pieces, 1), weight, ((1,), (1,)))
    back = jnp.concatenate([returned[n] for n in CORNERS], 0)
    found = edge_p_ref[...].astype(F32)
    spots = [dot(match(found[k : k + 1], 4 * TZ), back).astype(BF) for k in range(3)]
    pieces = []
    weights = []
    for place, number in enumerate(CORNERS):
        for step in range(3):
            pieces.append(jnp.where(inside(place, 0, (4 * TZ, C)), spots[step], BF(0)))
            weights.append(w_ref[toward(*DIRECTIONS[number])[step]])
    result = dot(jnp.concatenate(pieces, 1), jnp.concatenate(weights, 1), ((1,), (1,)))
    for place, number in enumerate(CORNERS):
        other, length = SPANS[7 - number]
        placed_ref[other : other + length, :] = result[place * TZ : (place + 1) * TZ, :]


def backward_kernel(grad_ref, lm_ref, w_ref, out_ref, *, begin):
    size = out_ref.shape[0]
    source = grad_ref[...].astype(F32).T.astype(BF)
    gathered = []
    for k in range(27):
        if k == 13:
            gathered.append(source[:, begin : begin + size])
        else:
            gathered.append(dot(source, hot(lm_ref[26 - k : 27 - k, begin : begin + size], ROWS)).astype(BF))
    weight = jnp.concatenate([w_ref[k] for k in range(27)], 1)
    out_ref[...] = dot(weight, jnp.concatenate(gathered, 0)).T


def final_kernel(*refs):
    placed_ref, rr_ref, act_ref, pair_ref, mixed_ref, out_ref = refs[-6:]
    both = dot(hot(rr_ref[...], ROWS), high_low(placed_ref[...]))
    both = both[:, :C] + both[:, C:]
    size = ROWS // len(refs[:-6])
    for index, ref in enumerate(refs[:-6]):
        rows = slice(index * size, (index + 1) * size)
        out_ref[rows, :] = (ref[...] + both[rows]).astype(BF)
    mixed_ref[...] = (act_ref[...].astype(F32) + pair_ref[...].astype(F32)).astype(BF)


def assemble_kernel(bits_ref, own_ref, one_ref, two_ref, four_ref, out_ref):
    place = bits_ref[0] * 4 + bits_ref[1] * 2 + bits_ref[2]
    blocks = [own_ref[...], one_ref[...]] + [two_ref[i] for i in range(2)] + [four_ref[i] for i in range(4)]
    for distance, block in enumerate(blocks):
        out_ref[place ^ distance] = block.astype(F32)


PARAMS = pltpu.CompilerParams(vmem_limit_bytes=30 * 2**20)


def shape(dims, dtype):
    return jax.ShapeDtypeStruct(dims, dtype)


def whole(dims):
    return pl.BlockSpec(dims, lambda *ids: (0,) * len(dims))


def pairing(axis, which):
    pairs = []
    for tile in range(lax.axis_size("space")):
        at_x, at_y = tile % TILES_X, tile // TILES_X
        tiles_y = lax.axis_size("space") // TILES_X
        if axis == "x":
            move = 1 if (at_x + which) % 2 == 0 else -1
            at_x = (at_x + move) % TILES_X
        else:
            move = 1 if (at_y + which) % 2 == 0 else -1
            at_y = (at_y + move) % tiles_y
        pairs.append((tile, at_y * TILES_X + at_x))
    return pairs


def exchange_x(xa, xb):
    return [lax.ppermute(v, "space", pairing("x", n)) for n, v in enumerate((xa, xb))]


def second_phase(ya, yb, xa, xb, sides, face, edge):
    sent = []
    for which, own in enumerate((ya, yb)):
        down = sides[1] != which
        corners = [jnp.where(down, v[face : face + edge], v[face + edge :]) for v in (xa, xb)]
        sent.append(jnp.concatenate([own] + corners, 0))
    return sent


def exchange_y(sent):
    return [lax.ppermute(v, "space", pairing("y", n)) for n, v in enumerate(sent)]


def swapped(array):
    return lax.ppermute(array, "segment", [(i, i ^ 1) for i in range(lax.axis_size("segment"))])


def xor_send(value, bits):
    return lax.ppermute(value, "space", [(i, i ^ bits) for i in range(lax.axis_size("space"))])


def pick(array, index):
    return lax.dynamic_index_in_dim(array, index, 0, False)


def cost(flops, data):
    return pl.CostEstimate(flops=int(flops), bytes_accessed=int(data), transcendentals=0)


def tie(value, other):
    return lax.optimization_barrier((value, other))[0]


def on_device(features, weights, cotangent, local_map, send_map, recv_map):
    x = features[0]
    w = weights[0]
    cot = cotangent[0]
    lm = local_map.T
    sm = send_map.T
    rr = recv_map.reshape(1, HALO)
    me = lax.axis_index("space")
    sides = jnp.stack([me % 2, me // TILES_X % 2, me % 2]).astype(jnp.int32)
    smem = pl.BlockSpec(memory_space=pltpu.SMEM)
    vmem = pl.BlockSpec(memory_space=pltpu.VMEM)
    def lists_shape(face, edge):
        return [shape((face + 2 * edge, C), BF)] * 2 + [shape((face, C), BF)] * 2

    xa, xb, ya, yb, face_p, edge_p = pl.pallas_call(
        start_kernel,
        in_specs=[smem] + [vmem] * 3,
        out_shape=lists_shape(CAP + 32, TZ + 16) + [shape((4, 32, C), BF), shape((16, C), BF)],
        compiler_params=PARAMS,
        cost_estimate=cost(2e9, 4e6),
        name="start",
    )(sides, x, rr, sm)
    cot_pair = swapped(cot)
    in_x = exchange_x(xa, xb)

    def forward(first, dims, x, *before):
        return pl.pallas_call(
            functools.partial(forward_kernel, width=1024, first=first),
            out_shape=[shape((13 * C, ROWS), BF), shape(dims, F32)],
            compiler_params=PARAMS,
            cost_estimate=cost(7e9, 5e6),
            name="forward",
        )(x, lm, w, *before)

    g0, pre = forward(0, (C, ROWS), x)
    in_x = [tie(v, pre) for v in in_x]
    sent = second_phase(ya, yb, *in_x, sides, CAP + 32, TZ + 16)
    in_y = exchange_y(sent)
    g1, pre = forward(14, (ROWS, C), tie(x, sent[0]), pre)
    in_y = [tie(v, pre) for v in in_y]
    act, grad, xa, xb, ya, yb, dw_halo = pl.pallas_call(
        activate_kernel,
        in_specs=[smem] + [vmem] * 9,
        out_shape=[shape((ROWS, C), BF)] * 2 + lists_shape(CAP, TZ) + [shape((27, C, C), F32)],
        compiler_params=PARAMS,
        cost_estimate=cost(4e9, 3e6),
        name="activate",
    )(sides, pre, *in_x, *in_y, rr, cot, cot_pair, w)
    half = 27 * C // 2
    in_x = exchange_x(xa, xb)
    first = pl.pallas_call(
        weight_first_kernel,
        out_shape=shape((14 * C, C), F32),
        compiler_params=PARAMS,
        cost_estimate=cost(4e9, 5e6),
        name="weight_first",
    )(g0, grad, x, dw_halo)
    kept, sent = pl.pallas_call(
        weight_second_kernel,
        in_specs=[smem] + [vmem] * 4,
        out_shape=[shape((half, C), F32), shape((half, C), BF)],
        scratch_shapes=[pltpu.VMEM((27 * C, C), F32)],
        compiler_params=PARAMS,
        cost_estimate=cost(4e9, 5e6),
        name="weight_second",
    )(sides, g1, grad, first, dw_halo)

    size = ROWS // 4

    def backward(index, grad):
        return pl.pallas_call(
            functools.partial(backward_kernel, begin=index * size),
            out_shape=shape((size, C), F32),
            compiler_params=PARAMS,
            cost_estimate=cost(3e9, 2e6),
            name="backward",
        )(grad, lm, w)

    bits = [me % 2, (me // 2 + me // 4) % 2, (me // 8 + me // 16) % 2]

    def halve(one, two, stage):
        kept, sent = [plus(pick(one, at), pick(two, at)) for at in (bits[stage], 1 - bits[stage])]
        return kept, sent.astype(BF)

    def plus(one, two):
        return one.astype(F32) + two.astype(F32)

    locals_ = []
    got = xor_send(sent, 1)
    kept, sent = halve(kept.reshape(2, 2, -1, C), got.reshape(2, 2, -1, C), 1)
    sent, in_x = lax.optimization_barrier((sent, in_x))
    got = xor_send(sent, 2)
    locals_.append(backward(0, tie(grad, sent)))
    locals_.append(backward(1, tie(grad, locals_[0])))
    kept, sent = halve(kept, tie(got, locals_[1]), 2)
    got = xor_send(sent, 8)
    in_y = exchange_y(second_phase(*[tie(v, sent) for v in (ya, yb, *in_x)], sides, CAP, TZ))
    own = plus(kept, got).astype(BF)
    got = xor_send(own, 6)
    act_pair = swapped(tie(act, own))
    locals_.append(backward(2, tie(grad, own)))
    own = plus(own, tie(got, locals_[2])).astype(BF)
    got = xor_send(own, 24)
    placed = pl.pallas_call(
        return_kernel,
        in_specs=[smem] + [vmem] * 7,
        out_shape=shape((HALO, C), F32),
        compiler_params=PARAMS,
        cost_estimate=cost(3e9, 4e6),
        name="returning",
    )(sides, *in_x, *in_y, face_p, edge_p, tie(w, own))
    own = plus(own, tie(got, placed)).astype(BF)
    one = xor_send(own, 8)
    locals_.append(backward(3, tie(grad, own)))
    one = tie(one, locals_[3])
    two = xor_send(jnp.stack([own, one]), 2)
    mixed, input_grad = pl.pallas_call(
        final_kernel,
        out_shape=[shape((ROWS, C), BF), shape((ROWS, C), BF)],
        compiler_params=PARAMS,
        cost_estimate=cost(1e9, 3e6),
        name="final",
    )(*locals_, tie(placed, one), rr, act, act_pair)
    two = tie(two, input_grad)
    four = xor_send(jnp.concatenate([jnp.stack([own, one]), two], 0), 1)
    weight_grad = pl.pallas_call(
        assemble_kernel,
        in_specs=[smem] + [vmem] * 4,
        out_shape=shape((8,) + own.shape, F32),
        compiler_params=PARAMS,
        cost_estimate=cost(1e6, 3e6),
        name="assemble",
    )(jnp.stack(bits).astype(jnp.int32), own, one, two, four)
    return (mixed[None], input_grad[None], weight_grad.reshape(w.shape)[None])


def solution(mesh):
    in_specs = (
        P("segment", "space", None),
        P("segment", None, None, None),
        P("segment", "space", None),
        P("space", None),
        P("space", None),
        P("space"),
    )
    out_specs = (
        P("segment", "space", None),
        P("segment", "space", None),
        P("segment", None, None, None),
    )
    return jax.shard_map(
        on_device, mesh=mesh, in_specs=in_specs, out_specs=out_specs, check_vma=False
    )
```
